32 devices in a mesh: dom: 16 (over z, x, core), sub: 2 (over y).
Axes of the slice: x: 2, y: 2, z: 4, core: 2. Of those that a mesh axis runs over, the one named last changes fastest.
Arguments:
- entity_table: float32 [16384, 256], P(('dom', 'sub')), may hold values from -3 to 3
- entity_state: float32 [16384], P(('dom', 'sub')), may hold values from 0.1 to 1
- relations: float32 [400, 256], replicated, may hold values from -4 to 4
- relation_state: float32 [400], replicated, may hold values from 0.1 to 1
- head_rows: int32 [16, 2, 8192], P('dom', 'sub'), may hold values from 0 to 1023
- tail_rows: int32 [16, 2, 8192], P('dom', 'sub'), may hold values from 0 to 1023
- relation_ids: int32 [16, 2, 8192], P('dom', 'sub'), may hold values from 0 to 399
- negative_rows: int32 [16, 2, 512], P('dom', 'sub'), may hold values from 0 to 1023
- edge_counts: int32 [16, 2], P('dom', 'sub'), may hold values from 1 to 8192, as said below
Outputs:
- new_table: float32 [16384, 256], P(('dom', 'sub'))
- new_state: float32 [16384], P(('dom', 'sub'))
- new_relations: float32 [400, 256], replicated
The draws below stay inside these ranges and needn't reach their ends.
Inputs may be any that keep to these rules, and one draw needn't show every extreme that they name: `edge_counts`: at least one device has all 8192 slots live.
All inputs are finite; a program needn't handle non-finite values.
Results may differ from the reference program's by a relative error of at most 0.0003.
The reference program's roundings to bfloat16 on the way (of `slabs`, `query_b` and `neg_coef`) count: a program that leaves them out, or rounds other values in their place, can miss the bound.
Values may be sent and summed in bfloat16 or wider, within the bound.
No kernel may reach another device: no remote copies, remote signals or barrier semaphores. Data moves between devices by JAX's collectives and lax.ppermute only.
A program may use at most 128 MiB of HBM per device.

```python
import math
import jax
import jax.numpy as jnp
import numpy as np
from jax import lax

D = 256
R = 400
NEG = 512
CAP = 8192
SLAB = 1024
ENTITIES = 16384
N_DOM = 16
N_SUB = 2


def draw_edge_counts(key, part):
    key = jax.random.fold_in(key, 5)
    first_key, second_key = jax.random.split(key)
    base = jax.random.randint(first_key, (N_DOM * N_SUB,), max(CAP // 8, 1), CAP // 2 + 1, dtype=jnp.int32)
    chosen = jax.random.randint(second_key, (), 0, N_DOM * N_SUB, dtype=jnp.int32)
    places = jnp.arange(N_DOM * N_SUB, dtype=jnp.int32)
    filled = jnp.where(places == chosen, CAP, base)
    return filled.reshape(N_DOM, N_SUB).astype(jnp.int32)


def touch_ends(entries, rng, least, largest):
    shape = entries.shape
    spot = [jax.random.randint(jax.random.fold_in(rng, axis), (), 0, shape[axis]) for axis in range(len(shape))]
    entries = entries.at[tuple(spot)].set(least)
    longest = shape.index(max(shape))
    spot[longest] = (spot[longest] + 1) % shape[longest]
    return entries.at[tuple(spot)].set(largest)


def block_scale(key, dims, shards, smallest, largest):
    gain = 1.0
    for dim, parts in shards:
        heights = jax.random.uniform(jax.random.fold_in(jax.random.fold_in(key, 6), dim), (parts,), jnp.float32, smallest / len(shards), largest / len(shards))
        gain = gain * jnp.repeat(jnp.exp(heights), dims[dim] // parts).reshape((-1,) + (1,) * (len(dims) - 1 - dim))
    return gain


def rank_bounds(number_of, skew):
    portions = [(1 << 20) // math.isqrt(rank ** skew) + 1 for rank in range(1, number_of + 1)]
    spread = 1 + sum(portions) // (1 << 30)
    return np.cumsum(np.array([max(1, weight // spread) for weight in portions]))


def skewed_ids(key, shape, amount, slope):
    grid = rank_bounds(amount, slope)
    ticket = jax.random.randint(jax.random.fold_in(key, 1), shape, 0, int(grid[amount - 1]))
    standing = jnp.searchsorted(jnp.asarray(grid, jnp.int32), ticket, side="right")
    return jax.random.permutation(jax.random.fold_in(key, 2), amount)[standing].astype(jnp.int32)


def normal_values(rng, extent, spread, bound, cuts=(), held_as=jnp.bfloat16):
    array = spread * jax.random.normal(rng, extent, jnp.float32)
    if cuts:
        array = array * block_scale(rng, extent, cuts, -0.22, 0.18)
    return jnp.clip(array, -bound, bound).astype(held_as)


def setup_inputs(seed: int = 0) -> dict:
    splits = jax.random.split(jax.random.key(seed), 10)
    entity_table = normal_values(splits[0], (ENTITIES, D), 0.5, 3.0, ((0, 32),), jnp.float32)
    entity_state = jnp.clip(jnp.exp(math.log(1.0) - 2.3025851 * jax.random.uniform(splits[1], (ENTITIES,), jnp.float32) ** block_scale(splits[1], (ENTITIES,), ((0, 32),), -0.2, 0.2)), 0.1, 1.0)
    relations = normal_values(splits[2], (R, D), 1.0, 4.0, (), jnp.float32)
    relation_state = jnp.clip(jnp.exp(jax.random.uniform(splits[3], (R,), jnp.float32, math.log(0.1), math.log(1.0))), 0.1, 1.0)
    head_rows = touch_ends(jax.random.randint(splits[4], (N_DOM, N_SUB, CAP), 0, SLAB), jax.random.fold_in(splits[4], 1), 0, SLAB - 1).astype(jnp.int32)
    tail_rows = touch_ends(jax.random.randint(splits[5], (N_DOM, N_SUB, CAP), 0, SLAB), jax.random.fold_in(splits[5], 1), 0, SLAB - 1).astype(jnp.int32)
    relation_ids = touch_ends(skewed_ids(splits[6], (N_DOM, N_SUB, CAP), R, 2), jax.random.fold_in(splits[6], 3), 0, R - 1).astype(jnp.int32)
    negative_rows = touch_ends(jax.random.randint(splits[7], (N_DOM, N_SUB, NEG), 0, SLAB), jax.random.fold_in(splits[7], 1), 0, SLAB - 1).astype(jnp.int32)
    edge_counts = draw_edge_counts(jax.random.fold_in(splits[9], 71), 0)
    return dict(entity_table=entity_table, entity_state=entity_state, relations=relations, relation_state=relation_state, head_rows=head_rows, tail_rows=tail_rows, relation_ids=relation_ids, negative_rows=negative_rows, edge_counts=edge_counts)


learn_rate = 0.1

def edge_terms(own_slab, far_slab, relations, heads, tails, kinds, negatives, count):
    head = own_slab[heads].astype(jnp.float32)
    tail = far_slab[tails].astype(jnp.float32)
    negative_table = far_slab[negatives]
    operator = relations[kinds]
    valid = (jnp.arange(heads.shape[0], dtype=jnp.int32) < count).astype(jnp.float32)
    query = head * operator
    query_b = query.astype(jnp.bfloat16)
    positive = lax.optimization_barrier(jnp.sum(query * tail, axis=-1))
    negative_scores = jnp.dot(query_b, negative_table.T, preferred_element_type=jnp.float32)
    pos_coef = -jax.nn.sigmoid(-positive) * valid
    neg_coef = (jax.nn.sigmoid(negative_scores) * (valid[:, None] / NEG)).astype(jnp.bfloat16)
    query_grad = pos_coef[:, None] * tail + jnp.dot(neg_coef, negative_table, preferred_element_type=jnp.float32)
    tail_grad = pos_coef[:, None] * query
    negative_grad = jnp.dot(neg_coef.T, query_b, preferred_element_type=jnp.float32)
    head_grad = query_grad * operator
    operator_grad = query_grad * head
    rows = own_slab.shape[0]
    own_grad = jax.ops.segment_sum(head_grad, heads, num_segments=rows)
    far_grad = jax.ops.segment_sum(tail_grad, tails, num_segments=rows)
    far_grad = far_grad + jax.ops.segment_sum(negative_grad, negatives, num_segments=rows)
    relation_grad = jax.ops.segment_sum(operator_grad, kinds, num_segments=relations.shape[0])
    return (own_grad, far_grad, relation_grad)

def reference(entity_table, entity_state, relations, relation_state, head_rows, tail_rows, relation_ids, negative_rows, edge_counts):
    slabs = entity_table.astype(jnp.bfloat16).reshape(N_DOM, SLAB, D)
    half_way = N_DOM // 2
    partner_ids = jnp.bitwise_xor(jnp.arange(N_DOM, dtype=jnp.int32), half_way)

    def per_domain(index):
        own_slab = slabs[index]
        far_slab = slabs[jnp.bitwise_xor(index, half_way)]
        terms = jax.vmap(edge_terms, in_axes=(None, None, None, 0, 0, 0, 0, 0))(own_slab, far_slab, relations, head_rows[index], tail_rows[index], relation_ids[index], negative_rows[index], edge_counts[index])
        return (lax.optimization_barrier(jnp.sum(terms[0], axis=0)), lax.optimization_barrier(jnp.sum(terms[1], axis=0)), lax.optimization_barrier(jnp.sum(terms[2], axis=0)))
    own_grads, far_grads, relation_grads = lax.map(per_domain, jnp.arange(N_DOM, dtype=jnp.int32))
    grad = (own_grads + far_grads[partner_ids]).reshape(ENTITIES, D)
    relation_grad = lax.optimization_barrier(jnp.sum(relation_grads, axis=0))
    new_state = entity_state + lax.optimization_barrier(jnp.mean(grad * grad, axis=-1))
    new_table = entity_table - learn_rate * grad / jnp.sqrt(new_state)[:, None]
    relation_total = relation_state + lax.optimization_barrier(jnp.mean(relation_grad * relation_grad, axis=-1))
    new_relations = relations - learn_rate * relation_grad / jnp.sqrt(relation_total)[:, None]
    return (new_table, new_state, new_relations)
```

```python
import functools

import jax
import jax.numpy as jnp
from jax import lax
from jax.experimental import pallas as pl
from jax.experimental.pallas import tpu as pltpu
from jax.sharding import PartitionSpec as P

learn_rate = 0.1
block = 512
bf16 = jnp.bfloat16
f32 = jnp.float32
vmem_bytes = 56 * 2**20


def dot(a, b):
    return jnp.dot(a, b, preferred_element_type=f32)


def dot_nt(a, b):
    return lax.dot_general(a, b, (((1,), (1,)), ((), ())), preferred_element_type=f32)


def one_hot(ids, rows):
    places = lax.broadcasted_iota(jnp.int16, (rows, ids.shape[1]), 0)
    return jnp.where(places == ids.astype(jnp.int16), jnp.ones((), bf16), jnp.zeros((), bf16))


def split(x):
    high = x.astype(bf16)
    return high, (x - high.astype(f32)).astype(bf16)


def gather_t(pieces, hot):
    rows = pieces[0].shape[1]
    total = dot(pieces[0][...], hot[:rows])
    for k in range(1, len(pieces)):
        total = total + dot(pieces[k][...], hot[k * rows : (k + 1) * rows])
    return total


def scatter_add(pieces, hot, values):
    rows = pieces[0].shape[0]
    for k, piece in enumerate(pieces):
        part = hot[k * rows : (k + 1) * rows]
        total = dot_nt(part, values[0])
        for value in values[1:]:
            total = total + dot_nt(part, value)
        piece[...] += total


def query_kernel(n, rel_rows, source, place, live, codes, ids, relations, *refs):
    slab, (head_out, operator_out), (rel_full, rel_split) = refs[:n], refs[n : n + 2], refs[n + 2 :]
    dims = relations.shape[1]

    @pl.when(pl.program_id(0) == 0)
    def _():
        rel_full[...] = jnp.zeros_like(rel_full)
        rel_full[: relations.shape[0], :] = relations[...]
        high, low = split(rel_full[...].T)
        rel_split[:dims, :] = high
        rel_split[dims:, :] = low

    @pl.when(pl.program_id(0) < codes[2])
    def _():
        rows = slab[0].shape[1]
        head = gather_t(slab, one_hot(ids[0, 0:1, :] ^ codes[0], n * rows))
        both = dot(rel_split[...], one_hot(ids[0, 2:3, :], rel_rows))
        head_out[0] = head.astype(bf16)
        operator_out[0] = both[:dims] + both[dims:]


def score_kernel(n, source, place, live, codes, ids, negatives, head_in, operator_in, *refs):
    slab, (head_grad, operator_grad), far = refs[:n], refs[n : n + 2], refs[n + 2 : 2 * n + 2]
    table, table_t, negative_grad = refs[2 * n + 2 :]
    step = pl.program_id(0)
    steps = codes[2]
    rows = slab[0].shape[1]
    here = source[step]
    count = table.shape[0]

    @pl.when(step == 0)
    def _():
        for piece in far:
            piece[...] = jnp.zeros_like(piece)

    @pl.when(pl.program_id(0) < codes[2])
    def _():
        @pl.when((step == 0) | (source[jnp.maximum(step - 1, 0)] != here))
        def _():
            found = gather_t(slab, one_hot(negatives[here] ^ codes[0], n * rows))
            table_t[...] = found.astype(bf16)
            table[...] = found.T.astype(bf16)
            negative_grad[...] = jnp.zeros_like(negative_grad)

        width = ids.shape[2]
        alive = (lax.broadcasted_iota(jnp.int32, (1, width), 1) < live[step]).astype(f32)
        hot = one_hot(ids[0, 1:2, :] ^ codes[0], n * rows)
        tail = gather_t(slab, hot)
        head = head_in[0].astype(f32)
        operator = operator_in[0]
        query = head * operator
        query_b = query.astype(bf16)
        positive = jnp.sum(query * tail, axis=0, keepdims=True)
        scores = dot(table[...], query_b)
        pos_coef = -jax.nn.sigmoid(-positive) * alive
        neg_coef = (jax.nn.sigmoid(scores) * (alive * (1.0 / count))).astype(bf16)
        query_grad = pos_coef * tail + dot(table_t[...], neg_coef)
        negative_grad[...] += dot_nt(neg_coef, query_b)
        head_grad[0, 0], head_grad[0, 1] = split(query_grad * operator)
        operator_grad[0, 0], operator_grad[0, 1] = split(query_grad * head)
        scatter_add(far, hot, split(pos_coef * query))

        @pl.when((step == steps - 1) | (source[jnp.minimum(step + 1, source.shape[0] - 1)] != here))
        def _():
            chosen = one_hot(negatives[here] ^ codes[0], n * rows)
            high, low = split(negative_grad[...])
            for k, piece in enumerate(far):
                part = chosen[k * rows : (k + 1) * rows]
                piece[...] += dot(part, high) + dot(part, low)


def scatter_kernel(n, source, place, live, codes, ids, head_grad, operator_grad, *refs):
    own, relation = refs[:n], refs[n:]
    rows = own[0].shape[0]

    @pl.when(pl.program_id(0) == 0)
    def _():
        for piece in refs:
            piece[...] = jnp.zeros_like(piece)

    @pl.when(pl.program_id(0) < codes[2])
    def _():
        hot = one_hot(ids[0, 0:1, :] ^ codes[0], n * rows)
        scatter_add(own, hot, (head_grad[0, 0], head_grad[0, 1]))
        rel_rows = len(relation) * relation[0].shape[0]
        hot = one_hot(ids[0, 2:3, :] ^ codes[1], rel_rows)
        scatter_add(relation, hot, (operator_grad[0, 0], operator_grad[0, 1]))


def relation_kernel(code, relations, state, *refs):
    pieces, out, grad = refs[:-2], refs[-2], refs[-1]
    rows = pieces[0].shape[0]
    for k, piece in enumerate(pieces):
        grad[pl.ds(pl.multiple_of((code[0] ^ k) * rows, rows), rows), :] = piece[...]
    g = grad[: relations.shape[0], :]
    total = state[...] + jnp.mean(g * g, axis=-1, keepdims=True)
    out[...] = relations[...] - learn_rate * g / jnp.sqrt(total)


def exchange(x, axis, mask):
    return lax.ppermute(x, axis, [(i, i ^ mask) for i in range(lax.axis_size(axis))])


def on_device(
    entity_table,
    entity_state,
    relations,
    relation_state,
    head_rows,
    tail_rows,
    relation_ids,
    negative_rows,
    edge_counts,
):
    n = lax.axis_size("sub")
    n_dom = lax.axis_size("dom")
    me_sub = lax.axis_index("sub")
    me_dom = lax.axis_index("dom")
    pair = n_dom // 2
    rows, dims = entity_table.shape
    slots = head_rows.shape[2]
    count = negative_rows.shape[2]
    per_source = slots // block
    rel_rows = -(-relations.shape[0] // 256) * 256
    near = min(4, n_dom)
    plane = near * n
    chunk = rel_rows // plane

    local = entity_table.T.astype(bf16)
    own_slab = [local] + [exchange(local, "sub", k) for k in range(1, n)]
    far_first = exchange(local, "dom", pair)
    far_slab = [far_first] + [exchange(far_first, "sub", k) for k in range(1, n)]
    ids = jnp.stack(
        [x.reshape(per_source, block) for x in (head_rows, tail_rows, relation_ids)], axis=1
    )
    small = jnp.concatenate([negative_rows.reshape(1, count), jnp.broadcast_to(edge_counts, (1, 128))], axis=1)
    all_ids = jnp.concatenate([ids] + [exchange(ids, "sub", k) for k in range(1, n)], axis=0)
    all_small = jnp.stack([small] + [exchange(small, "sub", k) for k in range(1, n)], axis=0)
    negatives = all_small[:, :, :count]
    counts = all_small[:, 0, count]

    spots = jnp.arange(n, dtype=jnp.int32)
    blocks = (counts + (block - 1)) // block
    before = jnp.sum(
        jnp.where((spots[None, :] ^ me_sub) < (spots[:, None] ^ me_sub), blocks[None, :], 0), axis=1
    )
    total = jnp.sum(blocks)
    low = me_sub * total // n
    high = (me_sub + 1) * total // n
    line = jnp.minimum(low + jnp.arange(per_source, dtype=jnp.int32), high - 1)
    inside = (line[:, None] >= before[None, :]) & (line[:, None] < (before + blocks)[None, :])
    source = jnp.sum(jnp.where(inside, spots[None, :], 0), axis=1)
    nth = jnp.sum(jnp.where(inside, line[:, None] - before[None, :], 0), axis=1)
    live = jnp.clip(
        jnp.sum(jnp.where(inside, counts[None, :], 0), axis=1) - nth * block, 0, block
    )
    steps = high - low
    place = source * per_source + nth
    near_code = (me_dom % near) * n + me_sub
    codes = jnp.stack([me_sub * rows, near_code * chunk, steps]).astype(jnp.int32)
    tables = (source, place, live, codes)

    params = pltpu.CompilerParams(vmem_limit_bytes=vmem_bytes)
    id_spec = pl.BlockSpec((1, 3, block), lambda i, s, p, l, c: (p[i], 0, 0))

    def whole(shape):
        return pl.BlockSpec(shape, lambda i, s, p, l, c: (0,) * len(shape))

    def stepped(*shape):
        return pl.BlockSpec((1, *shape), lambda i, s, p, l, c: (jnp.minimum(i, c[2] - 1),) + (0,) * len(shape))

    slab_specs = [whole((dims, rows))] * n
    sums = [jax.ShapeDtypeStruct((rows, dims), f32)] * n
    edge_work = per_source * block * dims
    head, operator = pl.pallas_call(
        functools.partial(query_kernel, n, rel_rows),
        grid_spec=pltpu.PrefetchScalarGridSpec(
            num_scalar_prefetch=4,
            grid=(per_source,),
            in_specs=[id_spec, whole(relations.shape), *slab_specs],
            out_specs=[stepped(dims, block), stepped(dims, block)],
            scratch_shapes=[pltpu.VMEM((rel_rows, dims), f32), pltpu.VMEM((2 * dims, rel_rows), bf16)],
        ),
        out_shape=[
            jax.ShapeDtypeStruct((per_source, dims, block), bf16),
            jax.ShapeDtypeStruct((per_source, dims, block), f32),
        ],
        compiler_params=params,
        cost_estimate=pl.CostEstimate(
            flops=2 * edge_work * (n * rows + 2 * rel_rows), bytes_accessed=6 * edge_work, transcendentals=0
        ),
        name="query_kernel",
    )(*tables, all_ids, relations, *own_slab)

    head_grad, operator_grad, *far_sum = pl.pallas_call(
        functools.partial(score_kernel, n),
        grid_spec=pltpu.PrefetchScalarGridSpec(
            num_scalar_prefetch=4,
            grid=(per_source,),
            in_specs=[
                id_spec,
                whole(negatives.shape),
                stepped(dims, block),
                stepped(dims, block),
                *slab_specs,
            ],
            out_specs=[stepped(2, dims, block), stepped(2, dims, block)] + [whole((rows, dims))] * n,
            scratch_shapes=[
                pltpu.VMEM((count, dims), bf16),
                pltpu.VMEM((dims, count), bf16),
                pltpu.VMEM((count, dims), f32),
            ],
        ),
        out_shape=[jax.ShapeDtypeStruct((per_source, 2, dims, block), bf16)] * 2 + sums,
        compiler_params=params,
        cost_estimate=pl.CostEstimate(
            flops=2 * edge_work * 3 * (n * rows + count), bytes_accessed=14 * edge_work, transcendentals=0
        ),
        name="score_kernel",
    )(*tables, all_ids, negatives, head, operator, *far_slab)

    far_total = far_sum[0]
    for k in range(1, n):
        far_total = far_total + exchange(far_sum[k], "sub", k)
    returned = exchange(far_total, "dom", pair)

    scattered = pl.pallas_call(
        functools.partial(scatter_kernel, n),
        grid_spec=pltpu.PrefetchScalarGridSpec(
            num_scalar_prefetch=4,
            grid=(per_source,),
            in_specs=[id_spec, stepped(2, dims, block), stepped(2, dims, block)],
            out_specs=[whole((rows, dims))] * n + [whole((chunk, dims))] * plane,
        ),
        out_shape=sums + [jax.ShapeDtypeStruct((chunk, dims), f32)] * plane,
        compiler_params=params,
        cost_estimate=pl.CostEstimate(
            flops=4 * edge_work * (n * rows + rel_rows), bytes_accessed=8 * edge_work, transcendentals=0
        ),
        name="scatter_kernel",
    )(*tables, all_ids, head_grad, operator_grad)
    own_sum, relation_sum = scattered[:n], scattered[n:]

    own_total = own_sum[0]
    for k in range(1, n):
        own_total = own_total + exchange(own_sum[k], "sub", k)

    def to_plane(x, mask):
        pairs = []
        for d in range(n_dom):
            for s in range(n):
                pairs.append((d * n + s, (d ^ (mask // n)) * n + (s ^ (mask % n))))
        return lax.ppermute(x, ("dom", "sub"), pairs)

    chunk_total = relation_sum[0]
    for k in range(1, plane):
        chunk_total = chunk_total + to_plane(relation_sum[k], k)
    mask = near
    while mask < n_dom:
        chunk_total = chunk_total + exchange(chunk_total, "dom", mask)
        mask *= 2
    chunks = [chunk_total] + [to_plane(chunk_total, k) for k in range(1, plane)]
    new_relations = pl.pallas_call(
        relation_kernel,
        in_specs=[pl.BlockSpec(memory_space=pltpu.SMEM)] + [pl.BlockSpec(memory_space=pltpu.VMEM)] * (2 + plane),
        out_shape=jax.ShapeDtypeStruct(relations.shape, f32),
        scratch_shapes=[pltpu.VMEM((rel_rows, dims), f32)],
        compiler_params=params,
        name="relation_kernel",
    )(near_code.reshape(1).astype(jnp.int32), relations, relation_state.reshape(-1, 1), *chunks)

    grad = own_total + returned
    new_state = entity_state + jnp.mean(grad * grad, axis=-1)
    new_table = entity_table - learn_rate * grad / jnp.sqrt(new_state)[:, None]
    return (new_table, new_state, new_relations)


def solution(mesh):
    in_specs = (
        P(("dom", "sub"), None),
        P(("dom", "sub")),
        P(),
        P(),
        P("dom", "sub", None),
        P("dom", "sub", None),
        P("dom", "sub", None),
        P("dom", "sub", None),
        P("dom", "sub"),
    )
    out_specs = (P(("dom", "sub"), None), P(("dom", "sub")), P())
    return jax.shard_map(
        on_device, mesh=mesh, in_specs=in_specs, out_specs=out_specs, check_vma=False
    )
```

```python
import functools

import jax
import jax.numpy as jnp
from jax import lax
from jax.experimental import pallas as pl
from jax.experimental.pallas import tpu as pltpu
from jax.sharding import PartitionSpec as P

learn_rate = 0.1
block = 512
bf16 = jnp.bfloat16
f32 = jnp.float32
vmem_bytes = 56 * 2**20


def dot(a, b):
    return jnp.dot(a, b, preferred_element_type=f32)


def dot_nt(a, b):
    return lax.dot_general(a, b, (((1,), (1,)), ((), ())), preferred_element_type=f32)


def one_hot(ids, rows):
    places = lax.broadcasted_iota(jnp.int16, (rows, ids.shape[1]), 0)
    return jnp.where(places == ids.astype(jnp.int16), jnp.ones((), bf16), jnp.zeros((), bf16))


def split(x):
    high = x.astype(bf16)
    return high, (x - high.astype(f32)).astype(bf16)


def gather_t(pieces, hot):
    rows = pieces[0].shape[1]
    total = dot(pieces[0][...], hot[:rows])
    for k in range(1, len(pieces)):
        total = total + dot(pieces[k][...], hot[k * rows : (k + 1) * rows])
    return total


def scatter_add(pieces, hot, values):
    start = 0
    for piece in pieces:
        part = hot[start : start + piece.shape[0]]
        start += piece.shape[0]
        total = dot_nt(part, values[0])
        for value in values[1:]:
            total = total + dot_nt(part, value)
        piece[...] += total


def edge_kernel(n, source, place, live, codes, ids, negatives, relations, *refs):
    near, away = refs[:n], refs[n : 2 * n]
    grad_out, near_sum, away_sum = refs[2 * n], refs[2 * n + 1 : 3 * n + 1], refs[3 * n + 1 : 4 * n + 1]
    relation_sum = refs[4 * n + 1 : -5]
    rel_full, rel_split, table, table_t, negative_grad = refs[-5:]
    step = pl.program_id(0)
    steps = codes[2]
    rows = near[0].shape[1]
    dims = relations.shape[1]
    rel_rows = rel_full.shape[0]
    here = source[step]
    swapped = here >= n
    count = table.shape[0]

    @pl.when(step == 0)
    def _():
        for piece in (*near_sum, *away_sum, *relation_sum):
            piece[...] = jnp.zeros_like(piece)
        rel_full[...] = jnp.zeros_like(rel_full)
        rel_full[: relations.shape[0], :] = relations[...]
        high, low = split(rel_full[...].T)
        rel_split[:dims, :] = high
        rel_split[dims:, :] = low

    def take_table(slab):
        found = gather_t(slab, one_hot(negatives[here] ^ codes[0], n * rows))
        table_t[...] = found.astype(bf16)
        table[...] = found.T.astype(bf16)
        negative_grad[...] = jnp.zeros_like(negative_grad)

    fresh = (step < steps) & ((step == 0) | (source[jnp.maximum(step - 1, 0)] != here))
    pl.when(fresh & ~swapped)(lambda: take_table(away))
    pl.when(fresh & swapped)(lambda: take_table(near))

    @pl.when(step < steps)
    def _():
        width = ids.shape[2]
        entries = ids[0].astype(jnp.int32)
        heads, tails, kinds = entries[0:1], entries[1:2], entries[2:3]
        alive = (lax.broadcasted_iota(jnp.int32, (1, width), 1) < live[step]).astype(f32)
        near_ids = jnp.where(swapped, tails, heads) ^ codes[0]
        away_hot = one_hot(jnp.where(swapped, heads, tails) ^ codes[0], n * rows)
        near_rows = gather_t(near, one_hot(near_ids, n * rows))
        away_rows = gather_t(away, away_hot)
        head = jnp.where(swapped, away_rows, near_rows)
        tail = jnp.where(swapped, near_rows, away_rows)
        both = dot(rel_split[...], one_hot(kinds, rel_rows))
        operator = both[:dims] + both[dims:]
        query = head * operator
        query_b = query.astype(bf16)
        positive = jnp.sum(query * tail, axis=0, keepdims=True)
        scores = dot(table[...], query_b)
        pos_coef = -jax.nn.sigmoid(-positive) * alive
        neg_coef = (jax.nn.sigmoid(scores) * (alive * (1.0 / count))).astype(bf16)
        query_grad = pos_coef * tail + dot(table_t[...], neg_coef)
        negative_grad[...] += dot_nt(neg_coef, query_b)
        head_grad = query_grad * operator
        tail_grad = pos_coef * query
        grad_out[0, 0], grad_out[0, 1] = split(jnp.where(swapped, tail_grad, head_grad))
        scatter_add(away_sum, away_hot, split(jnp.where(swapped, head_grad, tail_grad)))
        scatter_add(relation_sum, one_hot(kinds ^ codes[1], rel_rows), split(query_grad * head))

    def add_negatives(sums):
        chosen = one_hot(negatives[here] ^ codes[0], n * rows)
        high, low = split(negative_grad[...])
        for k, piece in enumerate(sums):
            part = chosen[k * rows : (k + 1) * rows]
            piece[...] += dot(part, high) + dot(part, low)

    final = (step == steps - 1) | ((step < steps) & (source[jnp.minimum(step + 1, steps - 1)] != here))
    pl.when(final & ~swapped)(lambda: add_negatives(away_sum))
    pl.when(final & swapped)(lambda: add_negatives(near_sum))


def near_kernel(n, source, place, live, codes, ids, grads, *refs):
    base, sums = refs[:n], refs[n:]
    rows = sums[0].shape[0]
    step = pl.program_id(0)

    @pl.when(step == 0)
    def _():
        for start, piece in zip(base, sums, strict=True):
            piece[...] = start[...]

    @pl.when(step < codes[2])
    def _():
        entries = ids[0].astype(jnp.int32)
        near_ids = jnp.where(source[step] >= n, entries[1:2], entries[0:1]) ^ codes[0]
        scatter_add(sums, one_hot(near_ids, n * rows), (grads[0, 0], grads[0, 1]))


def entity_kernel(n, table, state, returned, *refs):
    parts, (new_table, new_state) = refs[:n], refs[n:]
    grad = returned[...]
    for part in parts:
        grad = grad + part[...]
    lanes = 128
    before = jnp.broadcast_to(state[...], (lanes, table.shape[0])).T[:, :1]
    after = before + jnp.mean(grad * grad, axis=-1, keepdims=True)
    new_table[...] = table[...] - learn_rate * grad / jnp.sqrt(after)
    new_state[...] = jnp.broadcast_to(after, (table.shape[0], lanes)).T[:1]


def relation_kernel(chunk, code, relations, state, mine, theirs, out, grad):
    chunks = mine.shape[0] // chunk
    for k in range(2 * chunks):
        part = (mine, theirs)[k // chunks]
        start = (k % chunks) * chunk
        grad[pl.ds(pl.multiple_of((code[0] ^ k) * chunk, chunk), chunk), :] = part[start : start + chunk, :]
    g = grad[: relations.shape[0], :]
    total = state[...] + jnp.mean(g * g, axis=-1, keepdims=True)
    out[...] = relations[...] - learn_rate * g / jnp.sqrt(total)


def exchange(x, axis, mask):
    return lax.ppermute(x, axis, [(i, i ^ mask) for i in range(lax.axis_size(axis))])


def on_device(
    entity_table,
    entity_state,
    relations,
    relation_state,
    head_rows,
    tail_rows,
    relation_ids,
    negative_rows,
    edge_counts,
):
    n = lax.axis_size("sub")
    n_dom = lax.axis_size("dom")
    me_sub = lax.axis_index("sub")
    me_dom = lax.axis_index("dom")
    pair = n_dom // 2
    rows, dims = entity_table.shape
    slots = head_rows.shape[2]
    count = negative_rows.shape[2]
    per_source = slots // block
    rel_rows = -(-relations.shape[0] // 256) * 256
    chips = 2 * n
    chunk = rel_rows // (2 * chips)

    local = entity_table.T.astype(bf16)
    away_first = exchange(local, "dom", pair)
    near_slab = [local] + [exchange(local, "sub", k) for k in range(1, n)]
    away_slab = [away_first] + [exchange(away_first, "sub", k) for k in range(1, n)]

    def from_pair(x):
        across = exchange(x, "dom", pair)
        return [x, *(exchange(x, "sub", k) for k in range(1, n)), across, *(exchange(across, "sub", k) for k in range(1, n))]

    ids = jnp.stack(
        [x.reshape(per_source, block) for x in (head_rows, tail_rows, relation_ids)], axis=1
    ).astype(jnp.int16)
    small = jnp.concatenate([negative_rows.reshape(1, count), jnp.broadcast_to(edge_counts, (1, 128))], axis=1)
    all_ids = jnp.concatenate(from_pair(ids), axis=0)
    all_small = jnp.stack(from_pair(small), axis=0)
    negatives = all_small[:, :, :count]
    counts = all_small[:, 0, count]

    team = 2 * n
    me = (me_dom // pair) * n + me_sub
    spots = jnp.arange(team, dtype=jnp.int32)
    blocks = (counts + (block - 1)) // block
    before = jnp.sum(jnp.where((spots[None, :] ^ me) < (spots[:, None] ^ me), blocks[None, :], 0), axis=1)
    total = jnp.sum(blocks)
    low = me * total // team
    high = (me + 1) * total // team
    line = jnp.minimum(low + jnp.arange(per_source, dtype=jnp.int32), high - 1)
    inside = (line[:, None] >= before[None, :]) & (line[:, None] < (before + blocks)[None, :])
    source = jnp.sum(jnp.where(inside, spots[None, :], 0), axis=1)
    nth = jnp.sum(jnp.where(inside, line[:, None] - before[None, :], 0), axis=1)
    live = jnp.clip(
        jnp.sum(jnp.where(inside, counts[None, :], 0), axis=1) - nth * block, 0, block
    )
    place = source * per_source + nth
    chunk_code = (me_dom % 2) * chips + (me_dom // 2 % 2) * n + me_sub
    codes = jnp.stack([me_sub * rows, chunk_code * chunk, high - low]).astype(jnp.int32)
    tables = (source, place, live, codes)

    params = pltpu.CompilerParams(vmem_limit_bytes=vmem_bytes)
    id_spec = pl.BlockSpec((1, 3, block), lambda i, s, p, l, c: (p[i], 0, 0))

    def whole(shape):
        return pl.BlockSpec(shape, lambda i, s, p, l, c: (0,) * len(shape))

    grad_spec = pl.BlockSpec((1, 2, dims, block), lambda i, s, p, l, c: (jnp.minimum(i, c[2] - 1), 0, 0, 0))
    sums = [jax.ShapeDtypeStruct((rows, dims), f32)] * n
    edge_work = per_source * block * dims
    pieces = [(chunk, dims)] * chips + [(chips * chunk, dims)]
    grads, *found = pl.pallas_call(
        functools.partial(edge_kernel, n),
        grid_spec=pltpu.PrefetchScalarGridSpec(
            num_scalar_prefetch=4,
            grid=(per_source,),
            in_specs=[id_spec, whole(negatives.shape), whole(relations.shape)] + [whole((dims, rows))] * team,
            out_specs=[grad_spec] + [whole((rows, dims))] * team + [whole(x) for x in pieces],
            scratch_shapes=[
                pltpu.VMEM((rel_rows, dims), f32),
                pltpu.VMEM((2 * dims, rel_rows), bf16),
                pltpu.VMEM((count, dims), bf16),
                pltpu.VMEM((dims, count), bf16),
                pltpu.VMEM((count, dims), f32),
            ],
        ),
        out_shape=[jax.ShapeDtypeStruct((per_source, 2, dims, block), bf16)]
        + sums * 2
        + [jax.ShapeDtypeStruct(x, f32) for x in pieces],
        compiler_params=params,
        cost_estimate=pl.CostEstimate(
            flops=2 * edge_work * (4 * n * rows + 3 * count + 4 * rel_rows), bytes_accessed=8 * edge_work, transcendentals=0
        ),
        name="edge_kernel",
    )(*tables, all_ids, negatives, relations, *near_slab, *away_slab)
    near_base, away_sum, relation_keep, relation_send = found[:n], found[n:team], found[team:-1], found[-1]

    away_total = away_sum[0]
    for k in range(1, n):
        away_total = away_total + exchange(away_sum[k], "sub", k)
    returned = exchange(away_total, "dom", pair)

    def to_chip(x, mask):
        pairs = []
        for d in range(n_dom):
            for s in range(n):
                pairs.append((d * n + s, (d ^ (mask // n * 2)) * n + (s ^ (mask % n))))
        return lax.ppermute(x, ("dom", "sub"), pairs)

    other_core = exchange(relation_send, "dom", 1)
    parts = [relation_keep[k] + other_core[k * chunk : (k + 1) * chunk] for k in range(chips)]
    chunk_total = parts[0]
    for k in range(1, chips):
        chunk_total = chunk_total + to_chip(parts[k], k)
    mask = 4
    while mask < n_dom:
        chunk_total = chunk_total + exchange(chunk_total, "dom", mask)
        mask *= 2
    mine = jnp.concatenate([chunk_total] + [to_chip(chunk_total, k) for k in range(1, chips)], axis=0)
    theirs = exchange(mine, "dom", 1)

    near_sum = pl.pallas_call(
        functools.partial(near_kernel, n),
        grid_spec=pltpu.PrefetchScalarGridSpec(
            num_scalar_prefetch=4,
            grid=(per_source,),
            in_specs=[id_spec, grad_spec] + [whole((rows, dims))] * n,
            out_specs=[whole((rows, dims))] * n,
        ),
        out_shape=sums,
        compiler_params=params,
        cost_estimate=pl.CostEstimate(
            flops=2 * edge_work * n * rows, bytes_accessed=4 * edge_work, transcendentals=0
        ),
        name="near_kernel",
    )(*tables, all_ids, grads, *near_base)

    in_vmem = pl.BlockSpec(memory_space=pltpu.VMEM)
    new_table, new_state = pl.pallas_call(
        functools.partial(entity_kernel, n),
        in_specs=[in_vmem] * (3 + n),
        out_specs=[in_vmem] * 2,
        out_shape=[jax.ShapeDtypeStruct((rows, dims), f32), jax.ShapeDtypeStruct((1, rows), f32)],
        compiler_params=params,
        name="entity_kernel",
    )(
        entity_table,
        entity_state.reshape(1, rows),
        returned,
        near_sum[0],
        *(exchange(near_sum[k], "sub", k) for k in range(1, n)),
    )
    theirs, new_table, new_state = lax.optimization_barrier((theirs, new_table, new_state))
    new_relations = pl.pallas_call(
        functools.partial(relation_kernel, chunk),
        in_specs=[pl.BlockSpec(memory_space=pltpu.SMEM)] + [in_vmem] * 4,
        out_specs=in_vmem,
        out_shape=jax.ShapeDtypeStruct(relations.shape, f32),
        scratch_shapes=[pltpu.VMEM((rel_rows, dims), f32)],
        compiler_params=params,
        name="relation_kernel",
    )(chunk_code.reshape(1).astype(jnp.int32), relations, relation_state.reshape(-1, 1), mine, theirs)
    return (new_table, new_state.reshape(rows), new_relations)


def solution(mesh):
    in_specs = (
        P(("dom", "sub"), None),
        P(("dom", "sub")),
        P(),
        P(),
        P("dom", "sub", None),
        P("dom", "sub", None),
        P("dom", "sub", None),
        P("dom", "sub", None),
        P("dom", "sub"),
    )
    out_specs = (P(("dom", "sub"), None), P(("dom", "sub")), P())
    return jax.shard_map(
        on_device, mesh=mesh, in_specs=in_specs, out_specs=out_specs, check_vma=False
    )
```

```python
import functools

import jax
import jax.numpy as jnp
from jax import lax
from jax.experimental import pallas as pl
from jax.experimental.pallas import tpu as pltpu
from jax.sharding import PartitionSpec as P

learn_rate = 0.1
bf16 = jnp.bfloat16
f32 = jnp.float32
i32 = jnp.int32
params = pltpu.CompilerParams(vmem_limit_bytes=56 * 2**20)


def dot(a, b):
    return jnp.dot(a, b, preferred_element_type=f32)


def dot_nt(a, b):
    return lax.dot_general(a, b, (((1,), (1,)), ((), ())), preferred_element_type=f32)


def one_hot(ids, rows):
    places = lax.broadcasted_iota(jnp.int16, (rows, ids.shape[1]), 0)
    return jnp.where(places == ids.astype(jnp.int16), jnp.ones((), bf16), jnp.zeros((), bf16))


def split(x):
    high = x.astype(bf16)
    return jnp.concatenate([high, (x - high.astype(f32)).astype(bf16)], axis=1)


def gather(pieces, ids):
    rows = pieces[0].shape[1]
    hot = one_hot(ids, len(pieces) * rows)
    total = dot(pieces[0][...], hot[:rows])
    for k in range(1, len(pieces)):
        total = total + dot(pieces[k][...], hot[k * rows : (k + 1) * rows])
    return total


def scatter_add(pieces, ids, pair):
    hot = one_hot(ids, sum(piece.shape[0] for piece in pieces))
    hot = jnp.concatenate([hot, hot], axis=1)
    start = 0
    for piece in pieces:
        piece[...] += dot_nt(hot[start : start + piece.shape[0]], pair)
        start += piece.shape[0]


def prep_kernel(count, table, heads, tails, kinds, negatives, rows_out, ids_out):
    rows_out[...] = table[...].T.astype(bf16)
    blocks, _, width = ids_out.shape
    for j in range(blocks - 1):
        at = slice(j * width, (j + 1) * width)
        block = jnp.concatenate([heads[:, at], tails[:, at], kinds[:, at]], axis=0)
        ids_out[j] = block.astype(jnp.int16)
    last = jnp.concatenate([negatives[...], jnp.full((2, width), count[0, 0], i32)], axis=0)
    ids_out[blocks - 1] = last.astype(jnp.int16)


def plan_kernel(n, codes, *refs):
    sources, (plan, step_ids, negative_ids) = refs[:-3], refs[-3:]
    team = len(sources)
    most, _, width = step_ids.shape
    me = codes[0]
    counts, blocks = [], []
    for k, ids in enumerate(sources):
        last = ids[most].astype(i32)
        counts.append(jnp.max(last[1:2]))
        blocks.append(lax.div(counts[k] + (width - 1), i32(width)))
        negative_ids[k] = last[0:1] ^ codes[1]
    total = sum(blocks)
    low = lax.div(me * total, i32(team))
    high = lax.div((me + 1) * total, i32(team))
    plan[2 * most] = high - low
    before = []
    for k in range(team):
        ahead = [jnp.where((me ^ j) < (me ^ k), blocks[j], 0) for j in range(team) if j != k]
        before.append(sum(ahead))
        seen = (before[k] < high) & (before[k] + blocks[k] > low)
        plan[2 * most + 1 + k] = seen.astype(i32)

    def one_step(i, carry):
        line = jnp.minimum(low + i, high - 1)
        for k, ids in enumerate(sources):

            @pl.when((line >= before[k]) & (line < before[k] + blocks[k]))
            def _(k=k, ids=ids):
                nth = line - before[k]
                plan[i] = k
                plan[most + i] = jnp.clip(counts[k] - nth * width, 0, width)
                entries = ids[nth].astype(i32)
                near, away = (0, 1) if k < n else (1, 0)
                step_ids[i, 0:1] = entries[near : near + 1] ^ codes[1]
                step_ids[i, 1:2] = entries[away : away + 1] ^ codes[1]
                step_ids[i, 2:3] = entries[2:3]
                step_ids[i, 3:4] = entries[2:3] ^ codes[2]

        return carry

    lax.fori_loop(0, most, one_step, 0)


def near_kernel(plan, ids, relations, *refs):
    slab, (rows_out, operator_out, rel_full, rel_split) = refs[:-4], refs[-4:]
    dims = relations.shape[1]

    @pl.when(pl.program_id(0) == 0)
    def _():
        rel_full[...] = jnp.zeros_like(rel_full)
        rel_full[: relations.shape[0], :] = relations[...]
        full = rel_full[...].T
        high = full.astype(bf16)
        rel_split[:dims, :] = high
        rel_split[dims:, :] = (full - high.astype(f32)).astype(bf16)

    @pl.when(pl.program_id(0) < plan[2 * pl.num_programs(0)])
    def _():
        rows_out[0] = gather(slab, ids[0, 0:1, :]).astype(bf16)
        both = dot(rel_split[...], one_hot(ids[0, 2:3, :], rel_full.shape[0]))
        operator_out[0] = both[:dims] + both[dims:]


def edge_kernel(n, plan, ids, negative_ids, near_in, operator_in, *refs):
    near, away = refs[:n], refs[n : 2 * n]
    near_grad, away_grad, negative_out = refs[2 * n : 2 * n + 3]
    relation_sum, (table, table_t, negative_grad) = refs[2 * n + 3 : -3], refs[-3:]
    step = pl.program_id(0)
    most = pl.num_programs(0)
    steps = plan[2 * most]
    here = plan[step]
    swapped = here >= n
    count = table.shape[0]

    @pl.when(step == 0)
    def _():
        for piece in relation_sum:
            piece[...] = jnp.zeros_like(piece)

    def take_table(slab):
        found = gather(slab, negative_ids[here])
        table_t[...] = found.astype(bf16)
        table[...] = found.T.astype(bf16)
        negative_grad[...] = jnp.zeros_like(negative_grad)

    fresh = (step < steps) & ((step == 0) | (plan[jnp.maximum(step - 1, 0)] != here))
    pl.when(fresh & ~swapped)(lambda: take_table(away))
    pl.when(fresh & swapped)(lambda: take_table(near))

    @pl.when(step < steps)
    def _():
        width = ids.shape[2]
        alive = (lax.broadcasted_iota(i32, (1, width), 1) < plan[most + step]).astype(f32)
        near_rows = near_in[0].astype(f32)
        away_rows = gather(away, ids[0, 1:2, :])
        head = jnp.where(swapped, away_rows, near_rows)
        tail = jnp.where(swapped, near_rows, away_rows)
        operator = operator_in[0]
        query = head * operator
        query_b = query.astype(bf16)
        positive = jnp.sum(query * tail, axis=0, keepdims=True)
        scores = dot(table[...], query_b)
        pos_coef = -jax.nn.sigmoid(-positive) * alive
        neg_coef = (jax.nn.sigmoid(scores) * (alive * (1.0 / count))).astype(bf16)
        query_grad = pos_coef * tail + dot(table_t[...], neg_coef)
        negative_grad[...] += dot_nt(query_b, neg_coef)
        head_grad = query_grad * operator
        tail_grad = pos_coef * query
        near_grad[0] = split(jnp.where(swapped, tail_grad, head_grad))
        away_grad[0] = split(jnp.where(swapped, head_grad, tail_grad))
        scatter_add(relation_sum, ids[0, 3:4, :], split(query_grad * head))

    @pl.when((step == steps - 1) | ((step < steps) & (plan[jnp.minimum(step + 1, steps - 1)] != here)))
    def _():
        negative_out[0] = split(negative_grad[...])


def scatter_kernel(most, row, start, first, plan, ids, negative_ids, grads, negative_grads, *sums):
    step = pl.program_id(0)

    @pl.when(step == 0)
    def _():
        for piece in sums:
            piece[...] = jnp.zeros_like(piece)

    @pl.when(step < plan[2 * most])
    def _():
        scatter_add(sums, ids[0, row : row + 1, :] - start, grads[0])

    @pl.when((step >= most) & (plan[2 * most + 1 + first + jnp.maximum(step - most, 0)] != 0))
    def _():
        scatter_add(sums, negative_ids[0] - start, negative_grads[0])


def entity_kernel(n, table, state, returned, *refs):
    parts, (new_table, new_state) = refs[:n], refs[n:]
    grad = returned[...]
    for part in parts:
        grad = grad + part[...]
    lanes = 128
    before = jnp.broadcast_to(state[...], (lanes, table.shape[0])).T[:, :1]
    after = before + jnp.mean(grad * grad, axis=-1, keepdims=True)
    new_table[...] = table[...] - learn_rate * grad / jnp.sqrt(after)
    new_state[...] = jnp.broadcast_to(after, (table.shape[0], lanes)).T[:1]


def relation_kernel(chunk, codes, relations, state, mine, theirs, out, grad):
    chunks = mine.shape[0] // chunk
    for k in range(2 * chunks):
        part = (mine, theirs)[k // chunks]
        start = (k % chunks) * chunk
        grad[pl.ds(pl.multiple_of(codes[2] ^ (k * chunk), chunk), chunk), :] = part[start : start + chunk, :]
    g = grad[: relations.shape[0], :]
    total = state[...] + jnp.mean(g * g, axis=-1, keepdims=True)
    out[...] = relations[...] - learn_rate * g / jnp.sqrt(total)


def exchange(x, axis, mask):
    return lax.ppermute(x, axis, [(i, i ^ mask) for i in range(lax.axis_size(axis))])


def on_device(
    entity_table,
    entity_state,
    relations,
    relation_state,
    head_rows,
    tail_rows,
    relation_ids,
    negative_rows,
    edge_counts,
):
    n = lax.axis_size("sub")
    n_dom = lax.axis_size("dom")
    me_sub = lax.axis_index("sub")
    me_dom = lax.axis_index("dom")
    pair = n_dom // 2
    team = 2 * n
    rows, dims = entity_table.shape
    slots = head_rows.shape[2]
    count = negative_rows.shape[2]
    width = count
    most = slots // width
    rel_rows = -(-relations.shape[0] // 256) * 256
    chips = 2 * n
    chunk = rel_rows // (2 * chips)
    shape = jax.ShapeDtypeStruct
    in_vmem = pl.BlockSpec(memory_space=pltpu.VMEM)
    in_smem = pl.BlockSpec(memory_space=pltpu.SMEM)

    me = lax.shift_right_logical(me_dom, pair.bit_length() - 1) * n + me_sub
    chunk_code = (me_dom & 1) * chips + ((me_dom >> 1) & 1) * n + me_sub
    codes = jnp.stack([me, me_sub * rows, chunk_code * chunk]).astype(i32)

    local, ids = pl.pallas_call(
        prep_kernel,
        in_specs=[in_smem] + [in_vmem] * 5,
        out_specs=[in_vmem] * 2,
        out_shape=[shape((dims, rows), bf16), shape((most + 1, 3, width), jnp.int16)],
        compiler_params=params,
        name="prep_kernel",
    )(
        edge_counts,
        entity_table,
        head_rows.reshape(1, slots),
        tail_rows.reshape(1, slots),
        relation_ids.reshape(1, slots),
        negative_rows.reshape(1, count),
    )

    def along_sub(x):
        return [x] + [exchange(x, "sub", k) for k in range(1, n)]

    away_slab = along_sub(exchange(local, "dom", pair))
    all_ids = along_sub(ids) + along_sub(exchange(ids, "dom", pair))
    near_slab = along_sub(local)

    plan, step_ids, negative_ids = pl.pallas_call(
        functools.partial(plan_kernel, n),
        in_specs=[in_smem] + [in_vmem] * team,
        out_specs=[in_smem, in_vmem, in_vmem],
        out_shape=[
            shape((2 * most + 1 + team,), i32),
            shape((most, 4, width), i32),
            shape((team, 1, width), i32),
        ],
        compiler_params=params,
        name="plan_kernel",
    )(codes, *all_ids)

    def whole(*dims):
        return pl.BlockSpec(dims, lambda i, p: (0,) * len(dims))

    def stepped(*dims):
        return pl.BlockSpec((1, *dims), lambda i, p: (jnp.minimum(i, p[2 * most] - 1),) + (0,) * len(dims))

    def call(kernel, name, grid, in_specs, outs, scratch, unit, args):
        return pl.pallas_call(
            kernel,
            grid_spec=pltpu.PrefetchScalarGridSpec(
                num_scalar_prefetch=1,
                grid=(grid,),
                in_specs=in_specs,
                out_specs=[spec for spec, _ in outs],
                scratch_shapes=scratch,
            ),
            out_shape=[x for _, x in outs],
            compiler_params=params,
            cost_estimate=pl.CostEstimate(
                flops=2 * slots * dims * unit, bytes_accessed=4 * slots * dims, transcendentals=0
            ),
            name=name,
        )(plan, *args)

    id_spec = stepped(4, width)
    slab_specs = [whole(dims, rows)] * n
    near_rows, operator = call(
        near_kernel,
        "near_kernel",
        most,
        [id_spec, whole(*relations.shape)] + slab_specs,
        [
            (stepped(dims, width), shape((most, dims, width), bf16)),
            (stepped(dims, width), shape((most, dims, width), f32)),
        ],
        [pltpu.VMEM((rel_rows, dims), f32), pltpu.VMEM((2 * dims, rel_rows), bf16)],
        n * rows + 2 * rel_rows,
        (step_ids, relations, *near_slab),
    )

    grad_out = (stepped(dims, 2 * width), shape((most, dims, 2 * width), bf16))
    pieces = [(chunk, dims)] * chips + [(chips * chunk, dims)]
    near_grad, away_grad, negative_grad, *relation_part = call(
        functools.partial(edge_kernel, n),
        "edge_kernel",
        most,
        [id_spec, whole(team, 1, width), stepped(dims, width), stepped(dims, width)] + slab_specs * 2,
        [
            grad_out,
            grad_out,
            (
                pl.BlockSpec((1, dims, 2 * width), lambda i, p: (p[jnp.minimum(i, p[2 * most] - 1)], 0, 0)),
                shape((team, dims, 2 * width), bf16),
            ),
        ]
        + [(whole(*x), shape(x, f32)) for x in pieces],
        [pltpu.VMEM((count, dims), bf16), pltpu.VMEM((dims, count), bf16), pltpu.VMEM((dims, count), f32)],
        n * rows + 3 * count + 2 * rel_rows,
        (step_ids, negative_ids, near_rows, operator, *near_slab, *away_slab),
    )

    def scatter(name, row, start, parts, first, grads):
        def negative_spec(*dims):
            return pl.BlockSpec((1, *dims), lambda i, p: (first + jnp.maximum(i - most, 0),) + (0,) * len(dims))

        return call(
            functools.partial(scatter_kernel, most, row, start, first),
            name,
            most + n,
            [id_spec, negative_spec(1, width), stepped(dims, 2 * width), negative_spec(dims, 2 * width)],
            [(whole(rows, dims), shape((rows, dims), f32))] * parts,
            [],
            2 * parts * rows,
            (step_ids, negative_ids, grads, negative_grad),
        )

    away_other = scatter("away_other_kernel", 1, rows, n - 1, 0, away_grad)
    away_mine = scatter("away_mine_kernel", 1, 0, 1, 0, away_grad)
    away_total = away_mine[0]
    for k in range(1, n):
        away_total = away_total + exchange(away_other[k - 1], "sub", k)
    returned = exchange(away_total, "dom", pair)

    def to_chip(x, mask):
        pairs = []
        for d in range(n_dom):
            for s in range(n):
                pairs.append((d * n + s, (d ^ (mask // n * 2)) * n + (s ^ (mask % n))))
        return lax.ppermute(x, ("dom", "sub"), pairs)

    other_core = exchange(relation_part[chips], "dom", 1)
    parts = [relation_part[k] + other_core[k * chunk : (k + 1) * chunk] for k in range(chips)]
    chunk_total = parts[0]
    for k in range(1, chips):
        chunk_total = chunk_total + to_chip(parts[k], k)
    mask = 4
    while mask < n_dom:
        chunk_total = chunk_total + exchange(chunk_total, "dom", mask)
        mask *= 2
    mine = jnp.concatenate([chunk_total] + [to_chip(chunk_total, k) for k in range(1, chips)], axis=0)
    theirs = exchange(mine, "dom", 1)

    near_grad, away_total = lax.optimization_barrier((near_grad, away_total))
    near_sum = scatter("own_kernel", 0, 0, n, n, near_grad)

    new_table, new_state = pl.pallas_call(
        functools.partial(entity_kernel, n),
        in_specs=[in_vmem] * (3 + n),
        out_specs=[in_vmem] * 2,
        out_shape=[shape((rows, dims), f32), shape((1, rows), f32)],
        compiler_params=params,
        name="entity_kernel",
    )(
        entity_table,
        entity_state.reshape(1, rows),
        returned,
        near_sum[0],
        *(exchange(near_sum[k], "sub", k) for k in range(1, n)),
    )
    new_relations = pl.pallas_call(
        functools.partial(relation_kernel, chunk),
        in_specs=[in_smem] + [in_vmem] * 4,
        out_specs=in_vmem,
        out_shape=shape(relations.shape, f32),
        scratch_shapes=[pltpu.VMEM((rel_rows, dims), f32)],
        compiler_params=params,
        name="relation_kernel",
    )(codes, relations, relation_state.reshape(-1, 1), mine, theirs)
    return (new_table, new_state.reshape(rows), new_relations)


def solution(mesh):
    in_specs = (
        P(("dom", "sub"), None),
        P(("dom", "sub")),
        P(),
        P(),
        P("dom", "sub", None),
        P("dom", "sub", None),
        P("dom", "sub", None),
        P("dom", "sub", None),
        P("dom", "sub"),
    )
    out_specs = (P(("dom", "sub"), None), P(("dom", "sub")), P())
    return jax.shard_map(
        on_device, mesh=mesh, in_specs=in_specs, out_specs=out_specs, check_vma=False
    )
```

```python
import functools

import jax
import jax.numpy as jnp
from jax import lax
from jax.experimental import pallas as pl
from jax.experimental.pallas import tpu as pltpu
from jax.sharding import PartitionSpec as P

learn_rate = 0.1
bf16 = jnp.bfloat16
f32 = jnp.float32
i32 = jnp.int32
params = pltpu.CompilerParams(vmem_limit_bytes=10 * 2**20)


def dot(a, b):
    return jnp.dot(a, b, preferred_element_type=f32)


def dot_nt(a, b):
    return lax.dot_general(a, b, (((1,), (1,)), ((), ())), preferred_element_type=f32)


def one_hot(ids, rows):
    places = lax.broadcasted_iota(jnp.int16, (rows, ids.shape[1]), 0)
    return jnp.where(places == ids.astype(jnp.int16), jnp.ones((), bf16), jnp.zeros((), bf16))


def split(x):
    high = x.astype(bf16)
    return jnp.concatenate([high, (x - high.astype(f32)).astype(bf16)], axis=0)


def gather(pieces, ids):
    rows = pieces[0].shape[1]
    hot = one_hot(ids, len(pieces) * rows)
    total = dot(pieces[0][...], hot[:rows])
    for k in range(1, len(pieces)):
        total = total + dot(pieces[k][...], hot[k * rows : (k + 1) * rows])
    return total


def scatter_add(pieces, ids, pair):
    dims = pair.shape[0] // 2
    hot = one_hot(ids, sum(piece.shape[0] for piece in pieces))
    start = 0
    for piece in pieces:
        part = hot[start : start + piece.shape[0]]
        piece[...] += dot_nt(part, pair[:dims]) + dot_nt(part, pair[dims:])
        start += piece.shape[0]


def add_negatives(pieces, ids, pair):
    count = pair.shape[0] // 2
    hot = one_hot(ids, sum(piece.shape[0] for piece in pieces))
    start = 0
    for piece in pieces:
        part = hot[start : start + piece.shape[0]]
        piece[...] += dot(part, pair[:count]) + dot(part, pair[count:])
        start += piece.shape[0]


def prep_kernel(count, table, heads, tails, kinds, negatives, *refs):
    rows_out, ids_out = refs[:-1], refs[-1]
    each = rows_out[0].shape[1]
    for k, out in enumerate(rows_out):
        out[...] = table[k * each : (k + 1) * each, :].T.astype(bf16)
    blocks, _, width = ids_out.shape
    for j in range(blocks - 1):
        at = slice(j * width, (j + 1) * width)
        block = jnp.concatenate([heads[:, at], tails[:, at], kinds[:, at]], axis=0)
        ids_out[j] = block.astype(jnp.int16)
    last = jnp.concatenate([negatives[...], jnp.full((2, width), count[0, 0], i32)], axis=0)
    ids_out[blocks - 1] = last.astype(jnp.int16)


def plan_kernel(n, codes, *refs):
    sources, (plan, step_ids, negative_ids) = refs[:-3], refs[-3:]
    team = len(sources)
    most, _, width = step_ids.shape
    me = codes[0]
    counts, blocks = [], []
    for k, ids in enumerate(sources):
        last = ids[most].astype(i32)
        counts.append(jnp.max(last[1:2]))
        blocks.append(lax.div(counts[k] + (width - 1), i32(width)))
        negative_ids[k] = last[0:1] ^ codes[1]
    total = sum(blocks)
    low = lax.div(me * total, i32(team))
    high = lax.div((me + 1) * total, i32(team))
    plan[2 * most] = high - low
    before = []
    for k in range(team):
        ahead = [jnp.where((me ^ j) < (me ^ k), blocks[j], 0) for j in range(team) if j != k]
        before.append(sum(ahead))
        seen = (before[k] < high) & (before[k] + blocks[k] > low)
        plan[2 * most + 1 + k] = seen.astype(i32)

    def one_step(i, carry):
        line = jnp.minimum(low + i, high - 1)
        for k, ids in enumerate(sources):

            @pl.when((line >= before[k]) & (line < before[k] + blocks[k]))
            def _(k=k, ids=ids):
                nth = line - before[k]
                plan[i] = k
                plan[most + i] = jnp.clip(counts[k] - nth * width, 0, width)
                entries = ids[nth].astype(i32)
                near, away = (0, 1) if k < n else (1, 0)
                step_ids[i, 0:1] = entries[near : near + 1] ^ codes[1]
                step_ids[i, 1:2] = entries[away : away + 1] ^ codes[1]
                step_ids[i, 2:3] = entries[2:3]
                step_ids[i, 3:4] = entries[2:3] ^ codes[2]

        return carry

    lax.fori_loop(0, most, one_step, 0)


def near_kernel(plan, ids, relations, *refs):
    slab, (rows_out, operator_out, rel_full, rel_split) = refs[:-4], refs[-4:]
    dims = relations.shape[1]
    rel_full[...] = jnp.zeros_like(rel_full)
    rel_full[: relations.shape[0], :] = relations[...]
    rel_split[...] = split(rel_full[...].T)

    def one_block(i, carry):
        entries = ids[i]
        rows_out[i] = gather(slab, entries[0:1]).astype(bf16)
        both = dot(rel_split[...], one_hot(entries[2:3], rel_full.shape[0]))
        operator_out[i] = both[:dims] + both[dims:]
        return carry

    lax.fori_loop(0, plan[2 * ids.shape[0]], one_block, 0)


def edge_kernel(n, parts, plan, ids, negative_ids, near_in, operator_in, *refs):
    near, away = refs[:parts], refs[parts : 2 * parts]
    near_grad, away_grad, negative_out = refs[2 * parts : 2 * parts + 3]
    away_other = refs[2 * parts + 3 : 2 * parts + 2 + n]
    relation_sum, (table, table_t, negative_grad) = refs[2 * parts + 2 + n : -3], refs[-3:]
    most, _, width = ids.shape
    steps = plan[2 * most]
    count = table.shape[0]
    for piece in (*away_other, *relation_sum):
        piece[...] = jnp.zeros_like(piece)
    rows = sum(piece.shape[1] for piece in away) // n

    def one_block(i, carry):
        here = plan[i]
        swapped = here >= n

        def take_table(slab):
            found = gather(slab, negative_ids[here])
            table_t[...] = found.astype(bf16)
            table[...] = found.T.astype(bf16)
            negative_grad[...] = jnp.zeros_like(negative_grad)

        fresh = (i == 0) | (plan[jnp.maximum(i - 1, 0)] != here)
        pl.when(fresh & ~swapped)(lambda: take_table(away))
        pl.when(fresh & swapped)(lambda: take_table(near))

        entries = ids[i]
        alive = (lax.broadcasted_iota(i32, (1, width), 1) < plan[most + i]).astype(f32)
        near_rows = near_in[i].astype(f32)
        away_rows = gather(away, entries[1:2])
        head = jnp.where(swapped, away_rows, near_rows)
        tail = jnp.where(swapped, near_rows, away_rows)
        operator = operator_in[i]
        query = head * operator
        query_b = query.astype(bf16)
        positive = jnp.sum(query * tail, axis=0, keepdims=True)
        scores = dot(table[...], query_b)
        pos_coef = -jax.nn.sigmoid(-positive) * alive
        neg_coef = (jax.nn.sigmoid(scores) * (alive * (1.0 / count))).astype(bf16)
        query_grad = pos_coef * tail + dot(table_t[...], neg_coef)
        negative_grad[...] += dot_nt(neg_coef, query_b)
        head_grad = query_grad * operator
        tail_grad = pos_coef * query
        near_grad[i] = split(jnp.where(swapped, tail_grad, head_grad))
        away_pair = split(jnp.where(swapped, head_grad, tail_grad))
        away_grad[i] = away_pair
        scatter_add(away_other, entries[1:2] - rows, away_pair)
        scatter_add(relation_sum, entries[3:4], split(query_grad * head))

        ends = (i == steps - 1) | (plan[jnp.minimum(i + 1, steps - 1)] != here)

        @pl.when(ends)
        def _():
            negative_out[here] = split(negative_grad[...])

        @pl.when(ends & ~swapped)
        def _():
            add_negatives(away_other, negative_ids[here] - rows, negative_out[here])

        return carry

    lax.fori_loop(0, steps, one_block, 0)


def scatter_kernel(row, first, plan, ids, negative_ids, grads, negative_grads, *sums):
    most = ids.shape[0]
    for piece in sums:
        piece[...] = jnp.zeros_like(piece)

    def one_block(i, carry):
        scatter_add(sums, ids[i][row : row + 1], grads[i])
        return carry

    lax.fori_loop(0, plan[2 * most], one_block, 0)
    for k in range(first, first + negative_ids.shape[0] // 2):

        @pl.when(plan[2 * most + 1 + k] != 0)
        def _(k=k):
            add_negatives(sums, negative_ids[k], negative_grads[k])


def entity_kernel(n, table, state, returned, *refs):
    parts, (new_table, new_state) = refs[:n], refs[n:]
    grad = returned[...]
    for part in parts:
        grad = grad + part[...]
    lanes = 128
    before = jnp.broadcast_to(state[...], (lanes, table.shape[0])).T[:, :1]
    after = before + jnp.mean(grad * grad, axis=-1, keepdims=True)
    new_table[...] = table[...] - learn_rate * grad / jnp.sqrt(after)
    new_state[...] = jnp.broadcast_to(after, (table.shape[0], lanes)).T[:1]


def relation_kernel(chunk, codes, relations, state, mine, theirs, out, grad, column):
    chunks = mine.shape[0] // chunk
    for k in range(2 * chunks):
        part = (mine, theirs)[k // chunks]
        start = (k % chunks) * chunk
        grad[pl.ds(pl.multiple_of(codes[2] ^ (k * chunk), chunk), chunk), :] = part[start : start + chunk, :]
    count = relations.shape[0]
    column[...] = jnp.ones_like(column)
    column[:, :count] = jnp.broadcast_to(state[...], (column.shape[0], count))
    g = grad[:count, :]
    total = column[...].T[:count, :1] + jnp.mean(g * g, axis=-1, keepdims=True)
    out[...] = relations[...] - learn_rate * g / jnp.sqrt(total)


def exchange(x, axis, mask):
    return lax.ppermute(x, axis, [(i, i ^ mask) for i in range(lax.axis_size(axis))])


def on_device(
    entity_table,
    entity_state,
    relations,
    relation_state,
    head_rows,
    tail_rows,
    relation_ids,
    negative_rows,
    edge_counts,
):
    n = lax.axis_size("sub")
    n_dom = lax.axis_size("dom")
    me_sub = lax.axis_index("sub")
    me_dom = lax.axis_index("dom")
    pair = n_dom // 2
    team = 2 * n
    rows, dims = entity_table.shape
    slots = head_rows.shape[2]
    count = negative_rows.shape[2]
    width = count
    most = slots // width
    rel_rows = -(-relations.shape[0] // 256) * 256
    chips = 2 * n
    chunk = rel_rows // (2 * chips)
    me = lax.shift_right_logical(me_dom, pair.bit_length() - 1) * n + me_sub
    chunk_code = (me_dom & 1) * chips + ((me_dom >> 1) & 1) * n + me_sub
    codes = jnp.stack([me, me_sub * rows, chunk_code * chunk]).astype(i32)

    in_vmem = pl.BlockSpec(memory_space=pltpu.VMEM)
    in_smem = pl.BlockSpec(memory_space=pltpu.SMEM)

    def call(kernel, name, outs, scratch, unit, scalars, arrays, held=True):
        place = (lambda x, t: pltpu.VMEM(x, t)) if held else jax.ShapeDtypeStruct
        return pl.pallas_call(
            kernel,
            in_specs=[in_smem] * len(scalars) + [in_vmem] * len(arrays),
            out_specs=[in_vmem] * len(outs),
            out_shape=[place(x, t) for x, t in outs],
            scratch_shapes=scratch,
            compiler_params=params,
            cost_estimate=pl.CostEstimate(flops=slots * dims * unit, bytes_accessed=slots * dims, transcendentals=0),
            name=name,
        )(*scalars, *(pltpu.with_memory_space_constraint(x, pltpu.VMEM) for x in arrays))

    halves = 2
    *local, ids = call(
        prep_kernel,
        "prep_kernel",
        [((dims, rows // halves), bf16)] * halves + [((most + 1, 3, width), jnp.int16)],
        [],
        1,
        (edge_counts,),
        (
            entity_table,
            head_rows.reshape(1, slots),
            tail_rows.reshape(1, slots),
            relation_ids.reshape(1, slots),
            negative_rows.reshape(1, count),
        ),
    )

    def along_sub(x):
        return [x] + [exchange(x, "sub", k) for k in range(1, n)]

    def in_order(pieces):
        return [piece[k] for k in range(n) for piece in pieces]

    all_ids = along_sub(ids) + along_sub(exchange(ids, "dom", pair))
    away_slab = in_order([along_sub(exchange(x, "dom", pair)) for x in local])
    near_slab = in_order([along_sub(x) for x in local])
    parts = n * halves

    plan, step_ids, negative_ids = pl.pallas_call(
        functools.partial(plan_kernel, n),
        in_specs=[in_smem] + [in_vmem] * team,
        out_specs=[in_smem, in_vmem, in_vmem],
        out_shape=[
            jax.ShapeDtypeStruct((2 * most + 1 + team,), i32),
            pltpu.VMEM((most, 4, width), i32),
            pltpu.VMEM((team, 1, width), i32),
        ],
        compiler_params=params,
        name="plan_kernel",
    )(codes, *(pltpu.with_memory_space_constraint(x, pltpu.VMEM) for x in all_ids))

    near_rows, operator = call(
        near_kernel,
        "near_kernel",
        [((most, dims, width), bf16), ((most, dims, width), f32)],
        [pltpu.VMEM((rel_rows, dims), f32), pltpu.VMEM((2 * dims, rel_rows), bf16)],
        n * rows + 2 * rel_rows,
        (plan,),
        (step_ids, relations, *near_slab),
    )
    sums = ((rows, dims), f32)
    pair_out = ((most, 2 * dims, width), bf16)
    near_grad, away_grad, negative_grad, *found = call(
        functools.partial(edge_kernel, n, parts),
        "edge_kernel",
        [pair_out, pair_out, ((team, 2 * count, dims), bf16)]
        + [sums] * (n - 1)
        + [((chunk, dims), f32)] * chips
        + [((chips * chunk, dims), f32)],
        [pltpu.VMEM((count, dims), bf16), pltpu.VMEM((dims, count), bf16), pltpu.VMEM((count, dims), f32)],
        (2 * n - 1) * rows + 3 * count + 2 * rel_rows,
        (plan,),
        (step_ids, negative_ids, near_rows, operator, *near_slab, *away_slab),
    )
    away_other, relation_part = found[: n - 1], found[n - 1 :]
    (away_total,) = call(
        functools.partial(scatter_kernel, 1, 0),
        "away_kernel",
        [sums],
        [],
        2 * rows,
        (plan,),
        (step_ids, negative_ids, away_grad, negative_grad),
    )
    for k in range(1, n):
        away_total = away_total + exchange(away_other[k - 1], "sub", k)

    def to_chip(x, mask):
        pairs = []
        for d in range(n_dom):
            for s in range(n):
                pairs.append((d * n + s, (d ^ (mask // n * 2)) * n + (s ^ (mask % n))))
        return lax.ppermute(x, ("dom", "sub"), pairs)

    other_core = exchange(relation_part[chips], "dom", 1)
    partial = [relation_part[k] + other_core[k * chunk : (k + 1) * chunk] for k in range(chips)]
    chunk_total = partial[0]
    for k in range(1, chips):
        chunk_total = chunk_total + to_chip(partial[k], k)
    mask = 4
    while mask < n_dom:
        chunk_total = chunk_total + exchange(chunk_total, "dom", mask)
        mask *= 2

    plan, away_total, chunk_total = lax.optimization_barrier((plan, away_total, chunk_total))
    returned = exchange(away_total, "dom", pair)
    mine = jnp.concatenate([chunk_total] + [to_chip(chunk_total, k) for k in range(1, chips)], axis=0)
    theirs = exchange(mine, "dom", 1)
    near_sum = call(
        functools.partial(scatter_kernel, 0, n),
        "own_kernel",
        [sums] * n,
        [],
        2 * n * rows,
        (plan,),
        (step_ids, negative_ids, near_grad, negative_grad),
    )
    near_sum = [near_sum[0]] + [exchange(near_sum[k], "sub", k) for k in range(1, n)]
    (new_relations,) = call(
        functools.partial(relation_kernel, chunk),
        "relation_kernel",
        [(relations.shape, f32)],
        [pltpu.VMEM((rel_rows, dims), f32), pltpu.VMEM((128, rel_rows), f32)],
        1,
        (codes,),
        (relations, relation_state.reshape(1, -1), mine, theirs),
        held=False,
    )
    new_table, new_state = call(
        functools.partial(entity_kernel, n),
        "entity_kernel",
        [((rows, dims), f32), ((1, rows), f32)],
        [],
        1,
        (),
        (entity_table, entity_state.reshape(1, rows), returned, *near_sum),
        held=False,
    )
    return (new_table, new_state.reshape(rows), new_relations)


def solution(mesh):
    in_specs = (
        P(("dom", "sub"), None),
        P(("dom", "sub")),
        P(),
        P(),
        P("dom", "sub", None),
        P("dom", "sub", None),
        P("dom", "sub", None),
        P("dom", "sub", None),
        P("dom", "sub"),
    )
    out_specs = (P(("dom", "sub"), None), P(("dom", "sub")), P())
    return jax.shard_map(
        on_device, mesh=mesh, in_specs=in_specs, out_specs=out_specs, check_vma=False
    )
```

```python
import functools

import jax
import jax.numpy as jnp
from jax import lax
from jax.experimental import pallas as pl
from jax.experimental.pallas import tpu as pltpu
from jax.sharding import PartitionSpec as P

learn_rate = 0.1
bf16 = jnp.bfloat16
f32 = jnp.float32
i32 = jnp.int32
params = pltpu.CompilerParams(vmem_limit_bytes=10 * 2**20)


def dot(a, b):
    return jnp.dot(a, b, preferred_element_type=f32)


def dot_nt(a, b):
    return lax.dot_general(a, b, (((1,), (1,)), ((), ())), preferred_element_type=f32)


def one_hot(ids, rows):
    places = lax.broadcasted_iota(jnp.int16, (rows, ids.shape[1]), 0)
    return jnp.where(places == ids.astype(jnp.int16), jnp.ones((), bf16), jnp.zeros((), bf16))


def split(x):
    high = x.astype(bf16)
    return jnp.concatenate([high, (x - high.astype(f32)).astype(bf16)], axis=0)


def gather(pieces, ids):
    rows = pieces[0].shape[1]
    hot = one_hot(ids, len(pieces) * rows)
    total = dot(pieces[0][...], hot[:rows])
    for k in range(1, len(pieces)):
        total = total + dot(pieces[k][...], hot[k * rows : (k + 1) * rows])
    return total


def scatter_add(pieces, ids, pair):
    dims = pair.shape[0] // 2
    hot = one_hot(ids, sum(piece.shape[0] for piece in pieces))
    start = 0
    for piece in pieces:
        part = hot[start : start + piece.shape[0]]
        piece[...] += dot_nt(part, pair[:dims]) + dot_nt(part, pair[dims:])
        start += piece.shape[0]


def add_negatives(pieces, ids, pair):
    count = pair.shape[0] // 2
    hot = one_hot(ids, sum(piece.shape[0] for piece in pieces))
    start = 0
    for piece in pieces:
        part = hot[start : start + piece.shape[0]]
        piece[...] += dot(part, pair[:count]) + dot(part, pair[count:])
        start += piece.shape[0]


def rows_kernel(table, out):
    out[...] = table[...].T.astype(bf16)


def ids_kernel(count, heads, tails, kinds, negatives, ids_out):
    blocks, _, width = ids_out.shape
    for j in range(blocks - 1):
        at = slice(j * width, (j + 1) * width)
        block = jnp.concatenate([heads[:, at], tails[:, at], kinds[:, at]], axis=0)
        ids_out[j] = block.astype(jnp.int16)
    last = jnp.concatenate([negatives[...], jnp.full((2, width), count[0, 0], i32)], axis=0)
    ids_out[blocks - 1] = last.astype(jnp.int16)


def plan_kernel(n, codes, *refs):
    sources, (plan, step_ids, negative_ids) = refs[:-3], refs[-3:]
    team = len(sources)
    most, _, width = step_ids.shape
    me = codes[0]
    counts, blocks = [], []
    for k, ids in enumerate(sources):
        last = ids[most].astype(i32)
        counts.append(jnp.max(last[1:2]))
        blocks.append(lax.div(counts[k] + (width - 1), i32(width)))
        negative_ids[k] = last[0:1] ^ codes[1]
    total = sum(blocks)
    low = lax.div(me * total, i32(team))
    high = lax.div((me + 1) * total, i32(team))
    plan[2 * most] = high - low
    before = []
    for k in range(team):
        ahead = [jnp.where((me ^ j) < (me ^ k), blocks[j], 0) for j in range(team) if j != k]
        before.append(sum(ahead))
        seen = (before[k] < high) & (before[k] + blocks[k] > low)
        plan[2 * most + 1 + k] = seen.astype(i32)

    def one_step(i, carry):
        line = jnp.minimum(low + i, high - 1)
        for k, ids in enumerate(sources):

            @pl.when((line >= before[k]) & (line < before[k] + blocks[k]))
            def _(k=k, ids=ids):
                nth = line - before[k]
                plan[i] = k
                plan[most + i] = jnp.clip(counts[k] - nth * width, 0, width)
                entries = ids[nth].astype(i32)
                near, away = (0, 1) if k < n else (1, 0)
                step_ids[i, 0:1] = entries[near : near + 1] ^ codes[1]
                step_ids[i, 1:2] = entries[away : away + 1] ^ codes[1]
                step_ids[i, 2:3] = entries[2:3]
                step_ids[i, 3:4] = entries[2:3] ^ codes[2]

        return carry

    lax.fori_loop(0, high - low, one_step, 0)


def near_kernel(plan, ids, relations, *refs):
    slab, (rows_out, operator_out, rel_full, rel_split) = refs[:-4], refs[-4:]
    dims = relations.shape[1]
    rel_full[...] = jnp.zeros_like(rel_full)
    rel_full[: relations.shape[0], :] = relations[...]
    rel_split[...] = split(rel_full[...].T)

    def one_block(i, carry):
        entries = ids[i]
        rows_out[i] = gather(slab, entries[0:1]).astype(bf16)
        both = dot(rel_split[...], one_hot(entries[2:3], rel_full.shape[0]))
        operator_out[i] = both[:dims] + both[dims:]
        return carry

    lax.fori_loop(0, plan[2 * ids.shape[0]], one_block, 0)


def edge_kernel(n, plan, ids, negative_ids, near_in, operator_in, *refs):
    near, away = refs[:n], refs[n : 2 * n]
    near_grad, away_grad, negative_out = refs[2 * n : 2 * n + 3]
    away_other = refs[2 * n + 3 : 3 * n + 2]
    relation_sum, (table, table_t, negative_grad) = refs[3 * n + 2 : -3], refs[-3:]
    most, _, width = ids.shape
    steps = plan[2 * most]
    count = table.shape[0]
    for piece in (*away_other, *relation_sum):
        piece[...] = jnp.zeros_like(piece)
    rows = away[0].shape[1]

    def one_block(i, carry):
        here = plan[i]
        swapped = here >= n

        def take_table(slab):
            found = gather(slab, negative_ids[here])
            table_t[...] = found.astype(bf16)
            table[...] = found.T.astype(bf16)
            negative_grad[...] = jnp.zeros_like(negative_grad)

        fresh = (i == 0) | (plan[jnp.maximum(i - 1, 0)] != here)
        pl.when(fresh & ~swapped)(lambda: take_table(away))
        pl.when(fresh & swapped)(lambda: take_table(near))

        entries = ids[i]
        alive = (lax.broadcasted_iota(i32, (1, width), 1) < plan[most + i]).astype(f32)
        near_rows = near_in[i].astype(f32)
        away_rows = gather(away, entries[1:2])
        head = jnp.where(swapped, away_rows, near_rows)
        tail = jnp.where(swapped, near_rows, away_rows)
        operator = operator_in[i]
        query = head * operator
        query_b = query.astype(bf16)
        positive = jnp.sum(query * tail, axis=0, keepdims=True)
        scores = dot(table[...], query_b)
        pos_coef = -jax.nn.sigmoid(-positive) * alive
        neg_coef = (jax.nn.sigmoid(scores) * (alive * (1.0 / count))).astype(bf16)
        query_grad = pos_coef * tail + dot(table_t[...], neg_coef)
        negative_grad[...] += dot_nt(neg_coef, query_b)
        head_grad = query_grad * operator
        tail_grad = pos_coef * query
        near_grad[i] = split(jnp.where(swapped, tail_grad, head_grad))
        away_pair = split(jnp.where(swapped, head_grad, tail_grad))
        away_grad[i] = away_pair
        scatter_add(away_other, entries[1:2] - rows, away_pair)
        scatter_add(relation_sum, entries[3:4], split(query_grad * head))

        ends = (i == steps - 1) | (plan[jnp.minimum(i + 1, steps - 1)] != here)

        @pl.when(ends)
        def _():
            negative_out[here] = split(negative_grad[...])

        @pl.when(ends & ~swapped)
        def _():
            add_negatives(away_other, negative_ids[here] - rows, negative_out[here])

        return carry

    lax.fori_loop(0, steps, one_block, 0)


def scatter_kernel(row, start, first, plan, ids, negative_ids, grads, negative_grads, *sums):
    most = ids.shape[0]
    for piece in sums:
        piece[...] = jnp.zeros_like(piece)

    def one_block(i, carry):
        scatter_add(sums, ids[i][row : row + 1] - start, grads[i])
        return carry

    lax.fori_loop(0, plan[2 * most], one_block, 0)
    for k in range(first, first + negative_ids.shape[0] // 2):

        @pl.when(plan[2 * most + 1 + k] != 0)
        def _(k=k):
            add_negatives(sums, negative_ids[k] - start, negative_grads[k])


def entity_kernel(n, table, state, returned, *refs):
    parts, (new_table, new_state) = refs[:n], refs[n:]
    grad = returned[...]
    for part in parts:
        grad = grad + part[...]
    lanes = 128
    before = jnp.broadcast_to(state[...], (lanes, table.shape[0])).T[:, :1]
    after = before + jnp.mean(grad * grad, axis=-1, keepdims=True)
    new_table[...] = table[...] - learn_rate * grad / jnp.sqrt(after)
    new_state[...] = jnp.broadcast_to(after, (table.shape[0], lanes)).T[:1]


def relation_kernel(chunk, codes, relations, state, mine, theirs, out, grad, column):
    chunks = mine.shape[0] // chunk
    for k in range(2 * chunks):
        part = (mine, theirs)[k // chunks]
        start = (k % chunks) * chunk
        grad[pl.ds(pl.multiple_of(codes[2] ^ (k * chunk), chunk), chunk), :] = part[start : start + chunk, :]
    count = relations.shape[0]
    column[...] = jnp.ones_like(column)
    column[:, :count] = jnp.broadcast_to(state[...], (column.shape[0], count))
    g = grad[:count, :]
    total = column[...].T[:count, :1] + jnp.mean(g * g, axis=-1, keepdims=True)
    out[...] = relations[...] - learn_rate * g / jnp.sqrt(total)


def exchange(x, axis, mask):
    return lax.ppermute(x, axis, [(i, i ^ mask) for i in range(lax.axis_size(axis))])


def on_device(
    entity_table,
    entity_state,
    relations,
    relation_state,
    head_rows,
    tail_rows,
    relation_ids,
    negative_rows,
    edge_counts,
):
    n = lax.axis_size("sub")
    n_dom = lax.axis_size("dom")
    me_sub = lax.axis_index("sub")
    me_dom = lax.axis_index("dom")
    pair = n_dom // 2
    team = 2 * n
    rows, dims = entity_table.shape
    slots = head_rows.shape[2]
    count = negative_rows.shape[2]
    width = count
    most = slots // width
    rel_rows = -(-relations.shape[0] // 256) * 256
    chips = 2 * n
    chunk = rel_rows // (2 * chips)
    me = lax.shift_right_logical(me_dom, pair.bit_length() - 1) * n + me_sub
    chunk_code = (me_dom & 1) * chips + ((me_dom >> 1) & 1) * n + me_sub
    codes = jnp.stack([me, me_sub * rows, chunk_code * chunk]).astype(i32)

    in_vmem = pl.BlockSpec(memory_space=pltpu.VMEM)
    in_smem = pl.BlockSpec(memory_space=pltpu.SMEM)

    def call(kernel, name, outs, scratch, unit, scalars, arrays, held=True, fetch=False):
        place = (lambda x, t: pltpu.VMEM(x, t)) if held else jax.ShapeDtypeStruct
        return pl.pallas_call(
            kernel,
            in_specs=[in_smem] * len(scalars) + [in_vmem] * len(arrays),
            out_specs=[in_vmem] * len(outs),
            out_shape=[place(x, t) for x, t in outs],
            scratch_shapes=scratch,
            compiler_params=params,
            cost_estimate=pl.CostEstimate(flops=slots * dims * unit, bytes_accessed=slots * dims, transcendentals=0),
            name=name,
        )(*scalars, *(pltpu.with_memory_space_constraint(x, pltpu.HBM if fetch else pltpu.VMEM) for x in arrays))

    (ids,) = call(
        ids_kernel,
        "ids_kernel",
        [((most + 1, 3, width), jnp.int16)],
        [],
        1,
        (edge_counts,),
        (
            head_rows.reshape(1, slots),
            tail_rows.reshape(1, slots),
            relation_ids.reshape(1, slots),
            negative_rows.reshape(1, count),
        ),
        fetch=True,
    )
    ids, table = lax.optimization_barrier((ids, entity_table))
    (local,) = call(rows_kernel, "rows_kernel", [((dims, rows), bf16)], [], 1, (), (table,), fetch=True)

    def to_peer(x, across, aside):
        pairs = [(d * n + s, (d ^ across) * n + (s ^ aside)) for d in range(n_dom) for s in range(n)]
        return lax.ppermute(x, ("dom", "sub"), pairs)

    def along_sub(x):
        return [x] + [exchange(x, "sub", k) for k in range(1, n)]

    all_ids = along_sub(ids) + along_sub(exchange(ids, "dom", pair))
    near_slab = along_sub(local)
    away_first = exchange(local, "dom", pair)

    plan, step_ids, negative_ids = pl.pallas_call(
        functools.partial(plan_kernel, n),
        in_specs=[in_smem] + [in_vmem] * team,
        out_specs=[in_smem, in_vmem, in_vmem],
        out_shape=[
            jax.ShapeDtypeStruct((2 * most + 1 + team,), i32),
            pltpu.VMEM((most, 4, width), i32),
            pltpu.VMEM((team, 1, width), i32),
        ],
        compiler_params=params,
        cost_estimate=pl.CostEstimate(flops=32 * slots * dims * rows, bytes_accessed=slots * dims, transcendentals=0),
        name="plan_kernel",
    )(codes, *(pltpu.with_memory_space_constraint(x, pltpu.VMEM) for x in all_ids))

    near_plan, away_first = lax.optimization_barrier((plan, away_first))
    away_slab = along_sub(away_first)
    near_rows, operator = call(
        near_kernel,
        "near_kernel",
        [((most, dims, width), bf16), ((most, dims, width), f32)],
        [pltpu.VMEM((rel_rows, dims), f32), pltpu.VMEM((2 * dims, rel_rows), bf16)],
        n * rows + 2 * rel_rows,
        (near_plan,),
        (step_ids, relations, *near_slab),
    )
    sums = ((rows, dims), f32)
    pair_out = ((most, 2 * dims, width), bf16)
    near_grad, away_grad, negative_grad, *found = call(
        functools.partial(edge_kernel, n),
        "edge_kernel",
        [pair_out, pair_out, ((team, 2 * count, dims), bf16)]
        + [sums] * (n - 1)
        + [((chunk, dims), f32)] * chips
        + [((chips * chunk, dims), f32)],
        [pltpu.VMEM((count, dims), bf16), pltpu.VMEM((dims, count), bf16), pltpu.VMEM((count, dims), f32)],
        (2 * n - 1) * rows + 3 * count + 2 * rel_rows,
        (plan,),
        (step_ids, negative_ids, near_rows, operator, *near_slab, *away_slab),
    )
    away_other, relation_part = found[: n - 1], found[n - 1 :]

    def scatter(name, row, start, parts, first, plan, grads):
        return call(
            functools.partial(scatter_kernel, row, start, first),
            name,
            [sums] * parts,
            [],
            2 * parts * rows,
            (plan,),
            (step_ids, negative_ids, grads, negative_grad),
        )

    def to_chip(x, k):
        return to_peer(x, k // n * 2, k % n)

    other_core = exchange(relation_part[chips], "dom", 1)
    partial = [relation_part[k] + other_core[k * chunk : (k + 1) * chunk] for k in range(chips)]
    *partial, plan = lax.optimization_barrier((*partial, plan))
    chunk_total = partial[0]
    for k in range(1, chips):
        chunk_total = chunk_total + to_chip(partial[k], k)
    (away_total,) = scatter("away_kernel", 1, 0, 1, 0, plan, away_grad)
    chunk_total, away_total, plan, *away_other = lax.optimization_barrier((chunk_total, away_total, plan, *away_other))
    away_received = [exchange(away_other[k - 1], "sub", k) for k in range(1, n)]
    mask = 4
    while mask < n_dom:
        chunk_total = chunk_total + exchange(chunk_total, "dom", mask)
        mask *= 2
    near_other = scatter("own_other_kernel", 0, rows, n - 1, n, plan, near_grad)
    for x in away_received:
        away_total = away_total + x
    plan, away_total, chunk_total, *near_other = lax.optimization_barrier((plan, away_total, chunk_total, *near_other))
    returned = exchange(away_total, "dom", pair)
    mine = jnp.concatenate([chunk_total] + [to_chip(chunk_total, k) for k in range(1, chips)], axis=0)
    theirs = exchange(mine, "dom", 1)
    near_sum = [exchange(near_other[k - 1], "sub", k) for k in range(1, n)]
    near_sum += scatter("own_kernel", 0, 0, 1, n, plan, near_grad)
    (new_relations,) = call(
        functools.partial(relation_kernel, chunk),
        "relation_kernel",
        [(relations.shape, f32)],
        [pltpu.VMEM((rel_rows, dims), f32), pltpu.VMEM((128, rel_rows), f32)],
        1,
        (codes,),
        (relations, relation_state.reshape(1, -1), mine, theirs),
        held=False,
    )
    new_table, new_state = call(
        functools.partial(entity_kernel, n),
        "entity_kernel",
        [((rows, dims), f32), ((1, rows), f32)],
        [],
        1,
        (),
        (entity_table, entity_state.reshape(1, rows), returned, *near_sum),
        held=False,
    )
    return (new_table, new_state.reshape(rows), new_relations)


def solution(mesh):
    in_specs = (
        P(("dom", "sub"), None),
        P(("dom", "sub")),
        P(),
        P(),
        P("dom", "sub", None),
        P("dom", "sub", None),
        P("dom", "sub", None),
        P("dom", "sub", None),
        P("dom", "sub"),
    )
    out_specs = (P(("dom", "sub"), None), P(("dom", "sub")), P())
    return jax.shard_map(
        on_device, mesh=mesh, in_specs=in_specs, out_specs=out_specs, check_vma=False
    )
```

```python
import functools

import jax
import jax.numpy as jnp
from jax import lax
from jax.experimental import pallas as pl
from jax.experimental.pallas import tpu as pltpu
from jax.sharding import PartitionSpec as P

learn_rate = 0.1
bf16 = jnp.bfloat16
f32 = jnp.float32
i32 = jnp.int32
params = pltpu.CompilerParams(vmem_limit_bytes=10 * 2**20)


def dot(a, b):
    return jnp.dot(a, b, preferred_element_type=f32)


def dot_nt(a, b):
    return lax.dot_general(a, b, (((1,), (1,)), ((), ())), preferred_element_type=f32)


def one_hot(ids, rows):
    places = lax.broadcasted_iota(jnp.int16, (rows, ids.shape[1]), 0)
    return jnp.where(places == ids.astype(jnp.int16), jnp.ones((), bf16), jnp.zeros((), bf16))


def split(x):
    high = x.astype(bf16)
    return jnp.concatenate([high, (x - high.astype(f32)).astype(bf16)], axis=0)


def gather(pieces, ids):
    rows = pieces[0].shape[1]
    hot = one_hot(ids, len(pieces) * rows)
    total = dot(pieces[0][...], hot[:rows])
    for k in range(1, len(pieces)):
        total = total + dot(pieces[k][...], hot[k * rows : (k + 1) * rows])
    return total


def scatter_add(pieces, ids, pair):
    dims = pair.shape[0] // 2
    hot = one_hot(ids, sum(piece.shape[0] for piece in pieces))
    start = 0
    for piece in pieces:
        part = hot[start : start + piece.shape[0]]
        piece[...] += dot_nt(part, pair[:dims]) + dot_nt(part, pair[dims:])
        start += piece.shape[0]


def add_negatives(pieces, ids, pair):
    count = pair.shape[0] // 2
    hot = one_hot(ids, sum(piece.shape[0] for piece in pieces))
    start = 0
    for piece in pieces:
        part = hot[start : start + piece.shape[0]]
        piece[...] += dot(part, pair[:count]) + dot(part, pair[count:])
        start += piece.shape[0]


def rows_kernel(table, out):
    out[...] = table[...].T.astype(bf16)


def ids_kernel(count, heads, tails, kinds, negatives, ids_out):
    blocks, _, width = ids_out.shape
    for j in range(blocks - 1):
        at = slice(j * width, (j + 1) * width)
        block = jnp.concatenate([heads[:, at], tails[:, at], kinds[:, at]], axis=0)
        ids_out[j] = block.astype(jnp.int16)
    last = jnp.concatenate([negatives[...], jnp.full((2, width), count[0, 0], i32)], axis=0)
    ids_out[blocks - 1] = last.astype(jnp.int16)


def plan_kernel(n, codes, *refs):
    sources, (plan, step_ids, negative_ids) = refs[:-3], refs[-3:]
    team = len(sources)
    most, _, width = step_ids.shape
    me = codes[0]
    counts, blocks = [], []
    for k, ids in enumerate(sources):
        last = ids[most].astype(i32)
        counts.append(jnp.max(last[1:2]))
        blocks.append(lax.div(counts[k] + (width - 1), i32(width)))
        negative_ids[k] = last[0:1] ^ codes[1]
    total = sum(blocks)
    low = lax.div(me * total, i32(team))
    high = lax.div((me + 1) * total, i32(team))
    plan[2 * most] = high - low
    before = []
    for k in range(team):
        ahead = [jnp.where((me ^ j) < (me ^ k), blocks[j], 0) for j in range(team) if j != k]
        before.append(sum(ahead))
        seen = (before[k] < high) & (before[k] + blocks[k] > low)
        plan[2 * most + 1 + k] = seen.astype(i32)

    def one_step(i, carry):
        line = jnp.minimum(low + i, high - 1)
        for k, ids in enumerate(sources):

            @pl.when((line >= before[k]) & (line < before[k] + blocks[k]))
            def _(k=k, ids=ids):
                nth = line - before[k]
                plan[i] = k
                plan[most + i] = jnp.clip(counts[k] - nth * width, 0, width)
                entries = ids[nth].astype(i32)
                near, away = (0, 1) if k < n else (1, 0)
                step_ids[i, 0:1] = entries[near : near + 1] ^ codes[1]
                step_ids[i, 1:2] = entries[away : away + 1] ^ codes[1]
                step_ids[i, 2:3] = entries[2:3]
                step_ids[i, 3:4] = entries[2:3] ^ codes[2]

        return carry

    lax.fori_loop(0, high - low, one_step, 0)


def near_kernel(plan, ids, relations, *refs):
    slab, (rows_out, operator_out, rel_full, rel_split) = refs[:-4], refs[-4:]
    dims = relations.shape[1]
    rel_full[...] = jnp.zeros_like(rel_full)
    rel_full[: relations.shape[0], :] = relations[...]
    rel_split[...] = split(rel_full[...].T)

    def one_block(i, carry):
        entries = ids[i]
        rows_out[i] = gather(slab, entries[0:1]).astype(bf16)
        both = dot(rel_split[...], one_hot(entries[2:3], rel_full.shape[0]))
        operator_out[i] = both[:dims] + both[dims:]
        return carry

    lax.fori_loop(0, plan[2 * ids.shape[0]], one_block, 0)


def edge_kernel(n, plan, ids, negative_ids, near_in, operator_in, *refs):
    near, away = refs[:n], refs[n : 2 * n]
    near_grad, away_grad, negative_out = refs[2 * n : 2 * n + 3]
    away_out, away_other = refs[2 * n + 3 : 3 * n + 2], refs[1 - n :]
    relation_sum, (table, table_t, negative_grad) = refs[3 * n + 2 : -2 - n], refs[-2 - n : 1 - n]
    most, _, width = ids.shape
    steps = plan[2 * most]
    count = table.shape[0]
    for piece in (*away_other, *relation_sum):
        piece[...] = jnp.zeros_like(piece)
    rows = away[0].shape[1]

    def one_block(i, carry):
        here = plan[i]
        swapped = here >= n

        def take_table(slab):
            found = gather(slab, negative_ids[here])
            table_t[...] = found.astype(bf16)
            table[...] = found.T.astype(bf16)
            negative_grad[...] = jnp.zeros_like(negative_grad)

        fresh = (i == 0) | (plan[jnp.maximum(i - 1, 0)] != here)
        pl.when(fresh & ~swapped)(lambda: take_table(away))
        pl.when(fresh & swapped)(lambda: take_table(near))

        entries = ids[i]
        alive = (lax.broadcasted_iota(i32, (1, width), 1) < plan[most + i]).astype(f32)
        near_rows = near_in[i].astype(f32)
        away_rows = gather(away, entries[1:2])
        head = jnp.where(swapped, away_rows, near_rows)
        tail = jnp.where(swapped, near_rows, away_rows)
        operator = operator_in[i]
        query = head * operator
        query_b = query.astype(bf16)
        positive = jnp.sum(query * tail, axis=0, keepdims=True)
        scores = dot(table[...], query_b)
        pos_coef = -jax.nn.sigmoid(-positive) * alive
        neg_coef = (jax.nn.sigmoid(scores) * (alive * (1.0 / count))).astype(bf16)
        query_grad = pos_coef * tail + dot(table_t[...], neg_coef)
        negative_grad[...] += dot_nt(neg_coef, query_b)
        head_grad = query_grad * operator
        tail_grad = pos_coef * query
        near_grad[i] = split(jnp.where(swapped, tail_grad, head_grad))
        away_pair = split(jnp.where(swapped, head_grad, tail_grad))
        away_grad[i] = away_pair
        scatter_add(away_other, entries[1:2] - rows, away_pair)
        scatter_add(relation_sum, entries[3:4], split(query_grad * head))

        ends = (i == steps - 1) | (plan[jnp.minimum(i + 1, steps - 1)] != here)

        @pl.when(ends)
        def _():
            negative_out[here] = split(negative_grad[...])

        @pl.when(ends & ~swapped)
        def _():
            add_negatives(away_other, negative_ids[here] - rows, negative_out[here])

        return carry

    lax.fori_loop(0, steps, one_block, 0)
    for total, out in zip(away_other, away_out, strict=True):
        out[...] = total[...].astype(bf16)


def scatter_kernel(row, start, first, plan, ids, negative_ids, grads, negative_grads, *sums):
    most = ids.shape[0]
    for piece in sums:
        piece[...] = jnp.zeros_like(piece)

    def one_block(i, carry):
        scatter_add(sums, ids[i][row : row + 1] - start, grads[i])
        return carry

    lax.fori_loop(0, plan[2 * most], one_block, 0)
    for k in range(first, first + negative_ids.shape[0] // 2):

        @pl.when(plan[2 * most + 1 + k] != 0)
        def _(k=k):
            add_negatives(sums, negative_ids[k] - start, negative_grads[k])


def entity_kernel(n, table, state, returned, *refs):
    parts, (new_table, new_state) = refs[:n], refs[n:]
    grad = returned[...].astype(f32)
    for part in parts:
        grad = grad + part[...]
    lanes = 128
    before = jnp.broadcast_to(state[...], (lanes, table.shape[0])).T[:, :1]
    after = before + jnp.mean(grad * grad, axis=-1, keepdims=True)
    new_table[...] = table[...] - learn_rate * grad / jnp.sqrt(after)
    new_state[...] = jnp.broadcast_to(after, (table.shape[0], lanes)).T[:1]


def relation_kernel(chunk, codes, relations, state, mine, theirs, out, grad, column):
    chunks = mine.shape[0] // chunk
    for k in range(2 * chunks):
        part = (mine, theirs)[k // chunks]
        start = (k % chunks) * chunk
        grad[pl.ds(pl.multiple_of(codes[2] ^ (k * chunk), chunk), chunk), :] = part[start : start + chunk, :]
    count = relations.shape[0]
    column[...] = jnp.ones_like(column)
    column[:, :count] = jnp.broadcast_to(state[...], (column.shape[0], count))
    g = grad[:count, :]
    total = column[...].T[:count, :1] + jnp.mean(g * g, axis=-1, keepdims=True)
    out[...] = relations[...] - learn_rate * g / jnp.sqrt(total)


def exchange(x, axis, mask):
    return lax.ppermute(x, axis, [(i, i ^ mask) for i in range(lax.axis_size(axis))])


def on_device(
    entity_table,
    entity_state,
    relations,
    relation_state,
    head_rows,
    tail_rows,
    relation_ids,
    negative_rows,
    edge_counts,
):
    n = lax.axis_size("sub")
    n_dom = lax.axis_size("dom")
    me_sub = lax.axis_index("sub")
    me_dom = lax.axis_index("dom")
    pair = n_dom // 2
    team = 2 * n
    rows, dims = entity_table.shape
    slots = head_rows.shape[2]
    count = negative_rows.shape[2]
    width = count
    most = slots // width
    rel_rows = -(-relations.shape[0] // 256) * 256
    chips = 2 * n
    chunk = rel_rows // (2 * chips)
    me = lax.shift_right_logical(me_dom, pair.bit_length() - 1) * n + me_sub
    chunk_code = (me_dom & 1) * chips + ((me_dom >> 1) & 1) * n + me_sub
    codes = jnp.stack([me, me_sub * rows, chunk_code * chunk]).astype(i32)

    in_vmem = pl.BlockSpec(memory_space=pltpu.VMEM)
    in_smem = pl.BlockSpec(memory_space=pltpu.SMEM)

    def call(kernel, name, outs, scratch, unit, scalars, arrays, held=True, fetch=False):
        place = (lambda x, t: pltpu.VMEM(x, t)) if held else jax.ShapeDtypeStruct
        return pl.pallas_call(
            kernel,
            in_specs=[in_smem] * len(scalars) + [in_vmem] * len(arrays),
            out_specs=[in_vmem] * len(outs),
            out_shape=[place(x, t) for x, t in outs],
            scratch_shapes=scratch,
            compiler_params=params,
            cost_estimate=pl.CostEstimate(flops=slots * dims * unit, bytes_accessed=slots * dims, transcendentals=0),
            name=name,
        )(*scalars, *(pltpu.with_memory_space_constraint(x, pltpu.HBM if fetch else pltpu.VMEM) for x in arrays))

    (ids,) = call(
        ids_kernel,
        "ids_kernel",
        [((most + 1, 3, width), jnp.int16)],
        [],
        1,
        (edge_counts,),
        (
            head_rows.reshape(1, slots),
            tail_rows.reshape(1, slots),
            relation_ids.reshape(1, slots),
            negative_rows.reshape(1, count),
        ),
        fetch=True,
    )
    ids, table = lax.optimization_barrier((ids, entity_table))
    (local,) = call(rows_kernel, "rows_kernel", [((dims, rows), bf16)], [], 1, (), (table,), fetch=True)

    def to_peer(x, across, aside):
        pairs = [(d * n + s, (d ^ across) * n + (s ^ aside)) for d in range(n_dom) for s in range(n)]
        return lax.ppermute(x, ("dom", "sub"), pairs)

    def along_sub(x):
        return [x] + [exchange(x, "sub", k) for k in range(1, n)]

    all_ids = along_sub(ids) + along_sub(exchange(ids, "dom", pair))
    near_slab = along_sub(local)
    away_first = exchange(local, "dom", pair)

    plan, step_ids, negative_ids = pl.pallas_call(
        functools.partial(plan_kernel, n),
        in_specs=[in_smem] + [in_vmem] * team,
        out_specs=[in_smem, in_vmem, in_vmem],
        out_shape=[
            jax.ShapeDtypeStruct((2 * most + 1 + team,), i32),
            pltpu.VMEM((most, 4, width), i32),
            pltpu.VMEM((team, 1, width), i32),
        ],
        compiler_params=params,
        cost_estimate=pl.CostEstimate(flops=32 * slots * dims * rows, bytes_accessed=slots * dims, transcendentals=0),
        name="plan_kernel",
    )(codes, *(pltpu.with_memory_space_constraint(x, pltpu.VMEM) for x in all_ids))

    near_plan, away_first = lax.optimization_barrier((plan, away_first))
    away_slab = along_sub(away_first)
    near_rows, operator = call(
        near_kernel,
        "near_kernel",
        [((most, dims, width), bf16), ((most, dims, width), f32)],
        [pltpu.VMEM((rel_rows, dims), f32), pltpu.VMEM((2 * dims, rel_rows), bf16)],
        n * rows + 2 * rel_rows,
        (near_plan,),
        (step_ids, relations, *near_slab),
    )
    sums = ((rows, dims), f32)
    pair_out = ((most, 2 * dims, width), bf16)
    near_grad, away_grad, negative_grad, *found = call(
        functools.partial(edge_kernel, n),
        "edge_kernel",
        [pair_out, pair_out, ((team, 2 * count, dims), bf16)]
        + [((rows, dims), bf16)] * (n - 1)
        + [((chunk, dims), f32)] * chips
        + [((chips * chunk, dims), f32)],
        [pltpu.VMEM((count, dims), bf16), pltpu.VMEM((dims, count), bf16), pltpu.VMEM((count, dims), f32)]
        + [pltpu.VMEM((rows, dims), f32)] * (n - 1),
        (2 * n - 1) * rows + 3 * count + 2 * rel_rows,
        (plan,),
        (step_ids, negative_ids, near_rows, operator, *near_slab, *away_slab),
    )
    away_other, relation_part = found[: n - 1], found[n - 1 :]

    def scatter(name, row, start, parts, first, plan, grads):
        return call(
            functools.partial(scatter_kernel, row, start, first),
            name,
            [sums] * parts,
            [],
            2 * parts * rows,
            (plan,),
            (step_ids, negative_ids, grads, negative_grad),
        )

    def to_chip(x, k):
        return to_peer(x, k // n * 2, k % n)

    other_core = exchange(relation_part[chips], "dom", 1)
    partial = [relation_part[k] + other_core[k * chunk : (k + 1) * chunk] for k in range(chips)]
    *partial, plan = lax.optimization_barrier((*partial, plan))
    chunk_total = partial[0]
    for k in range(1, chips):
        chunk_total = chunk_total + to_chip(partial[k], k)
    away_received = [exchange(away_other[k - 1], "sub", k) for k in range(1, n)]
    (away_total,) = scatter("away_kernel", 1, 0, 1, 0, plan, away_grad)
    chunk_total, away_total, plan = lax.optimization_barrier((chunk_total, away_total, plan))
    mask = 4
    while mask < n_dom:
        chunk_total = chunk_total + exchange(chunk_total, "dom", mask)
        mask *= 2
    near_other = scatter("own_other_kernel", 0, rows, n - 1, n, plan, near_grad)
    for x in away_received:
        away_total = away_total + x.astype(f32)
    away_total = away_total.astype(bf16)
    plan, away_total, chunk_total, *near_other = lax.optimization_barrier((plan, away_total, chunk_total, *near_other))
    returned = exchange(away_total, "dom", pair)
    mine = jnp.concatenate([chunk_total] + [to_chip(chunk_total, k) for k in range(1, chips)], axis=0)
    theirs = exchange(mine, "dom", 1)
    near_sum = [exchange(near_other[k - 1], "sub", k) for k in range(1, n)]
    near_sum += scatter("own_kernel", 0, 0, 1, n, plan, near_grad)
    (new_relations,) = call(
        functools.partial(relation_kernel, chunk),
        "relation_kernel",
        [(relations.shape, f32)],
        [pltpu.VMEM((rel_rows, dims), f32), pltpu.VMEM((128, rel_rows), f32)],
        1,
        (codes,),
        (relations, relation_state.reshape(1, -1), mine, theirs),
        held=False,
    )
    new_table, new_state = call(
        functools.partial(entity_kernel, n),
        "entity_kernel",
        [((rows, dims), f32), ((1, rows), f32)],
        [],
        1,
        (),
        (entity_table, entity_state.reshape(1, rows), returned, *near_sum),
        held=False,
    )
    return (new_table, new_state.reshape(rows), new_relations)


def solution(mesh):
    in_specs = (
        P(("dom", "sub"), None),
        P(("dom", "sub")),
        P(),
        P(),
        P("dom", "sub", None),
        P("dom", "sub", None),
        P("dom", "sub", None),
        P("dom", "sub", None),
        P("dom", "sub"),
    )
    out_specs = (P(("dom", "sub"), None), P(("dom", "sub")), P())
    return jax.shard_map(
        on_device, mesh=mesh, in_specs=in_specs, out_specs=out_specs, check_vma=False
    )
```

```python
import functools
import math

import jax
import jax.numpy as jnp
from jax import lax
from jax.experimental import pallas as pl
from jax.experimental.pallas import tpu as pltpu
from jax.sharding import PartitionSpec as P

learn_rate = 0.1
bf16 = jnp.bfloat16
f32 = jnp.float32
i32 = jnp.int32
params = pltpu.CompilerParams(vmem_limit_bytes=10 * 2**20)


def dot(a, b):
    return jnp.dot(a, b, preferred_element_type=f32)


def dot_nt(a, b):
    return lax.dot_general(a, b, (((1,), (1,)), ((), ())), preferred_element_type=f32)


def one_hot(ids, rows):
    places = lax.broadcasted_iota(jnp.int16, (rows, ids.shape[1]), 0)
    return jnp.where(places == ids.astype(jnp.int16), jnp.ones((), bf16), jnp.zeros((), bf16))


def split(x):
    high = x.astype(bf16)
    return jnp.concatenate([high, (x - high.astype(f32)).astype(bf16)], axis=0)


def gather(pieces, ids):
    rows = pieces[0].shape[1]
    hot = one_hot(ids, len(pieces) * rows)
    total = dot(pieces[0][...], hot[:rows])
    for k in range(1, len(pieces)):
        total = total + dot(pieces[k][...], hot[k * rows : (k + 1) * rows])
    return total


def scatter_add(pieces, ids, pair):
    dims = pair.shape[0] // 2
    hot = one_hot(ids, sum(piece.shape[0] for piece in pieces))
    start = 0
    for piece in pieces:
        part = hot[start : start + piece.shape[0]]
        piece[...] += dot_nt(part, pair[:dims]) + dot_nt(part, pair[dims:])
        start += piece.shape[0]


def add_negatives(pieces, ids, pair):
    count = pair.shape[0] // 2
    hot = one_hot(ids, sum(piece.shape[0] for piece in pieces))
    start = 0
    for piece in pieces:
        part = hot[start : start + piece.shape[0]]
        piece[...] += dot(part, pair[:count]) + dot(part, pair[count:])
        start += piece.shape[0]


def rows_kernel(table, out):
    out[...] = table[...].T.astype(bf16)


def ids_kernel(count, heads, tails, kinds, negatives, ids_out):
    blocks, _, width = ids_out.shape
    for j in range(blocks - 1):
        at = slice(j * width, (j + 1) * width)
        block = jnp.concatenate([heads[:, at], tails[:, at], kinds[:, at]], axis=0)
        ids_out[j] = block.astype(jnp.int16)
    last = jnp.concatenate([negatives[...], jnp.full((2, width), count[0, 0], i32)], axis=0)
    ids_out[blocks - 1] = last.astype(jnp.int16)


def plan_kernel(n, codes, *refs):
    sources, (plan, step_ids, negative_ids) = refs[:-3], refs[-3:]
    team = len(sources)
    most, _, width = step_ids.shape
    me = codes[0]
    counts, blocks = [], []
    for k, ids in enumerate(sources):
        last = ids[most].astype(i32)
        counts.append(jnp.max(last[1:2]))
        blocks.append(lax.div(counts[k] + (width - 1), i32(width)))
        negative_ids[k] = last[0:1] ^ codes[1]
    total = sum(blocks)
    low = lax.div(me * total, i32(team))
    high = lax.div((me + 1) * total, i32(team))
    plan[2 * most] = high - low
    before = []
    for k in range(team):
        ahead = [jnp.where((me ^ j) < (me ^ k), blocks[j], 0) for j in range(team) if j != k]
        before.append(sum(ahead))
        seen = (before[k] < high) & (before[k] + blocks[k] > low)
        plan[2 * most + 1 + k] = seen.astype(i32)

    def one_step(i, carry):
        line = jnp.minimum(low + i, high - 1)
        for k, ids in enumerate(sources):

            @pl.when((line >= before[k]) & (line < before[k] + blocks[k]))
            def _(k=k, ids=ids):
                nth = line - before[k]
                plan[i] = k
                plan[most + i] = jnp.clip(counts[k] - nth * width, 0, width)
                entries = ids[nth].astype(i32)
                near, away = (0, 1) if k < n else (1, 0)
                step_ids[i, 0:1] = entries[near : near + 1] ^ codes[1]
                step_ids[i, 1:2] = entries[away : away + 1] ^ codes[1]
                step_ids[i, 2:3] = entries[2:3]
                step_ids[i, 3:4] = entries[2:3] ^ codes[2]

        return carry

    lax.fori_loop(0, high - low, one_step, 0)


def near_kernel(plan, ids, relations, *refs):
    slab, (rows_out, operator_out, rel_full, rel_split) = refs[:-4], refs[-4:]
    dims = relations.shape[1]
    rel_full[...] = jnp.zeros_like(rel_full)
    rel_full[: relations.shape[0], :] = relations[...]
    rel_split[...] = split(rel_full[...].T)

    def one_block(i, carry):
        entries = ids[i]
        rows_out[i] = gather(slab, entries[0:1]).astype(bf16)
        both = dot(rel_split[...], one_hot(entries[2:3], rel_full.shape[0]))
        operator_out[i] = both[:dims] + both[dims:]
        return carry

    lax.fori_loop(0, plan[2 * ids.shape[0]], one_block, 0)


def edge_kernel(n, plan, ids, negative_ids, near_in, operator_in, *refs):
    near, away = refs[:n], refs[n : 2 * n]
    near_grad, away_grad, negative_out = refs[2 * n : 2 * n + 3]
    away_other = refs[2 * n + 3 : 3 * n + 2]
    relation_sum, (table, table_t, negative_grad) = refs[3 * n + 2 : -3], refs[-3:]
    most, _, width = ids.shape
    steps = plan[2 * most]
    count = table.shape[0]
    for piece in (*away_other, *relation_sum):
        piece[...] = jnp.zeros_like(piece)
    rows = away[0].shape[1]

    def one_block(i, carry):
        here = plan[i]
        swapped = here >= n

        def take_table(slab):
            found = gather(slab, negative_ids[here])
            table_t[...] = found.astype(bf16)
            table[...] = found.T.astype(bf16)
            negative_grad[...] = jnp.zeros_like(negative_grad)

        fresh = (i == 0) | (plan[jnp.maximum(i - 1, 0)] != here)
        pl.when(fresh & ~swapped)(lambda: take_table(away))
        pl.when(fresh & swapped)(lambda: take_table(near))

        entries = ids[i]
        alive = (lax.broadcasted_iota(i32, (1, width), 1) < plan[most + i]).astype(f32)
        near_rows = near_in[i].astype(f32)
        away_rows = gather(away, entries[1:2])
        head = jnp.where(swapped, away_rows, near_rows)
        tail = jnp.where(swapped, near_rows, away_rows)
        operator = operator_in[i]
        query = head * operator
        query_b = query.astype(bf16)
        positive = jnp.sum(query * tail, axis=0, keepdims=True)
        scores = dot(table[...], query_b)
        pos_coef = -jax.nn.sigmoid(-positive) * alive
        neg_coef = (jax.nn.sigmoid(scores) * (alive * (1.0 / count))).astype(bf16)
        query_grad = pos_coef * tail + dot(table_t[...], neg_coef)
        negative_grad[...] += dot_nt(neg_coef, query_b)
        head_grad = query_grad * operator
        tail_grad = pos_coef * query
        near_grad[i] = split(jnp.where(swapped, tail_grad, head_grad))
        away_pair = split(jnp.where(swapped, head_grad, tail_grad))
        away_grad[i] = away_pair
        scatter_add(away_other, entries[1:2] - rows, away_pair)
        scatter_add(relation_sum, entries[3:4], split(query_grad * head))

        ends = (i == steps - 1) | (plan[jnp.minimum(i + 1, steps - 1)] != here)

        @pl.when(ends)
        def _():
            negative_out[here] = split(negative_grad[...])

        @pl.when(ends & ~swapped)
        def _():
            add_negatives(away_other, negative_ids[here] - rows, negative_out[here])

        return carry

    lax.fori_loop(0, steps, one_block, 0)


def scatter_kernel(row, start, first, plan, ids, negative_ids, grads, negative_grads, *sums):
    most = ids.shape[0]
    for piece in sums:
        piece[...] = jnp.zeros_like(piece)

    def one_block(i, carry):
        scatter_add(sums, ids[i][row : row + 1] - start, grads[i])
        return carry

    lax.fori_loop(0, plan[2 * most], one_block, 0)
    for k in range(first, first + negative_ids.shape[0] // 2):

        @pl.when(plan[2 * most + 1 + k] != 0)
        def _(k=k):
            add_negatives(sums, negative_ids[k] - start, negative_grads[k])


def entity_kernel(table, state, returned, own, new_table, new_state):
    grad = returned[...] + own[...]
    lanes = 128
    before = jnp.broadcast_to(state[...], (lanes, table.shape[0])).T[:, :1]
    after = before + jnp.mean(grad * grad, axis=-1, keepdims=True)
    new_table[...] = table[...] - learn_rate * grad / jnp.sqrt(after)
    new_state[...] = jnp.broadcast_to(after, (table.shape[0], lanes)).T[:1]


def relation_kernel(chunk, codes, relations, state, mine, theirs, out, grad, column):
    chunks = mine.shape[0] // chunk
    for k in range(2 * chunks):
        part = (mine, theirs)[k // chunks]
        start = (k % chunks) * chunk
        grad[pl.ds(pl.multiple_of(codes[2] ^ (k * chunk), chunk), chunk), :] = part[start : start + chunk, :]
    count = relations.shape[0]
    column[...] = jnp.ones_like(column)
    column[:, :count] = jnp.broadcast_to(state[...], (column.shape[0], count))
    g = grad[:count, :]
    total = column[...].T[:count, :1] + jnp.mean(g * g, axis=-1, keepdims=True)
    out[...] = relations[...] - learn_rate * g / jnp.sqrt(total)


def exchange(x, axis, mask):
    return lax.ppermute(x, axis, [(i, i ^ mask) for i in range(lax.axis_size(axis))])


def on_device(
    entity_table,
    entity_state,
    relations,
    relation_state,
    head_rows,
    tail_rows,
    relation_ids,
    negative_rows,
    edge_counts,
):
    n = lax.axis_size("sub")
    n_dom = lax.axis_size("dom")
    me_sub = lax.axis_index("sub")
    me_dom = lax.axis_index("dom")
    pair = n_dom // 2
    team = 2 * n
    rows, dims = entity_table.shape
    slots = head_rows.shape[2]
    count = negative_rows.shape[2]
    width = count
    most = slots // width
    rel_rows = -(-relations.shape[0] // 256) * 256
    chips = 2 * n
    chunk = rel_rows // (2 * chips)
    me = lax.shift_right_logical(me_dom, pair.bit_length() - 1) * n + me_sub
    chunk_code = (me_dom & 1) * chips + ((me_dom >> 1) & 1) * n + me_sub
    codes = jnp.stack([me, me_sub * rows, chunk_code * chunk]).astype(i32)

    in_vmem = pl.BlockSpec(memory_space=pltpu.VMEM)
    in_smem = pl.BlockSpec(memory_space=pltpu.SMEM)

    def call(kernel, name, outs, scratch, unit, scalars, arrays, held=True, fetch=False):
        place = (lambda x, t: pltpu.VMEM(x, t)) if held else jax.ShapeDtypeStruct
        return pl.pallas_call(
            kernel,
            in_specs=[in_smem] * len(scalars) + [in_vmem] * len(arrays),
            out_specs=[in_vmem] * len(outs),
            out_shape=[place(x, t) for x, t in outs],
            scratch_shapes=scratch,
            compiler_params=params,
            cost_estimate=pl.CostEstimate(flops=int(slots * dims * unit), bytes_accessed=rows * dims, transcendentals=0),
            name=name,
        )(*scalars, *(pltpu.with_memory_space_constraint(x, pltpu.HBM if fetch else pltpu.VMEM) for x in arrays))

    (ids,) = call(
        ids_kernel,
        "ids_kernel",
        [((most + 1, 3, width), jnp.int16)],
        [],
        1,
        (edge_counts,),
        (
            head_rows.reshape(1, slots),
            tail_rows.reshape(1, slots),
            relation_ids.reshape(1, slots),
            negative_rows.reshape(1, count),
        ),
        fetch=True,
    )
    ids, table = lax.optimization_barrier((ids, entity_table))
    (local,) = call(rows_kernel, "rows_kernel", [((dims, rows), bf16)], [], 1, (), (table,), fetch=True)

    def to_peer(x, across, aside):
        pairs = [(d * n + s, (d ^ across) * n + (s ^ aside)) for d in range(n_dom) for s in range(n)]
        return lax.ppermute(x, ("dom", "sub"), pairs)

    def along_sub(x):
        return [x] + [exchange(x, "sub", k) for k in range(1, n)]

    all_ids = along_sub(ids) + along_sub(exchange(ids, "dom", pair))
    near_slab = along_sub(local)
    away_first = exchange(local, "dom", pair)

    plan, step_ids, negative_ids = pl.pallas_call(
        functools.partial(plan_kernel, n),
        in_specs=[in_smem] + [in_vmem] * team,
        out_specs=[in_smem, in_vmem, in_vmem],
        out_shape=[
            jax.ShapeDtypeStruct((2 * most + 1 + team,), i32),
            pltpu.VMEM((most, 4, width), i32),
            pltpu.VMEM((team, 1, width), i32),
        ],
        compiler_params=params,
        cost_estimate=pl.CostEstimate(flops=32 * slots * dims * rows, bytes_accessed=slots * dims, transcendentals=0),
        name="plan_kernel",
    )(codes, *(pltpu.with_memory_space_constraint(x, pltpu.VMEM) for x in all_ids))

    near_plan, away_first = lax.optimization_barrier((plan, away_first))
    away_slab = along_sub(away_first)
    near_rows, operator = call(
        near_kernel,
        "near_kernel",
        [((most, dims, width), bf16), ((most, dims, width), f32)],
        [pltpu.VMEM((rel_rows, dims), f32), pltpu.VMEM((2 * dims, rel_rows), bf16)],
        n * rows + 2 * rel_rows,
        (near_plan,),
        (step_ids, relations, *near_slab),
    )
    sums = ((rows, dims), f32)
    pair_out = ((most, 2 * dims, width), bf16)
    near_grad, away_grad, negative_grad, *found = call(
        functools.partial(edge_kernel, n),
        "edge_kernel",
        [pair_out, pair_out, ((team, 2 * count, dims), bf16)]
        + [sums] * (n - 1)
        + [((chunk, dims), f32)] * chips
        + [((chips * chunk, dims), f32)],
        [pltpu.VMEM((count, dims), bf16), pltpu.VMEM((dims, count), bf16), pltpu.VMEM((count, dims), f32)],
        (2 * n - 1) * rows + 3 * count + 2 * rel_rows,
        (plan,),
        (step_ids, negative_ids, near_rows, operator, *near_slab, *away_slab),
    )
    away_other, relation_part = found[: n - 1], found[n - 1 :]

    def scatter(name, row, start, parts, first, plan, grads):
        return call(
            functools.partial(scatter_kernel, row, start, first),
            name,
            [sums] * parts,
            [],
            0,
            (plan,),
            (step_ids, negative_ids, grads, negative_grad),
        )

    scale = 2.0 ** -(math.ceil(math.log2(team * slots * 24 / 65504.0)) + 1)

    def narrow(x):
        return (x * scale).astype(jnp.float16)

    def widen(x):
        return x.astype(f32) * (1.0 / scale)

    def to_chip(x, k):
        return to_peer(x, k // n * 2, k % n)

    other_core = exchange(relation_part[chips], "dom", 1)
    partial = [relation_part[k] + other_core[k * chunk : (k + 1) * chunk] for k in range(chips)]
    away_other = [narrow(x) for x in away_other]
    partial, plan, away_other = lax.optimization_barrier((partial, plan, away_other))
    chunk_total = partial[0]
    for k in range(1, chips):
        chunk_total = chunk_total + to_chip(partial[k], k)
    away_received = [widen(exchange(away_other[k - 1], "sub", k)) for k in range(1, n)]
    (away_total,) = scatter("away_kernel", 1, 0, 1, 0, plan, away_grad)
    chunk_total, away_total, plan = lax.optimization_barrier((chunk_total, away_total, plan))
    mask = 4
    while mask < n_dom:
        chunk_total = chunk_total + exchange(chunk_total, "dom", mask)
        mask *= 2
    near_other = scatter("own_other_kernel", 0, rows, n - 1, n, plan, near_grad)
    near_other = [narrow(x) for x in near_other]
    for x in away_received:
        away_total = away_total + x
    away_total = narrow(away_total)
    plan, away_total, chunk_total, *near_other = lax.optimization_barrier((plan, away_total, chunk_total, *near_other))
    returned = exchange(away_total, "dom", pair)
    mine = jnp.concatenate([chunk_total] + [to_chip(chunk_total, k) for k in range(1, chips)], axis=0)
    near_received = [widen(exchange(near_other[k - 1], "sub", k)) for k in range(1, n)]
    (near_sum,) = scatter("own_kernel", 0, 0, 1, n, plan, near_grad)
    returned, mine, near_sum = lax.optimization_barrier((returned, mine, near_sum))
    theirs = exchange(mine, "dom", 1)
    (new_relations,) = call(
        functools.partial(relation_kernel, chunk),
        "relation_kernel",
        [(relations.shape, f32)],
        [pltpu.VMEM((rel_rows, dims), f32), pltpu.VMEM((128, rel_rows), f32)],
        0,
        (codes,),
        (relations, relation_state.reshape(1, -1), mine, theirs),
        held=False,
    )
    returned = widen(returned)
    for x in near_received:
        returned = returned + x
    new_table, new_state = call(
        entity_kernel,
        "entity_kernel",
        [((rows, dims), f32), ((1, rows), f32)],
        [],
        1,
        (),
        (entity_table, entity_state.reshape(1, rows), returned, near_sum),
        held=False,
    )
    return (new_table, new_state.reshape(rows), new_relations)


def solution(mesh):
    in_specs = (
        P(("dom", "sub"), None),
        P(("dom", "sub")),
        P(),
        P(),
        P("dom", "sub", None),
        P("dom", "sub", None),
        P("dom", "sub", None),
        P("dom", "sub", None),
        P("dom", "sub"),
    )
    out_specs = (P(("dom", "sub"), None), P(("dom", "sub")), P())
    return jax.shard_map(
        on_device, mesh=mesh, in_specs=in_specs, out_specs=out_specs, check_vma=False
    )
```

```python
import functools
import math

import jax
import jax.numpy as jnp
from jax import lax
from jax.experimental import pallas as pl
from jax.experimental.pallas import tpu as pltpu
from jax.sharding import PartitionSpec as P

learn_rate = 0.1
bf16 = jnp.bfloat16
f32 = jnp.float32
i32 = jnp.int32
params = pltpu.CompilerParams(vmem_limit_bytes=10 * 2**20)


def dot(a, b):
    return jnp.dot(a, b, preferred_element_type=f32)


def dot_nt(a, b):
    return lax.dot_general(a, b, (((1,), (1,)), ((), ())), preferred_element_type=f32)


def one_hot(ids, rows):
    places = lax.broadcasted_iota(jnp.int16, (rows, ids.shape[1]), 0)
    return jnp.where(places == ids.astype(jnp.int16), jnp.ones((), bf16), jnp.zeros((), bf16))


def split(x):
    high = x.astype(bf16)
    return jnp.concatenate([high, (x - high.astype(f32)).astype(bf16)], axis=0)


def gather(pieces, ids):
    rows = pieces[0].shape[1]
    hot = one_hot(ids, len(pieces) * rows)
    total = dot(pieces[0][...], hot[:rows])
    for k in range(1, len(pieces)):
        total = total + dot(pieces[k][...], hot[k * rows : (k + 1) * rows])
    return total


def scatter_add(pieces, ids, pair):
    dims = pair.shape[0] // 2
    hot = one_hot(ids, sum(piece.shape[0] for piece in pieces))
    start = 0
    for piece in pieces:
        part = hot[start : start + piece.shape[0]]
        piece[...] += dot_nt(part, pair[:dims]) + dot_nt(part, pair[dims:])
        start += piece.shape[0]


def add_negatives(pieces, ids, pair):
    count = pair.shape[0] // 2
    hot = one_hot(ids, sum(piece.shape[0] for piece in pieces))
    start = 0
    for piece in pieces:
        part = hot[start : start + piece.shape[0]]
        piece[...] += dot(part, pair[:count]) + dot(part, pair[count:])
        start += piece.shape[0]


def rows_kernel(table, out):
    out[...] = table[...].T.astype(bf16)


def ids_kernel(count, heads, tails, kinds, negatives, ids_out):
    blocks, _, width = ids_out.shape
    for j in range(blocks - 1):
        at = slice(j * width, (j + 1) * width)
        block = jnp.concatenate([heads[:, at], tails[:, at], kinds[:, at]], axis=0)
        ids_out[j] = block.astype(jnp.int16)
    last = jnp.concatenate([negatives[...], jnp.full((2, width), count[0, 0], i32)], axis=0)
    ids_out[blocks - 1] = last.astype(jnp.int16)


def plan_kernel(n, codes, *refs):
    sources, (plan, step_ids, negative_ids) = refs[:-3], refs[-3:]
    team = len(sources)
    most, _, width = step_ids.shape
    me = codes[0]
    counts, blocks = [], []
    for k, ids in enumerate(sources):
        last = ids[most].astype(i32)
        counts.append(jnp.max(last[1:2]))
        blocks.append(lax.div(counts[k] + (width - 1), i32(width)))
        negative_ids[k] = last[0:1] ^ codes[1]
    total = sum(blocks)
    low = lax.div(me * total, i32(team))
    high = lax.div((me + 1) * total, i32(team))
    plan[2 * most] = high - low
    before = []
    for k in range(team):
        ahead = [jnp.where((me ^ j) < (me ^ k), blocks[j], 0) for j in range(team) if j != k]
        before.append(sum(ahead))
        seen = (before[k] < high) & (before[k] + blocks[k] > low)
        plan[2 * most + 1 + k] = seen.astype(i32)

    def one_step(i, carry):
        line = jnp.minimum(low + i, high - 1)
        for k, ids in enumerate(sources):

            @pl.when((line >= before[k]) & (line < before[k] + blocks[k]))
            def _(k=k, ids=ids):
                nth = line - before[k]
                plan[i] = k
                plan[most + i] = jnp.clip(counts[k] - nth * width, 0, width)
                entries = ids[nth].astype(i32)
                near, away = (0, 1) if k < n else (1, 0)
                step_ids[i, 0:1] = entries[near : near + 1] ^ codes[1]
                step_ids[i, 1:2] = entries[away : away + 1] ^ codes[1]
                step_ids[i, 2:3] = entries[2:3]
                step_ids[i, 3:4] = entries[2:3] ^ codes[2]

        return carry

    lax.fori_loop(0, high - low, one_step, 0)


def near_kernel(plan, ids, relations, *refs):
    slab, (rows_out, operator_out, rel_full, rel_split) = refs[:-4], refs[-4:]
    dims = relations.shape[1]
    rel_full[...] = jnp.zeros_like(rel_full)
    rel_full[: relations.shape[0], :] = relations[...]
    rel_split[...] = split(rel_full[...].T)

    def one_block(i, carry):
        entries = ids[i]
        rows_out[i] = gather(slab, entries[0:1]).astype(bf16)
        both = dot(rel_split[...], one_hot(entries[2:3], rel_full.shape[0]))
        operator_out[i] = both[:dims] + both[dims:]
        return carry

    lax.fori_loop(0, plan[2 * ids.shape[0]], one_block, 0)


def edge_kernel(n, plan, ids, negative_ids, near_in, operator_in, *refs):
    near, away = refs[:n], refs[n : 2 * n]
    near_grad, away_grad, negative_out = refs[2 * n : 2 * n + 3]
    away_other = refs[2 * n + 3 : 3 * n + 2]
    relation_out, (table, table_t, negative_grad, relation_sum) = refs[3 * n + 2 : -4], refs[-4:]
    most, _, width = ids.shape
    steps = plan[2 * most]
    count = table.shape[0]
    for piece in (*away_other, relation_sum):
        piece[...] = jnp.zeros_like(piece)
    rows = away[0].shape[1]

    def one_block(i, carry):
        here = plan[i]
        swapped = here >= n

        def take_table(slab):
            found = gather(slab, negative_ids[here])
            table_t[...] = found.astype(bf16)
            table[...] = found.T.astype(bf16)
            negative_grad[...] = jnp.zeros_like(negative_grad)

        fresh = (i == 0) | (plan[jnp.maximum(i - 1, 0)] != here)
        pl.when(fresh & ~swapped)(lambda: take_table(away))
        pl.when(fresh & swapped)(lambda: take_table(near))

        entries = ids[i]

        def score(swapped):
            alive = (lax.broadcasted_iota(i32, (1, width), 1) < plan[most + i]).astype(f32)
            near_rows = near_in[i].astype(f32)
            away_rows = gather(away, entries[1:2])
            head, tail = (away_rows, near_rows) if swapped else (near_rows, away_rows)
            operator = operator_in[i]
            query = head * operator
            query_b = query.astype(bf16)
            positive = jnp.sum(query * tail, axis=0, keepdims=True)
            scores = dot(table[...], query_b)
            pos_coef = -jax.nn.sigmoid(-positive) * alive
            neg_coef = (jax.nn.sigmoid(scores) * (alive * (1.0 / count))).astype(bf16)
            query_grad = pos_coef * tail + dot(table_t[...], neg_coef)
            negative_grad[...] += dot_nt(neg_coef, query_b)
            head_pair, tail_pair = split(query_grad * operator), split(pos_coef * query)
            near_pair, away_pair = (tail_pair, head_pair) if swapped else (head_pair, tail_pair)
            near_grad[i] = near_pair
            away_grad[i] = away_pair
            scatter_add(away_other, entries[1:2] - rows, away_pair)
            scatter_add([relation_sum], entries[3:4], split(query_grad * head))

        pl.when(~swapped)(lambda: score(False))
        pl.when(swapped)(lambda: score(True))

        ends = (i == steps - 1) | (plan[jnp.minimum(i + 1, steps - 1)] != here)

        @pl.when(ends)
        def _():
            negative_out[here] = split(negative_grad[...])

        @pl.when(ends & ~swapped)
        def _():
            add_negatives(away_other, negative_ids[here] - rows, negative_out[here])

        return carry

    lax.fori_loop(0, steps, one_block, 0)
    start = 0
    for piece in relation_out:
        piece[...] = relation_sum[start : start + piece.shape[0], :]
        start += piece.shape[0]


def scatter_kernel(row, start, first, plan, ids, negative_ids, grads, negative_grads, *sums):
    most = ids.shape[0]
    for piece in sums:
        piece[...] = jnp.zeros_like(piece)

    def one_block(i, carry):
        scatter_add(sums, ids[i][row : row + 1] - start, grads[i])
        return carry

    lax.fori_loop(0, plan[2 * most], one_block, 0)
    for k in range(first, first + negative_ids.shape[0] // 2):

        @pl.when(plan[2 * most + 1 + k] != 0)
        def _(k=k):
            add_negatives(sums, negative_ids[k] - start, negative_grads[k])


def entity_kernel(table, state, returned, own, new_table, new_state):
    grad = returned[...] + own[...]
    lanes = 128
    before = jnp.broadcast_to(state[...], (lanes, table.shape[0])).T[:, :1]
    after = before + jnp.mean(grad * grad, axis=-1, keepdims=True)
    new_table[...] = table[...] - learn_rate * grad / jnp.sqrt(after)
    new_state[...] = jnp.broadcast_to(after, (table.shape[0], lanes)).T[:1]


def relation_kernel(chunk, codes, relations, state, mine, theirs, out, grad, column):
    chunks = mine.shape[0] // chunk
    for k in range(2 * chunks):
        part = (mine, theirs)[k // chunks]
        start = (k % chunks) * chunk
        grad[pl.ds(pl.multiple_of(codes[2] ^ (k * chunk), chunk), chunk), :] = part[start : start + chunk, :]
    count = relations.shape[0]
    column[...] = jnp.ones_like(column)
    column[:, :count] = jnp.broadcast_to(state[...], (column.shape[0], count))
    g = grad[:count, :]
    total = column[...].T[:count, :1] + jnp.mean(g * g, axis=-1, keepdims=True)
    out[...] = relations[...] - learn_rate * g / jnp.sqrt(total)


def exchange(x, axis, mask):
    return lax.ppermute(x, axis, [(i, i ^ mask) for i in range(lax.axis_size(axis))])


def on_device(
    entity_table,
    entity_state,
    relations,
    relation_state,
    head_rows,
    tail_rows,
    relation_ids,
    negative_rows,
    edge_counts,
):
    n = lax.axis_size("sub")
    n_dom = lax.axis_size("dom")
    me_sub = lax.axis_index("sub")
    me_dom = lax.axis_index("dom")
    pair = n_dom // 2
    team = 2 * n
    rows, dims = entity_table.shape
    slots = head_rows.shape[2]
    count = negative_rows.shape[2]
    width = count
    most = slots // width
    rel_rows = -(-relations.shape[0] // 256) * 256
    chips = 2 * n
    chunk = rel_rows // (2 * chips)
    me = lax.shift_right_logical(me_dom, pair.bit_length() - 1) * n + me_sub
    chunk_code = (me_dom & 1) * chips + ((me_dom >> 1) & 1) * n + me_sub
    codes = jnp.stack([me, me_sub * rows, chunk_code * chunk]).astype(i32)

    in_vmem = pl.BlockSpec(memory_space=pltpu.VMEM)
    in_smem = pl.BlockSpec(memory_space=pltpu.SMEM)

    def call(kernel, name, outs, scratch, unit, scalars, arrays, held=True, fetch=False):
        place = (lambda x, t: pltpu.VMEM(x, t)) if held else jax.ShapeDtypeStruct
        return pl.pallas_call(
            kernel,
            in_specs=[in_smem] * len(scalars) + [in_vmem] * len(arrays),
            out_specs=[in_vmem] * len(outs),
            out_shape=[place(x, t) for x, t in outs],
            scratch_shapes=scratch,
            compiler_params=params,
            cost_estimate=pl.CostEstimate(flops=int(slots * dims * unit), bytes_accessed=rows * dims, transcendentals=0),
            name=name,
        )(*scalars, *(pltpu.with_memory_space_constraint(x, pltpu.HBM if fetch else pltpu.VMEM) for x in arrays))

    (ids,) = call(
        ids_kernel,
        "ids_kernel",
        [((most + 1, 3, width), jnp.int16)],
        [],
        1,
        (edge_counts,),
        (
            head_rows.reshape(1, slots),
            tail_rows.reshape(1, slots),
            relation_ids.reshape(1, slots),
            negative_rows.reshape(1, count),
        ),
        fetch=True,
    )
    ids, table = lax.optimization_barrier((ids, entity_table))
    (local,) = call(rows_kernel, "rows_kernel", [((dims, rows), bf16)], [], 1, (), (table,), fetch=True)

    def to_peer(x, across, aside):
        pairs = [(d * n + s, (d ^ across) * n + (s ^ aside)) for d in range(n_dom) for s in range(n)]
        return lax.ppermute(x, ("dom", "sub"), pairs)

    def along_sub(x):
        return [x] + [exchange(x, "sub", k) for k in range(1, n)]

    all_ids = along_sub(ids) + along_sub(exchange(ids, "dom", pair))
    near_slab = along_sub(local)
    away_first = exchange(local, "dom", pair)

    plan, step_ids, negative_ids = pl.pallas_call(
        functools.partial(plan_kernel, n),
        in_specs=[in_smem] + [in_vmem] * team,
        out_specs=[in_smem, in_vmem, in_vmem],
        out_shape=[
            jax.ShapeDtypeStruct((2 * most + 1 + team,), i32),
            pltpu.VMEM((most, 4, width), i32),
            pltpu.VMEM((team, 1, width), i32),
        ],
        compiler_params=params,
        cost_estimate=pl.CostEstimate(flops=32 * slots * dims * rows, bytes_accessed=slots * dims, transcendentals=0),
        name="plan_kernel",
    )(codes, *(pltpu.with_memory_space_constraint(x, pltpu.VMEM) for x in all_ids))

    near_plan, away_first = lax.optimization_barrier((plan, away_first))
    away_slab = along_sub(away_first)
    near_rows, operator = call(
        near_kernel,
        "near_kernel",
        [((most, dims, width), bf16), ((most, dims, width), f32)],
        [pltpu.VMEM((rel_rows, dims), f32), pltpu.VMEM((2 * dims, rel_rows), bf16)],
        n * rows + 2 * rel_rows,
        (near_plan,),
        (step_ids, relations, *near_slab),
    )
    sums = ((rows, dims), f32)
    pair_out = ((most, 2 * dims, width), bf16)
    near_grad, away_grad, negative_grad, *found = call(
        functools.partial(edge_kernel, n),
        "edge_kernel",
        [pair_out, pair_out, ((team, 2 * count, dims), bf16)]
        + [sums] * (n - 1)
        + [((chunk, dims), f32)] * chips
        + [((chips * chunk, dims), f32)],
        [pltpu.VMEM((count, dims), bf16), pltpu.VMEM((dims, count), bf16), pltpu.VMEM((count, dims), f32), pltpu.VMEM((rel_rows, dims), f32)],
        (2 * n - 1) * rows + 3 * count + 2 * rel_rows,
        (plan,),
        (step_ids, negative_ids, near_rows, operator, *near_slab, *away_slab),
    )
    away_other, relation_part = found[: n - 1], found[n - 1 :]

    def scatter(name, row, start, parts, first, plan, grads):
        return call(
            functools.partial(scatter_kernel, row, start, first),
            name,
            [sums] * parts,
            [],
            0,
            (plan,),
            (step_ids, negative_ids, grads, negative_grad),
        )

    scale = 2.0 ** -(math.ceil(math.log2(team * slots * 24 / 65504.0)) + 1)

    def narrow(x):
        return (x * scale).astype(jnp.float16)

    def widen(x):
        return x.astype(f32) * (1.0 / scale)

    def to_chip(x, k):
        return to_peer(x, k // n * 2, k % n)

    other_core = exchange(relation_part[chips], "dom", 1)
    partial = [relation_part[k] + other_core[k * chunk : (k + 1) * chunk] for k in range(chips)]
    away_other = [narrow(x) for x in away_other]
    partial, plan, away_other = lax.optimization_barrier((partial, plan, away_other))
    chunk_total = partial[0]
    for k in range(1, chips):
        chunk_total = chunk_total + to_chip(partial[k], k)
    away_received = [widen(exchange(away_other[k - 1], "sub", k)) for k in range(1, n)]
    (away_total,) = scatter("away_kernel", 1, 0, 1, 0, plan, away_grad)
    chunk_total, away_total, plan = lax.optimization_barrier((chunk_total, away_total, plan))
    mask = 4
    while mask < n_dom:
        chunk_total = chunk_total + exchange(chunk_total, "dom", mask)
        mask *= 2
    for x in away_received:
        away_total = away_total + x
    away_total = narrow(away_total)
    plan, away_total, chunk_total = lax.optimization_barrier((plan, away_total, chunk_total))
    returned = exchange(away_total, "dom", pair)
    mine = jnp.concatenate([chunk_total] + [to_chip(chunk_total, k) for k in range(1, chips)], axis=0)
    near_other = scatter("own_other_kernel", 0, rows, n - 1, n, plan, near_grad)
    near_other = [narrow(x) for x in near_other]
    plan, near_other, mine = lax.optimization_barrier((plan, near_other, mine))
    near_received = [widen(exchange(near_other[k - 1], "sub", k)) for k in range(1, n)]
    (near_sum,) = scatter("own_kernel", 0, 0, 1, n, plan, near_grad)
    returned, mine, near_sum = lax.optimization_barrier((returned, mine, near_sum))
    theirs = exchange(mine, "dom", 1)
    (new_relations,) = call(
        functools.partial(relation_kernel, chunk),
        "relation_kernel",
        [(relations.shape, f32)],
        [pltpu.VMEM((rel_rows, dims), f32), pltpu.VMEM((128, rel_rows), f32)],
        0,
        (codes,),
        (relations, relation_state.reshape(1, -1), mine, theirs),
        held=False,
    )
    returned = widen(returned)
    for x in near_received:
        returned = returned + x
    new_table, new_state = call(
        entity_kernel,
        "entity_kernel",
        [((rows, dims), f32), ((1, rows), f32)],
        [],
        1,
        (),
        (entity_table, entity_state.reshape(1, rows), returned, near_sum),
        held=False,
    )
    return (new_table, new_state.reshape(rows), new_relations)


def solution(mesh):
    in_specs = (
        P(("dom", "sub"), None),
        P(("dom", "sub")),
        P(),
        P(),
        P("dom", "sub", None),
        P("dom", "sub", None),
        P("dom", "sub", None),
        P("dom", "sub", None),
        P("dom", "sub"),
    )
    out_specs = (P(("dom", "sub"), None), P(("dom", "sub")), P())
    return jax.shard_map(
        on_device, mesh=mesh, in_specs=in_specs, out_specs=out_specs, check_vma=False
    )
```

```python
import functools
import math

import jax
import jax.numpy as jnp
from jax import lax
from jax.experimental import pallas as pl
from jax.experimental.pallas import tpu as pltpu
from jax.sharding import PartitionSpec as P

learn_rate = 0.1
bf16 = jnp.bfloat16
f32 = jnp.float32
i32 = jnp.int32
params = pltpu.CompilerParams(vmem_limit_bytes=10 * 2**20)


def dot(a, b):
    return jnp.dot(a, b, preferred_element_type=f32)


def dot_nt(a, b):
    return lax.dot_general(a, b, (((1,), (1,)), ((), ())), preferred_element_type=f32)


def one_hot(ids, rows):
    places = lax.broadcasted_iota(jnp.int16, (rows, ids.shape[1]), 0)
    return jnp.where(places == ids.astype(jnp.int16), jnp.ones((), bf16), jnp.zeros((), bf16))


def split(x):
    high = x.astype(bf16)
    return jnp.concatenate([high, (x - high.astype(f32)).astype(bf16)], axis=0)


def gather(pieces, ids):
    rows = pieces[0].shape[1]
    hot = one_hot(ids, len(pieces) * rows)
    total = dot(pieces[0][...], hot[:rows])
    for k in range(1, len(pieces)):
        total = total + dot(pieces[k][...], hot[k * rows : (k + 1) * rows])
    return total


def scatter_add(pieces, ids, pair):
    dims = pair.shape[0] // 2
    hot = one_hot(ids, sum(piece.shape[0] for piece in pieces))
    start = 0
    for piece in pieces:
        part = hot[start : start + piece.shape[0]]
        piece[...] += dot_nt(part, pair[:dims]) + dot_nt(part, pair[dims:])
        start += piece.shape[0]


def add_negatives(pieces, ids, pair):
    count = pair.shape[0] // 2
    hot = one_hot(ids, sum(piece.shape[0] for piece in pieces))
    start = 0
    for piece in pieces:
        part = hot[start : start + piece.shape[0]]
        piece[...] += dot(part, pair[:count]) + dot(part, pair[count:])
        start += piece.shape[0]


def prep_kernel(count, table, heads, tails, kinds, negatives, rows_out, ids_out):
    rows_out[...] = table[...].T.astype(bf16)
    blocks, _, width = ids_out.shape
    for j in range(blocks - 1):
        at = slice(j * width, (j + 1) * width)
        block = jnp.concatenate([heads[:, at], tails[:, at], kinds[:, at]], axis=0)
        ids_out[j] = block.astype(jnp.int16)
    last = jnp.concatenate([negatives[...], jnp.full((2, width), count[0, 0], i32)], axis=0)
    ids_out[blocks - 1] = last.astype(jnp.int16)


def plan_kernel(n, codes, *refs):
    sources, (plan, step_ids, negative_ids) = refs[:-3], refs[-3:]
    team = len(sources)
    most, _, width = step_ids.shape
    me = codes[0]
    counts, blocks = [], []
    for k, ids in enumerate(sources):
        last = ids[most].astype(i32)
        counts.append(jnp.max(last[1:2]))
        blocks.append(lax.div(counts[k] + (width - 1), i32(width)))
        negative_ids[k] = last[0:1] ^ codes[1]
    total = sum(blocks)
    low = lax.div(me * total, i32(team))
    high = lax.div((me + 1) * total, i32(team))
    plan[2 * most] = high - low
    before = []
    for k in range(team):
        ahead = [jnp.where((me ^ j) < (me ^ k), blocks[j], 0) for j in range(team) if j != k]
        before.append(sum(ahead))
        seen = (before[k] < high) & (before[k] + blocks[k] > low)
        plan[2 * most + 1 + k] = seen.astype(i32)

    def one_step(i, carry):
        line = jnp.minimum(low + i, high - 1)
        for k, ids in enumerate(sources):

            @pl.when((line >= before[k]) & (line < before[k] + blocks[k]))
            def _(k=k, ids=ids):
                nth = line - before[k]
                plan[i] = k
                plan[most + i] = jnp.clip(counts[k] - nth * width, 0, width)
                entries = ids[nth].astype(i32)
                near, away = (0, 1) if k < n else (1, 0)
                step_ids[i, 0:1] = entries[near : near + 1] ^ codes[1]
                step_ids[i, 1:2] = entries[away : away + 1] ^ codes[1]
                step_ids[i, 2:3] = entries[2:3]
                step_ids[i, 3:4] = entries[2:3] ^ codes[2]

        return carry

    lax.fori_loop(0, high - low, one_step, 0)


def near_kernel(plan, ids, relations, *refs):
    slab, (rows_out, operator_out, rel_full, rel_split) = refs[:-4], refs[-4:]
    dims = relations.shape[1]
    rel_full[...] = jnp.zeros_like(rel_full)
    rel_full[: relations.shape[0], :] = relations[...]
    rel_split[...] = split(rel_full[...].T)

    def one_block(i, carry):
        entries = ids[i]
        rows_out[i] = gather(slab, entries[0:1]).astype(bf16)
        both = dot(rel_split[...], one_hot(entries[2:3], rel_full.shape[0]))
        operator_out[i] = both[:dims] + both[dims:]
        return carry

    lax.fori_loop(0, plan[2 * ids.shape[0]], one_block, 0)


def edge_kernel(n, plan, ids, negative_ids, near_in, operator_in, *refs):
    near, away = refs[:n], refs[n : 2 * n]
    near_grad, away_grad, negative_out = refs[2 * n : 2 * n + 3]
    away_other = refs[2 * n + 3 : 3 * n + 2]
    relation_out, (table, table_t, negative_grad, relation_sum) = refs[3 * n + 2 : -4], refs[-4:]
    most, _, width = ids.shape
    steps = plan[2 * most]
    count = table.shape[0]
    for piece in (*away_other, relation_sum):
        piece[...] = jnp.zeros_like(piece)
    rows = away[0].shape[1]

    def one_block(i, carry):
        here = plan[i]
        swapped = here >= n

        def take_table(slab):
            found = gather(slab, negative_ids[here])
            table_t[...] = found.astype(bf16)
            table[...] = found.T.astype(bf16)
            negative_grad[...] = jnp.zeros_like(negative_grad)

        fresh = (i == 0) | (plan[jnp.maximum(i - 1, 0)] != here)
        pl.when(fresh & ~swapped)(lambda: take_table(away))
        pl.when(fresh & swapped)(lambda: take_table(near))

        entries = ids[i]

        def score(swapped):
            alive = (lax.broadcasted_iota(i32, (1, width), 1) < plan[most + i]).astype(f32)
            near_rows = near_in[i].astype(f32)
            away_rows = gather(away, entries[1:2])
            head, tail = (away_rows, near_rows) if swapped else (near_rows, away_rows)
            operator = operator_in[i]
            query = head * operator
            query_b = query.astype(bf16)
            positive = jnp.sum(query * tail, axis=0, keepdims=True)
            scores = dot(table[...], query_b)
            pos_coef = -jax.nn.sigmoid(-positive) * alive
            neg_coef = (jax.nn.sigmoid(scores) * (alive * (1.0 / count))).astype(bf16)
            query_grad = pos_coef * tail + dot(table_t[...], neg_coef)
            negative_grad[...] += dot_nt(neg_coef, query_b)
            head_pair, tail_pair = split(query_grad * operator), split(pos_coef * query)
            near_pair, away_pair = (tail_pair, head_pair) if swapped else (head_pair, tail_pair)
            near_grad[i] = near_pair
            away_grad[i] = away_pair
            scatter_add(away_other, entries[1:2] - rows, away_pair)
            scatter_add([relation_sum], entries[3:4], split(query_grad * head))

        pl.when(~swapped)(lambda: score(False))
        pl.when(swapped)(lambda: score(True))

        ends = (i == steps - 1) | (plan[jnp.minimum(i + 1, steps - 1)] != here)

        @pl.when(ends)
        def _():
            negative_out[here] = split(negative_grad[...])

        @pl.when(ends & ~swapped)
        def _():
            add_negatives(away_other, negative_ids[here] - rows, negative_out[here])

        return carry

    lax.fori_loop(0, steps, one_block, 0)
    start = 0
    for piece in relation_out:
        piece[...] = relation_sum[start : start + piece.shape[0], :]
        start += piece.shape[0]


def scatter_kernel(row, start, first, plan, ids, negative_ids, grads, negative_grads, *sums):
    most = ids.shape[0]
    for piece in sums:
        piece[...] = jnp.zeros_like(piece)

    def one_block(i, carry):
        scatter_add(sums, ids[i][row : row + 1] - start, grads[i])
        return carry

    lax.fori_loop(0, plan[2 * most], one_block, 0)
    for k in range(first, first + negative_ids.shape[0] // 2):

        @pl.when(plan[2 * most + 1 + k] != 0)
        def _(k=k):
            add_negatives(sums, negative_ids[k] - start, negative_grads[k])


def entity_kernel(table, state, returned, own, new_table, new_state):
    grad = returned[...] + own[...]
    lanes = 128
    before = jnp.broadcast_to(state[...], (lanes, table.shape[0])).T[:, :1]
    after = before + jnp.mean(grad * grad, axis=-1, keepdims=True)
    new_table[...] = table[...] - learn_rate * grad / jnp.sqrt(after)
    new_state[...] = jnp.broadcast_to(after, (table.shape[0], lanes)).T[:1]


def relation_kernel(chunk, codes, relations, state, mine, theirs, out, grad, column):
    chunks = mine.shape[0] // chunk
    for k in range(2 * chunks):
        part = (mine, theirs)[k // chunks]
        start = (k % chunks) * chunk
        grad[pl.ds(pl.multiple_of(codes[2] ^ (k * chunk), chunk), chunk), :] = part[start : start + chunk, :]
    count = relations.shape[0]
    column[...] = jnp.ones_like(column)
    column[:, :count] = jnp.broadcast_to(state[...], (column.shape[0], count))
    g = grad[:count, :]
    total = column[...].T[:count, :1] + jnp.mean(g * g, axis=-1, keepdims=True)
    out[...] = relations[...] - learn_rate * g / jnp.sqrt(total)


def exchange(x, axis, mask):
    return lax.ppermute(x, axis, [(i, i ^ mask) for i in range(lax.axis_size(axis))])


def on_device(
    entity_table,
    entity_state,
    relations,
    relation_state,
    head_rows,
    tail_rows,
    relation_ids,
    negative_rows,
    edge_counts,
):
    n = lax.axis_size("sub")
    n_dom = lax.axis_size("dom")
    me_sub = lax.axis_index("sub")
    me_dom = lax.axis_index("dom")
    pair = n_dom // 2
    team = 2 * n
    rows, dims = entity_table.shape
    slots = head_rows.shape[2]
    count = negative_rows.shape[2]
    width = count
    most = slots // width
    rel_rows = -(-relations.shape[0] // 256) * 256
    chips = 2 * n
    chunk = rel_rows // (2 * chips)
    me = lax.shift_right_logical(me_dom, pair.bit_length() - 1) * n + me_sub
    chunk_code = (me_dom & 1) * chips + ((me_dom >> 1) & 1) * n + me_sub
    codes = jnp.stack([me, me_sub * rows, chunk_code * chunk]).astype(i32)

    in_vmem = pl.BlockSpec(memory_space=pltpu.VMEM)
    in_smem = pl.BlockSpec(memory_space=pltpu.SMEM)

    def call(kernel, name, outs, scratch, unit, scalars, arrays, held=True, fetch=False):
        place = (lambda x, t: pltpu.VMEM(x, t)) if held else jax.ShapeDtypeStruct
        return pl.pallas_call(
            kernel,
            in_specs=[in_smem] * len(scalars) + [in_vmem] * len(arrays),
            out_specs=[in_vmem] * len(outs),
            out_shape=[place(x, t) for x, t in outs],
            scratch_shapes=scratch,
            compiler_params=params,
            cost_estimate=pl.CostEstimate(flops=int(slots * dims * unit), bytes_accessed=rows * dims, transcendentals=0),
            name=name,
        )(*scalars, *(pltpu.with_memory_space_constraint(x, pltpu.HBM if fetch else pltpu.VMEM) for x in arrays))

    local, ids = call(
        prep_kernel,
        "prep_kernel",
        [((dims, rows), bf16), ((most + 1, 3, width), jnp.int16)],
        [],
        1,
        (edge_counts,),
        (
            entity_table,
            head_rows.reshape(1, slots),
            tail_rows.reshape(1, slots),
            relation_ids.reshape(1, slots),
            negative_rows.reshape(1, count),
        ),
        fetch=True,
    )

    def to_peer(x, across, aside):
        pairs = [(d * n + s, (d ^ across) * n + (s ^ aside)) for d in range(n_dom) for s in range(n)]
        return lax.ppermute(x, ("dom", "sub"), pairs)

    def along_sub(x):
        return [x] + [exchange(x, "sub", k) for k in range(1, n)]

    away_first = exchange(local, "dom", pair)
    across, local, ids = lax.optimization_barrier((exchange(ids, "dom", pair), local, ids))
    all_ids = along_sub(ids) + along_sub(across)
    near_slab = along_sub(local)

    plan, step_ids, negative_ids = pl.pallas_call(
        functools.partial(plan_kernel, n),
        in_specs=[in_smem] + [in_vmem] * team,
        out_specs=[in_smem, in_vmem, in_vmem],
        out_shape=[
            jax.ShapeDtypeStruct((2 * most + 1 + team,), i32),
            pltpu.VMEM((most, 4, width), i32),
            pltpu.VMEM((team, 1, width), i32),
        ],
        compiler_params=params,
        cost_estimate=pl.CostEstimate(flops=32 * slots * dims * rows, bytes_accessed=slots * dims, transcendentals=0),
        name="plan_kernel",
    )(codes, *(pltpu.with_memory_space_constraint(x, pltpu.VMEM) for x in all_ids))

    near_plan, away_first = lax.optimization_barrier((plan, away_first))
    away_slab = along_sub(away_first)
    near_rows, operator = call(
        near_kernel,
        "near_kernel",
        [((most, dims, width), bf16), ((most, dims, width), f32)],
        [pltpu.VMEM((rel_rows, dims), f32), pltpu.VMEM((2 * dims, rel_rows), bf16)],
        n * rows + 2 * rel_rows,
        (near_plan,),
        (step_ids, relations, *near_slab),
    )
    sums = ((rows, dims), f32)
    pair_out = ((most, 2 * dims, width), bf16)
    near_grad, away_grad, negative_grad, *found = call(
        functools.partial(edge_kernel, n),
        "edge_kernel",
        [pair_out, pair_out, ((team, 2 * count, dims), bf16)]
        + [sums] * (n - 1)
        + [((chunk, dims), f32)] * chips
        + [((chips * chunk, dims), f32)],
        [pltpu.VMEM((count, dims), bf16), pltpu.VMEM((dims, count), bf16), pltpu.VMEM((count, dims), f32), pltpu.VMEM((rel_rows, dims), f32)],
        (2 * n - 1) * rows + 3 * count + 2 * rel_rows,
        (plan,),
        (step_ids, negative_ids, near_rows, operator, *near_slab, *away_slab),
    )
    away_other, relation_part = found[: n - 1], found[n - 1 :]

    def scatter(name, row, start, parts, first, plan, grads):
        return call(
            functools.partial(scatter_kernel, row, start, first),
            name,
            [sums] * parts,
            [],
            0,
            (plan,),
            (step_ids, negative_ids, grads, negative_grad),
        )

    scale = 2.0 ** -(math.ceil(math.log2(team * slots * 24 / 65504.0)) + 1)

    def narrow(x):
        return (x * scale).astype(jnp.float16)

    def widen(x):
        return x.astype(f32) * (1.0 / scale)

    def to_chip(x, k):
        return to_peer(x, k // n * 2, k % n)

    other_core = exchange(relation_part[chips], "dom", 1)
    partial = [relation_part[k] + other_core[k * chunk : (k + 1) * chunk] for k in range(chips)]
    away_other = [narrow(x) for x in away_other]
    partial, plan, away_other = lax.optimization_barrier((partial, plan, away_other))
    chunk_total = partial[0]
    for k in range(1, chips):
        chunk_total = chunk_total + to_chip(partial[k], k)
    away_received = [widen(exchange(away_other[k - 1], "sub", k)) for k in range(1, n)]
    chunk_total, plan = lax.optimization_barrier((chunk_total, plan))
    terms = [chunk_total] + [exchange(chunk_total, "dom", mask) for mask in range(4, n_dom, 4)]
    (away_total,) = scatter("away_kernel", 1, 0, 1, 0, plan, away_grad)
    for x in away_received:
        away_total = away_total + x
    away_total = narrow(away_total)
    while len(terms) > 1:
        terms = [terms[k] + terms[k + 1] for k in range(0, len(terms), 2)]
    plan, away_total, chunk_total = lax.optimization_barrier((plan, away_total, terms[0]))
    returned = exchange(away_total, "dom", pair)
    near_other = scatter("own_other_kernel", 0, rows, n - 1, n, plan, near_grad)
    near_other = [narrow(x) for x in near_other]
    plan, near_other, chunk_total = lax.optimization_barrier((plan, near_other, chunk_total))
    mine = jnp.concatenate([chunk_total] + [to_chip(chunk_total, k) for k in range(1, chips)], axis=0)
    near_received = [widen(exchange(near_other[k - 1], "sub", k)) for k in range(1, n)]
    (near_sum,) = scatter("own_kernel", 0, 0, 1, n, plan, near_grad)
    returned, mine, near_sum = lax.optimization_barrier((returned, mine, near_sum))
    theirs = exchange(mine, "dom", 1)
    (new_relations,) = call(
        functools.partial(relation_kernel, chunk),
        "relation_kernel",
        [(relations.shape, f32)],
        [pltpu.VMEM((rel_rows, dims), f32), pltpu.VMEM((128, rel_rows), f32)],
        0,
        (codes,),
        (relations, relation_state.reshape(1, -1), mine, theirs),
        held=False,
    )
    returned = widen(returned)
    for x in near_received:
        returned = returned + x
    new_table, new_state = call(
        entity_kernel,
        "entity_kernel",
        [((rows, dims), f32), ((1, rows), f32)],
        [],
        1,
        (),
        (entity_table, entity_state.reshape(1, rows), returned, near_sum),
        held=False,
    )
    return (new_table, new_state.reshape(rows), new_relations)


def solution(mesh):
    in_specs = (
        P(("dom", "sub"), None),
        P(("dom", "sub")),
        P(),
        P(),
        P("dom", "sub", None),
        P("dom", "sub", None),
        P("dom", "sub", None),
        P("dom", "sub", None),
        P("dom", "sub"),
    )
    out_specs = (P(("dom", "sub"), None), P(("dom", "sub")), P())
    return jax.shard_map(
        on_device, mesh=mesh, in_specs=in_specs, out_specs=out_specs, check_vma=False
    )
```

```python
import functools
import math

import jax
import jax.numpy as jnp
from jax import lax
from jax.experimental import pallas as pl
from jax.experimental.pallas import tpu as pltpu
from jax.sharding import PartitionSpec as P

learn_rate = 0.1
bf16 = jnp.bfloat16
f32 = jnp.float32
i32 = jnp.int32
params = pltpu.CompilerParams(vmem_limit_bytes=10 * 2**20)


def dot(a, b):
    return jnp.dot(a, b, preferred_element_type=f32)


def dot_nt(a, b):
    return lax.dot_general(a, b, (((1,), (1,)), ((), ())), preferred_element_type=f32)


def one_hot(ids, rows):
    places = lax.broadcasted_iota(jnp.int16, (rows, ids.shape[1]), 0)
    return jnp.where(places == ids.astype(jnp.int16), jnp.ones((), bf16), jnp.zeros((), bf16))


def split(x):
    high = x.astype(bf16)
    return jnp.concatenate([high, (x - high.astype(f32)).astype(bf16)], axis=0)


def gather(pieces, ids):
    rows = pieces[0].shape[1]
    hot = one_hot(ids, len(pieces) * rows)
    total = dot(pieces[0][...], hot[:rows])
    for k in range(1, len(pieces)):
        total = total + dot(pieces[k][...], hot[k * rows : (k + 1) * rows])
    return total


def scatter_add(pieces, ids, pair):
    dims = pair.shape[0] // 2
    hot = one_hot(ids, sum(piece.shape[0] for piece in pieces))
    start = 0
    for piece in pieces:
        part = hot[start : start + piece.shape[0]]
        piece[...] += dot_nt(part, pair[:dims]) + dot_nt(part, pair[dims:])
        start += piece.shape[0]


def add_negatives(pieces, ids, pair):
    count = pair.shape[0] // 2
    hot = one_hot(ids, sum(piece.shape[0] for piece in pieces))
    start = 0
    for piece in pieces:
        part = hot[start : start + piece.shape[0]]
        piece[...] += dot(part, pair[:count]) + dot(part, pair[count:])
        start += piece.shape[0]


def rows_kernel(table, out):
    out[...] = table[...].T.astype(bf16)


def ids_kernel(count, heads, tails, kinds, negatives, ids_out):
    blocks, _, width = ids_out.shape
    for j in range(blocks - 1):
        at = slice(j * width, (j + 1) * width)
        block = jnp.concatenate([heads[:, at], tails[:, at], kinds[:, at]], axis=0)
        ids_out[j] = block.astype(jnp.int16)
    last = jnp.concatenate([negatives[...], jnp.full((2, width), count[0, 0], i32)], axis=0)
    ids_out[blocks - 1] = last.astype(jnp.int16)


def plan_kernel(n, codes, *refs):
    sources, (plan, step_ids, negative_ids) = refs[:-3], refs[-3:]
    team = len(sources)
    most, _, width = step_ids.shape
    me = codes[0]
    counts, blocks = [], []
    for k, ids in enumerate(sources):
        last = ids[most].astype(i32)
        counts.append(jnp.max(last[1:2]))
        blocks.append(lax.div(counts[k] + (width - 1), i32(width)))
        negative_ids[k] = last[0:1] ^ codes[1]
    total = sum(blocks)
    low = lax.div(me * total, i32(team))
    high = lax.div((me + 1) * total, i32(team))
    plan[2 * most] = high - low
    before = []
    for k in range(team):
        ahead = [jnp.where((me ^ j) < (me ^ k), blocks[j], 0) for j in range(team) if j != k]
        before.append(sum(ahead))
        seen = (before[k] < high) & (before[k] + blocks[k] > low)
        plan[2 * most + 1 + k] = seen.astype(i32)

    def one_step(i, carry):
        line = jnp.minimum(low + i, high - 1)
        for k, ids in enumerate(sources):

            @pl.when((line >= before[k]) & (line < before[k] + blocks[k]))
            def _(k=k, ids=ids):
                nth = line - before[k]
                plan[i] = k
                plan[most + i] = jnp.clip(counts[k] - nth * width, 0, width)
                entries = ids[nth].astype(i32)
                near, away = (0, 1) if k < n else (1, 0)
                step_ids[i, 0:1] = entries[near : near + 1] ^ codes[1]
                step_ids[i, 1:2] = entries[away : away + 1] ^ codes[1]
                step_ids[i, 2:3] = entries[2:3]
                step_ids[i, 3:4] = entries[2:3] ^ codes[2]

        return carry

    lax.fori_loop(0, high - low, one_step, 0)


def near_kernel(plan, ids, relations, *refs):
    slab, (rows_out, operator_out, rel_full, rel_split) = refs[:-4], refs[-4:]
    dims = relations.shape[1]
    rel_full[...] = jnp.zeros_like(rel_full)
    rel_full[: relations.shape[0], :] = relations[...]
    rel_split[...] = split(rel_full[...].T)

    def one_block(i, carry):
        entries = ids[i]
        rows_out[i] = gather(slab, entries[0:1]).astype(bf16)
        both = dot(rel_split[...], one_hot(entries[2:3], rel_full.shape[0]))
        operator_out[i] = both[:dims] + both[dims:]
        return carry

    lax.fori_loop(0, plan[2 * ids.shape[0]], one_block, 0)


def edge_kernel(n, plan, ids, negative_ids, near_in, operator_in, *refs):
    near, away = refs[:n], refs[n : 2 * n]
    near_grad, away_grad, negative_out = refs[2 * n : 2 * n + 3]
    away_other = refs[2 * n + 3 : 3 * n + 2]
    relation_out, (table, table_t, negative_grad, relation_sum) = refs[3 * n + 2 : -4], refs[-4:]
    most, _, width = ids.shape
    steps = plan[2 * most]
    count = table.shape[0]
    for piece in (*away_other, relation_sum):
        piece[...] = jnp.zeros_like(piece)
    rows = away[0].shape[1]

    def one_block(i, carry):
        here = plan[i]
        swapped = here >= n

        def take_table(slab):
            found = gather(slab, negative_ids[here])
            table_t[...] = found.astype(bf16)
            table[...] = found.T.astype(bf16)
            negative_grad[...] = jnp.zeros_like(negative_grad)

        fresh = (i == 0) | (plan[jnp.maximum(i - 1, 0)] != here)
        pl.when(fresh & ~swapped)(lambda: take_table(away))
        pl.when(fresh & swapped)(lambda: take_table(near))

        entries = ids[i]

        def score(swapped):
            alive = (lax.broadcasted_iota(i32, (1, width), 1) < plan[most + i]).astype(f32)
            near_rows = near_in[i].astype(f32)
            away_rows = gather(away, entries[1:2])
            head, tail = (away_rows, near_rows) if swapped else (near_rows, away_rows)
            operator = operator_in[i]
            query = head * operator
            query_b = query.astype(bf16)
            positive = jnp.sum(query * tail, axis=0, keepdims=True)
            scores = dot(table[...], query_b)
            pos_coef = -jax.nn.sigmoid(-positive) * alive
            neg_coef = (jax.nn.sigmoid(scores) * (alive * (1.0 / count))).astype(bf16)
            query_grad = pos_coef * tail + dot(table_t[...], neg_coef)
            negative_grad[...] += dot_nt(neg_coef, query_b)
            head_pair, tail_pair = split(query_grad * operator), split(pos_coef * query)
            near_pair, away_pair = (tail_pair, head_pair) if swapped else (head_pair, tail_pair)
            near_grad[i] = near_pair
            away_grad[i] = away_pair
            scatter_add(away_other, entries[1:2] - rows, away_pair)
            scatter_add([relation_sum], entries[3:4], split(query_grad * head))

        pl.when(~swapped)(lambda: score(False))
        pl.when(swapped)(lambda: score(True))

        ends = (i == steps - 1) | (plan[jnp.minimum(i + 1, steps - 1)] != here)

        @pl.when(ends)
        def _():
            negative_out[here] = split(negative_grad[...])

        @pl.when(ends & ~swapped)
        def _():
            add_negatives(away_other, negative_ids[here] - rows, negative_out[here])

        return carry

    lax.fori_loop(0, steps, one_block, 0)
    start = 0
    for piece in relation_out:
        piece[...] = relation_sum[start : start + piece.shape[0], :]
        start += piece.shape[0]


def scatter_kernel(row, start, first, plan, ids, negative_ids, grads, negative_grads, *sums):
    most = ids.shape[0]
    for piece in sums:
        piece[...] = jnp.zeros_like(piece)

    def one_block(i, carry):
        scatter_add(sums, ids[i][row : row + 1] - start, grads[i])
        return carry

    lax.fori_loop(0, plan[2 * most], one_block, 0)
    for k in range(first, first + negative_ids.shape[0] // 2):

        @pl.when(plan[2 * most + 1 + k] != 0)
        def _(k=k):
            add_negatives(sums, negative_ids[k] - start, negative_grads[k])


def entity_kernel(table, state, returned, own, new_table, new_state):
    grad = returned[...] + own[...]
    lanes = 128
    before = jnp.broadcast_to(state[...], (lanes, table.shape[0])).T[:, :1]
    after = before + jnp.mean(grad * grad, axis=-1, keepdims=True)
    new_table[...] = table[...] - learn_rate * grad / jnp.sqrt(after)
    new_state[...] = jnp.broadcast_to(after, (table.shape[0], lanes)).T[:1]


def relation_kernel(chunk, codes, relations, state, mine, theirs, out, grad, column):
    chunks = mine.shape[0] // chunk
    for k in range(2 * chunks):
        part = (mine, theirs)[k // chunks]
        start = (k % chunks) * chunk
        grad[pl.ds(pl.multiple_of(codes[2] ^ (k * chunk), chunk), chunk), :] = part[start : start + chunk, :]
    count = relations.shape[0]
    column[...] = jnp.ones_like(column)
    column[:, :count] = jnp.broadcast_to(state[...], (column.shape[0], count))
    g = grad[:count, :]
    total = column[...].T[:count, :1] + jnp.mean(g * g, axis=-1, keepdims=True)
    out[...] = relations[...] - learn_rate * g / jnp.sqrt(total)


def exchange(x, axis, mask):
    return lax.ppermute(x, axis, [(i, i ^ mask) for i in range(lax.axis_size(axis))])


def on_device(
    entity_table,
    entity_state,
    relations,
    relation_state,
    head_rows,
    tail_rows,
    relation_ids,
    negative_rows,
    edge_counts,
):
    n = lax.axis_size("sub")
    n_dom = lax.axis_size("dom")
    me_sub = lax.axis_index("sub")
    me_dom = lax.axis_index("dom")
    pair = n_dom // 2
    team = 2 * n
    rows, dims = entity_table.shape
    slots = head_rows.shape[2]
    count = negative_rows.shape[2]
    width = count
    most = slots // width
    rel_rows = -(-relations.shape[0] // 256) * 256
    chips = 2 * n
    chunk = rel_rows // (2 * chips)
    me = lax.shift_right_logical(me_dom, pair.bit_length() - 1) * n + me_sub
    chunk_code = (me_dom & 1) * chips + ((me_dom >> 1) & 1) * n + me_sub
    codes = jnp.stack([me, me_sub * rows, chunk_code * chunk]).astype(i32)

    in_vmem = pl.BlockSpec(memory_space=pltpu.VMEM)
    in_smem = pl.BlockSpec(memory_space=pltpu.SMEM)

    def call(kernel, name, outs, scratch, unit, scalars, arrays, held=True, fetch=False):
        place = (lambda x, t: pltpu.VMEM(x, t)) if held else jax.ShapeDtypeStruct
        return pl.pallas_call(
            kernel,
            in_specs=[in_smem] * len(scalars) + [in_vmem] * len(arrays),
            out_specs=[in_vmem] * len(outs),
            out_shape=[place(x, t) for x, t in outs],
            scratch_shapes=scratch,
            compiler_params=params,
            cost_estimate=pl.CostEstimate(flops=int(slots * dims * unit), bytes_accessed=rows * dims, transcendentals=0),
            name=name,
        )(*scalars, *(pltpu.with_memory_space_constraint(x, pltpu.HBM if fetch else pltpu.VMEM) for x in arrays))

    (ids,) = call(
        ids_kernel,
        "ids_kernel",
        [((most + 1, 3, width), jnp.int16)],
        [],
        1,
        (edge_counts,),
        (
            head_rows.reshape(1, slots),
            tail_rows.reshape(1, slots),
            relation_ids.reshape(1, slots),
            negative_rows.reshape(1, count),
        ),
        fetch=True,
    )
    ids, table = lax.optimization_barrier((ids, entity_table))
    (local,) = call(rows_kernel, "rows_kernel", [((dims, rows), bf16)], [], 1, (), (table,), fetch=True)

    def to_peer(x, across, aside):
        pairs = [(d * n + s, (d ^ across) * n + (s ^ aside)) for d in range(n_dom) for s in range(n)]
        return lax.ppermute(x, ("dom", "sub"), pairs)

    def along_sub(x):
        return [x] + [exchange(x, "sub", k) for k in range(1, n)]

    all_ids = along_sub(ids) + along_sub(exchange(ids, "dom", pair))
    near_slab = along_sub(local)
    away_first = exchange(local, "dom", pair)

    plan, step_ids, negative_ids = pl.pallas_call(
        functools.partial(plan_kernel, n),
        in_specs=[in_smem] + [in_vmem] * team,
        out_specs=[in_smem, in_vmem, in_vmem],
        out_shape=[
            jax.ShapeDtypeStruct((2 * most + 1 + team,), i32),
            pltpu.VMEM((most, 4, width), i32),
            pltpu.VMEM((team, 1, width), i32),
        ],
        compiler_params=params,
        cost_estimate=pl.CostEstimate(flops=32 * slots * dims * rows, bytes_accessed=slots * dims, transcendentals=0),
        name="plan_kernel",
    )(codes, *(pltpu.with_memory_space_constraint(x, pltpu.VMEM) for x in all_ids))

    near_plan, away_first = lax.optimization_barrier((plan, away_first))
    away_slab = along_sub(away_first)
    near_rows, operator = call(
        near_kernel,
        "near_kernel",
        [((most, dims, width), bf16), ((most, dims, width), f32)],
        [pltpu.VMEM((rel_rows, dims), f32), pltpu.VMEM((2 * dims, rel_rows), bf16)],
        n * rows + 2 * rel_rows,
        (near_plan,),
        (step_ids, relations, *near_slab),
    )
    sums = ((rows, dims), f32)
    pair_out = ((most, 2 * dims, width), bf16)
    near_grad, away_grad, negative_grad, *found = call(
        functools.partial(edge_kernel, n),
        "edge_kernel",
        [pair_out, pair_out, ((team, 2 * count, dims), bf16)]
        + [sums] * (n - 1)
        + [((chunk, dims), f32)] * chips
        + [((chips * chunk, dims), f32)],
        [pltpu.VMEM((count, dims), bf16), pltpu.VMEM((dims, count), bf16), pltpu.VMEM((count, dims), f32), pltpu.VMEM((rel_rows, dims), f32)],
        (2 * n - 1) * rows + 3 * count + 2 * rel_rows,
        (plan,),
        (step_ids, negative_ids, near_rows, operator, *near_slab, *away_slab),
    )
    away_other, relation_part = found[: n - 1], found[n - 1 :]

    def scatter(name, row, start, parts, first, plan, grads):
        return call(
            functools.partial(scatter_kernel, row, start, first),
            name,
            [sums] * parts,
            [],
            0,
            (plan,),
            (step_ids, negative_ids, grads, negative_grad),
        )

    scale = 2.0 ** -(math.ceil(math.log2(team * slots * 24 / 65504.0)) + 1)

    def narrow(x):
        return (x * scale).astype(jnp.float16)

    def widen(x):
        return x.astype(f32) * (1.0 / scale)

    def to_chip(x, k):
        return to_peer(x, k // n * 2, k % n)

    other_core = exchange(relation_part[chips], "dom", 1)
    partial = [relation_part[k] + other_core[k * chunk : (k + 1) * chunk] for k in range(chips)]
    away_other = [narrow(x) for x in away_other]
    partial, plan, away_other = lax.optimization_barrier((partial, plan, away_other))
    chunk_total = partial[0]
    for k in range(1, chips):
        chunk_total = chunk_total + to_chip(partial[k], k)
    away_received = [widen(exchange(away_other[k - 1], "sub", k)) for k in range(1, n)]
    (away_total,) = scatter("away_kernel", 1, 0, 1, 0, plan, away_grad)
    chunk_total, away_total, plan = lax.optimization_barrier((chunk_total, away_total, plan))
    masks = [4 << k for k in range((n_dom // 4).bit_length() - 1)]
    for mask in masks[:-1]:
        chunk_total = chunk_total + exchange(chunk_total, "dom", mask)
    near_other = scatter("own_other_kernel", 0, rows, n - 1, n, plan, near_grad)
    near_other = [narrow(x) for x in near_other]
    chunk_total, near_other, plan = lax.optimization_barrier((chunk_total, near_other, plan))
    near_received = [widen(exchange(near_other[k - 1], "sub", k)) for k in range(1, n)]
    for mask in masks[-1:]:
        chunk_total = chunk_total + exchange(chunk_total, "dom", mask)
    (near_sum,) = scatter("own_kernel", 0, 0, 1, n, plan, near_grad)
    for x in away_received:
        away_total = away_total + x
    away_total = narrow(away_total)
    chunk_total, away_total, near_sum = lax.optimization_barrier((chunk_total, away_total, near_sum))
    returned = exchange(away_total, "dom", pair)
    chunk_total, near_received = lax.optimization_barrier((chunk_total, near_received))
    mine = jnp.concatenate([chunk_total] + [to_chip(chunk_total, k) for k in range(1, chips)], axis=0)
    returned, mine = lax.optimization_barrier((returned, mine))
    theirs = exchange(mine, "dom", 1)
    (new_relations,) = call(
        functools.partial(relation_kernel, chunk),
        "relation_kernel",
        [(relations.shape, f32)],
        [pltpu.VMEM((rel_rows, dims), f32), pltpu.VMEM((128, rel_rows), f32)],
        0,
        (codes,),
        (relations, relation_state.reshape(1, -1), mine, theirs),
        held=False,
    )
    returned = widen(returned)
    for x in near_received:
        returned = returned + x
    new_table, new_state = call(
        entity_kernel,
        "entity_kernel",
        [((rows, dims), f32), ((1, rows), f32)],
        [],
        1,
        (),
        (entity_table, entity_state.reshape(1, rows), returned, near_sum),
        held=False,
    )
    return (new_table, new_state.reshape(rows), new_relations)


def solution(mesh):
    in_specs = (
        P(("dom", "sub"), None),
        P(("dom", "sub")),
        P(),
        P(),
        P("dom", "sub", None),
        P("dom", "sub", None),
        P("dom", "sub", None),
        P("dom", "sub", None),
        P("dom", "sub"),
    )
    out_specs = (P(("dom", "sub"), None), P(("dom", "sub")), P())
    return jax.shard_map(
        on_device, mesh=mesh, in_specs=in_specs, out_specs=out_specs, check_vma=False
    )
```

```python
import functools
import math

import jax
import jax.numpy as jnp
from jax import lax
from jax.experimental import pallas as pl
from jax.experimental.pallas import tpu as pltpu
from jax.sharding import PartitionSpec as P

learn_rate = 0.1
bf16 = jnp.bfloat16
f32 = jnp.float32
i32 = jnp.int32
params = pltpu.CompilerParams(vmem_limit_bytes=10 * 2**20)


def dot(a, b):
    return jnp.dot(a, b, preferred_element_type=f32)


def dot_nt(a, b):
    return lax.dot_general(a, b, (((1,), (1,)), ((), ())), preferred_element_type=f32)


def one_hot(ids, rows):
    places = lax.broadcasted_iota(jnp.int16, (rows, ids.shape[1]), 0)
    return jnp.where(places == ids.astype(jnp.int16), jnp.ones((), bf16), jnp.zeros((), bf16))


def split(x):
    high = x.astype(bf16)
    return jnp.concatenate([high, (x - high.astype(f32)).astype(bf16)], axis=0)


def gather(pieces, hot):
    rows = pieces[0].shape[1]
    total = dot(pieces[0][...], hot[:rows])
    for k in range(1, len(pieces)):
        total = total + dot(pieces[k][...], hot[k * rows : (k + 1) * rows])
    return total


def scatter_add(pieces, hot, pair):
    dims = pair.shape[0] // 2
    start = 0
    for piece in pieces:
        part = hot[start : start + piece.shape[0]]
        piece[...] += dot_nt(part, pair[:dims]) + dot_nt(part, pair[dims:])
        start += piece.shape[0]


def add_negatives(pieces, hot, pair):
    count = pair.shape[0] // 2
    start = 0
    for piece in pieces:
        part = hot[start : start + piece.shape[0]]
        piece[...] += dot(part, pair[:count]) + dot(part, pair[count:])
        start += piece.shape[0]


def rows_kernel(table, out):
    out[...] = table[...].T.astype(bf16)


def ids_kernel(count, heads, tails, kinds, negatives, ids_out):
    blocks, _, width = ids_out.shape
    for j in range(blocks - 1):
        at = slice(j * width, (j + 1) * width)
        block = jnp.concatenate([heads[:, at], tails[:, at], kinds[:, at]], axis=0)
        ids_out[j] = block.astype(jnp.int16)
    last = jnp.concatenate([negatives[...], jnp.full((2, width), count[0, 0], i32)], axis=0)
    ids_out[blocks - 1] = last.astype(jnp.int16)


def plan_kernel(n, codes, *refs):
    sources, (plan, step_ids, negative_ids) = refs[:-3], refs[-3:]
    team = len(sources)
    most, _, width = step_ids.shape
    me = codes[0]
    counts, blocks = [], []
    for k, ids in enumerate(sources):
        last = ids[most].astype(i32)
        counts.append(jnp.max(last[1:2]))
        blocks.append(lax.div(counts[k] + (width - 1), i32(width)))
        negative_ids[k] = last[0:1] ^ codes[1]
    total = sum(blocks)
    low = lax.div(me * total, i32(team))
    high = lax.div((me + 1) * total, i32(team))
    plan[2 * most] = high - low
    before = []
    for k in range(team):
        ahead = [jnp.where((me ^ j) < (me ^ k), blocks[j], 0) for j in range(team) if j != k]
        before.append(sum(ahead))
        seen = (before[k] < high) & (before[k] + blocks[k] > low)
        plan[2 * most + 1 + k] = seen.astype(i32)

    def one_step(i, carry):
        line = jnp.minimum(low + i, high - 1)
        for k, ids in enumerate(sources):

            @pl.when((line >= before[k]) & (line < before[k] + blocks[k]))
            def _(k=k, ids=ids):
                nth = line - before[k]
                plan[i] = k
                plan[most + i] = jnp.clip(counts[k] - nth * width, 0, width)
                entries = ids[nth].astype(i32)
                near, away = (0, 1) if k < n else (1, 0)
                step_ids[i, 0:1] = entries[near : near + 1] ^ codes[1]
                step_ids[i, 1:2] = entries[away : away + 1] ^ codes[1]
                step_ids[i, 2:3] = entries[2:3]

        return carry

    lax.fori_loop(0, high - low, one_step, 0)


def near_kernel(plan, ids, relations, *refs):
    slab, (rows_out, operator_out, rel_full, rel_split) = refs[:-4], refs[-4:]
    dims = relations.shape[1]
    n, rows = len(slab), slab[0].shape[1]
    rel_full[...] = jnp.zeros_like(rel_full)
    rel_full[: relations.shape[0], :] = relations[...]
    rel_split[...] = split(rel_full[...].T)

    def one_block(i):
        entries = ids[i]
        rows_out[i] = gather(slab, one_hot(entries[0:1], n * rows)).astype(bf16)
        both = dot(rel_split[...], one_hot(entries[2:3], rel_full.shape[0]))
        operator_out[i] = both[:dims] + both[dims:]

    steps = plan[2 * ids.shape[0]]

    def two_blocks(i, carry):
        one_block(2 * i)
        one_block(2 * i + 1)
        return carry

    lax.fori_loop(0, steps >> 1, two_blocks, 0)
    pl.when((steps & 1) == 1)(lambda: one_block(steps - 1))


def edge_kernel(n, codes, plan, ids, negative_ids, near_in, operator_in, *refs):
    near, away = refs[:n], refs[n : 2 * n]
    near_grad, away_grad, negative_out = refs[2 * n : 2 * n + 3]
    away_other = refs[2 * n + 3 : 3 * n + 2]
    relation_out = refs[3 * n + 2 : -5]
    table, table_t, negative_grad, relation_sum, ordered = refs[-5:]
    most, _, width = ids.shape
    steps = plan[2 * most]
    count = table.shape[0]
    for piece in (*away_other, relation_sum):
        piece[...] = jnp.zeros_like(piece)
    rows = away[0].shape[1]

    def one_block(i, carry):
        here = plan[i]
        swapped = here >= n

        def take_table(slab):
            found = gather(slab, one_hot(negative_ids[here], n * rows))
            table_t[...] = found.astype(bf16)
            table[...] = found.T.astype(bf16)
            negative_grad[...] = jnp.zeros_like(negative_grad)

        fresh = (i == 0) | (plan[jnp.maximum(i - 1, 0)] != here)
        pl.when(fresh & ~swapped)(lambda: take_table(away))
        pl.when(fresh & swapped)(lambda: take_table(near))

        entries = ids[i]

        def score(swapped):
            alive = (lax.broadcasted_iota(i32, (1, width), 1) < plan[most + i]).astype(f32)
            near_rows = near_in[i].astype(f32)
            away_hot = one_hot(entries[1:2], n * rows)
            away_rows = gather(away, away_hot)
            head, tail = (away_rows, near_rows) if swapped else (near_rows, away_rows)
            operator = operator_in[i]
            query = head * operator
            query_b = query.astype(bf16)
            positive = jnp.sum(query * tail, axis=0, keepdims=True)
            scores = dot(table[...], query_b)
            pos_coef = -jax.nn.sigmoid(-positive) * alive
            neg_coef = (jax.nn.sigmoid(scores) * (alive * (1.0 / count))).astype(bf16)
            query_grad = pos_coef * tail + dot(table_t[...], neg_coef)
            negative_grad[...] += dot_nt(neg_coef, query_b)
            head_pair, tail_pair = split(query_grad * operator), split(pos_coef * query)
            near_pair, away_pair = (tail_pair, head_pair) if swapped else (head_pair, tail_pair)
            near_grad[i] = near_pair
            away_grad[i] = away_pair
            scatter_add(away_other, away_hot[rows:], away_pair)
            scatter_add([relation_sum], one_hot(entries[2:3], relation_sum.shape[0]), split(query_grad * head))

        pl.when(~swapped)(lambda: score(False))
        pl.when(swapped)(lambda: score(True))

        ends = (i == steps - 1) | (plan[jnp.minimum(i + 1, steps - 1)] != here)

        @pl.when(ends)
        def _():
            negative_out[here] = split(negative_grad[...])

        @pl.when(ends & ~swapped)
        def _():
            add_negatives(away_other, one_hot(negative_ids[here] - rows, (n - 1) * rows), negative_out[here])

        return carry

    lax.fori_loop(0, steps, one_block, 0)
    chunk = relation_out[0].shape[0]
    ordered[...] = jnp.zeros_like(ordered)
    ordered[: relation_sum.shape[0], :] = relation_sum[...]
    start = 0
    for piece in relation_out:
        for k in range(0, piece.shape[0], chunk):
            at = pl.multiple_of(codes[2] ^ (start + k), chunk)
            piece[k : k + chunk, :] = ordered[pl.ds(at, chunk), :]
        start += piece.shape[0]


def scatter_kernel(row, start, first, plan, ids, negative_ids, grads, negative_grads, *sums):
    most = ids.shape[0]
    height = sum(piece.shape[0] for piece in sums)
    for piece in sums:
        piece[...] = jnp.zeros_like(piece)

    steps = plan[2 * most]

    def hot_of(i):
        return one_hot(ids[i][row : row + 1] - start, height)

    def two_blocks(i, carry):
        hot = jnp.concatenate([hot_of(2 * i), hot_of(2 * i + 1)], axis=1)
        scatter_add(sums, hot, jnp.concatenate([grads[2 * i], grads[2 * i + 1]], axis=1))
        return carry

    lax.fori_loop(0, steps >> 1, two_blocks, 0)

    @pl.when((steps & 1) == 1)
    def _():
        scatter_add(sums, hot_of(steps - 1), grads[steps - 1])

    for k in range(first, first + negative_ids.shape[0] // 2):

        @pl.when(plan[2 * most + 1 + k] != 0)
        def _(k=k):
            add_negatives(sums, one_hot(negative_ids[k] - start, height), negative_grads[k])


def entity_kernel(table, state, returned, own, new_table, new_state):
    grad = returned[...] + own[...]
    lanes = 128
    before = jnp.broadcast_to(state[...], (lanes, table.shape[0])).T[:, :1]
    after = before + jnp.mean(grad * grad, axis=-1, keepdims=True)
    new_table[...] = table[...] - learn_rate * grad / jnp.sqrt(after)
    new_state[...] = jnp.broadcast_to(after, (table.shape[0], lanes)).T[:1]


def relation_kernel(chunk, codes, relations, state, mine, theirs, out, grad, column):
    chunks = mine.shape[0] // chunk
    for k in range(2 * chunks):
        part = (mine, theirs)[k // chunks]
        start = (k % chunks) * chunk
        grad[pl.ds(pl.multiple_of(codes[2] ^ (k * chunk), chunk), chunk), :] = part[start : start + chunk, :]
    count = relations.shape[0]
    column[...] = jnp.ones_like(column)
    column[:, :count] = jnp.broadcast_to(state[...], (column.shape[0], count))
    g = grad[:count, :]
    total = column[...].T[:count, :1] + jnp.mean(g * g, axis=-1, keepdims=True)
    out[...] = relations[...] - learn_rate * g / jnp.sqrt(total)


def exchange(x, axis, mask):
    return lax.ppermute(x, axis, [(i, i ^ mask) for i in range(lax.axis_size(axis))])


def on_device(
    entity_table,
    entity_state,
    relations,
    relation_state,
    head_rows,
    tail_rows,
    relation_ids,
    negative_rows,
    edge_counts,
):
    n = lax.axis_size("sub")
    n_dom = lax.axis_size("dom")
    me_sub = lax.axis_index("sub")
    me_dom = lax.axis_index("dom")
    pair = n_dom // 2
    team = 2 * n
    rows, dims = entity_table.shape
    slots = head_rows.shape[2]
    count = negative_rows.shape[2]
    width = count
    most = slots // width
    rel_rows = -(-relations.shape[0] // 256) * 256
    chips = 2 * n
    chunk = rel_rows // (2 * chips)
    me = lax.shift_right_logical(me_dom, pair.bit_length() - 1) * n + me_sub
    chunk_code = (me_dom & 1) * chips + ((me_dom >> 1) & 1) * n + me_sub
    codes = jnp.stack([me, me_sub * rows, chunk_code * chunk]).astype(i32)

    in_vmem = pl.BlockSpec(memory_space=pltpu.VMEM)
    in_smem = pl.BlockSpec(memory_space=pltpu.SMEM)

    def call(kernel, name, outs, scratch, unit, scalars, arrays, held=True, fetch=False):
        place = (lambda x, t: pltpu.VMEM(x, t)) if held else jax.ShapeDtypeStruct
        return pl.pallas_call(
            kernel,
            in_specs=[in_smem] * len(scalars) + [in_vmem] * len(arrays),
            out_specs=[in_vmem] * len(outs),
            out_shape=[place(x, t) for x, t in outs],
            scratch_shapes=scratch,
            compiler_params=params,
            cost_estimate=pl.CostEstimate(flops=int(slots * dims * unit), bytes_accessed=rows * dims, transcendentals=0),
            name=name,
        )(*scalars, *(pltpu.with_memory_space_constraint(x, pltpu.HBM if fetch else pltpu.VMEM) for x in arrays))

    (ids,) = call(
        ids_kernel,
        "ids_kernel",
        [((most + 1, 3, width), jnp.int16)],
        [],
        1,
        (edge_counts,),
        (
            head_rows.reshape(1, slots),
            tail_rows.reshape(1, slots),
            relation_ids.reshape(1, slots),
            negative_rows.reshape(1, count),
        ),
        fetch=True,
    )
    ids, table = lax.optimization_barrier((ids, entity_table))
    (local,) = call(rows_kernel, "rows_kernel", [((dims, rows), bf16)], [], 1, (), (table,), fetch=True)

    def to_peer(x, across, aside):
        pairs = [(d * n + s, (d ^ across) * n + (s ^ aside)) for d in range(n_dom) for s in range(n)]
        return lax.ppermute(x, ("dom", "sub"), pairs)

    def along_sub(x):
        return [x] + [exchange(x, "sub", k) for k in range(1, n)]

    all_ids = along_sub(ids) + along_sub(exchange(ids, "dom", pair))
    near_slab = along_sub(local)
    away_first = exchange(local, "dom", pair)

    plan, step_ids, negative_ids = pl.pallas_call(
        functools.partial(plan_kernel, n),
        in_specs=[in_smem] + [in_vmem] * team,
        out_specs=[in_smem, in_vmem, in_vmem],
        out_shape=[
            jax.ShapeDtypeStruct((2 * most + 1 + team,), i32),
            pltpu.VMEM((most, 3, width), i32),
            pltpu.VMEM((team, 1, width), i32),
        ],
        compiler_params=params,
        cost_estimate=pl.CostEstimate(flops=32 * slots * dims * rows, bytes_accessed=slots * dims, transcendentals=0),
        name="plan_kernel",
    )(codes, *(pltpu.with_memory_space_constraint(x, pltpu.VMEM) for x in all_ids))

    near_plan, away_first = lax.optimization_barrier((plan, away_first))
    away_slab = along_sub(away_first)
    near_rows, operator = call(
        near_kernel,
        "near_kernel",
        [((most, dims, width), bf16), ((most, dims, width), f32)],
        [pltpu.VMEM((rel_rows, dims), f32), pltpu.VMEM((2 * dims, rel_rows), bf16)],
        n * rows + 2 * rel_rows,
        (near_plan,),
        (step_ids, relations, *near_slab),
    )
    sums = ((rows, dims), f32)
    pair_out = ((most, 2 * dims, width), bf16)
    near_grad, away_grad, negative_grad, *found = call(
        functools.partial(edge_kernel, n),
        "edge_kernel",
        [pair_out, pair_out, ((team, 2 * count, dims), bf16)]
        + [sums] * (n - 1)
        + [((chunk, dims), f32)] * chips
        + [((chips * chunk, dims), f32)],
        [pltpu.VMEM((count, dims), bf16), pltpu.VMEM((dims, count), bf16), pltpu.VMEM((count, dims), f32)]
        + [pltpu.VMEM((-(-relations.shape[0] // 16) * 16, dims), f32), pltpu.VMEM((rel_rows, dims), f32)],
        3 * n * rows + 3 * count + 2 * rel_rows,
        (codes, plan),
        (step_ids, negative_ids, near_rows, operator, *near_slab, *away_slab),
    )
    away_other, relation_part = found[: n - 1], found[n - 1 :]

    def scatter(name, row, start, parts, first, plan, grads):
        return call(
            functools.partial(scatter_kernel, row, start, first),
            name,
            [sums] * parts,
            [],
            0,
            (plan,),
            (step_ids, negative_ids, grads, negative_grad),
        )

    scale = 2.0 ** -(math.ceil(math.log2(team * slots * 24 / 65504.0)) + 1)

    def narrow(x):
        return (x * scale).astype(jnp.float16)

    def widen(x):
        return x.astype(f32) * (1.0 / scale)

    def to_chip(x, k):
        return to_peer(x, k // n * 2, k % n)

    other_core = exchange(relation_part[chips], "dom", 1)
    partial = [relation_part[k] + other_core[k * chunk : (k + 1) * chunk] for k in range(chips)]
    away_other = [narrow(x) for x in away_other]
    partial, plan, away_other = lax.optimization_barrier((partial, plan, away_other))
    chunk_total = partial[0]
    for k in range(1, chips):
        chunk_total = chunk_total + to_chip(partial[k], k)
    away_received = [widen(exchange(away_other[k - 1], "sub", k)) for k in range(1, n)]
    (away_total,) = scatter("away_kernel", 1, 0, 1, 0, plan, away_grad)
    chunk_total, away_total, plan = lax.optimization_barrier((chunk_total, away_total, plan))
    masks = [4 << k for k in range((n_dom // 4).bit_length() - 1)]
    for mask in masks[:-1]:
        chunk_total = chunk_total + exchange(chunk_total, "dom", mask)
    near_other = scatter("own_other_kernel", 0, rows, n - 1, n, plan, near_grad)
    near_other = [narrow(x) for x in near_other]
    for x in away_received:
        away_total = away_total + x
    away_total = narrow(away_total)
    chunk_total, away_total, near_other, plan = lax.optimization_barrier((chunk_total, away_total, near_other, plan))
    near_received = [widen(exchange(near_other[k - 1], "sub", k)) for k in range(1, n)]
    for mask in masks[-1:]:
        chunk_total = chunk_total + exchange(chunk_total, "dom", mask)
    chunk_total, away_total, plan = lax.optimization_barrier((chunk_total, away_total, plan))
    returned = exchange(away_total, "dom", pair)
    mine = jnp.concatenate([chunk_total] + [to_chip(chunk_total, k) for k in range(1, chips)], axis=0)
    (near_sum,) = scatter("own_kernel", 0, 0, 1, n, plan, near_grad)
    returned, mine, near_sum = lax.optimization_barrier((returned, mine, near_sum))
    theirs = exchange(mine, "dom", 1)
    (new_relations,) = call(
        functools.partial(relation_kernel, chunk),
        "relation_kernel",
        [(relations.shape, f32)],
        [pltpu.VMEM((rel_rows, dims), f32), pltpu.VMEM((128, rel_rows), f32)],
        0,
        (codes,),
        (relations, relation_state.reshape(1, -1), mine, theirs),
        held=False,
    )
    returned = widen(returned)
    for x in near_received:
        returned = returned + x
    new_table, new_state = call(
        entity_kernel,
        "entity_kernel",
        [((rows, dims), f32), ((1, rows), f32)],
        [],
        1,
        (),
        (entity_table, entity_state.reshape(1, rows), returned, near_sum),
        held=False,
    )
    return (new_table, new_state.reshape(rows), new_relations)


def solution(mesh):
    in_specs = (
        P(("dom", "sub"), None),
        P(("dom", "sub")),
        P(),
        P(),
        P("dom", "sub", None),
        P("dom", "sub", None),
        P("dom", "sub", None),
        P("dom", "sub", None),
        P("dom", "sub"),
    )
    out_specs = (P(("dom", "sub"), None), P(("dom", "sub")), P())
    return jax.shard_map(
        on_device, mesh=mesh, in_specs=in_specs, out_specs=out_specs, check_vma=False
    )
```

```python
import functools
import math

import jax
import jax.numpy as jnp
from jax import lax
from jax.experimental import pallas as pl
from jax.experimental.pallas import tpu as pltpu
from jax.sharding import PartitionSpec as P

learn_rate = 0.1
bf16 = jnp.bfloat16
f32 = jnp.float32
i32 = jnp.int32
params = pltpu.CompilerParams(vmem_limit_bytes=10 * 2**20)


def dot(a, b):
    return jnp.dot(a, b, preferred_element_type=f32)


def dot_nt(a, b):
    return lax.dot_general(a, b, (((1,), (1,)), ((), ())), preferred_element_type=f32)


def one_hot(ids, rows):
    places = lax.broadcasted_iota(jnp.int16, (rows, ids.shape[1]), 0)
    return jnp.where(places == ids.astype(jnp.int16), jnp.ones((), bf16), jnp.zeros((), bf16))


def split(x):
    high = x.astype(bf16)
    return jnp.concatenate([high, (x - high.astype(f32)).astype(bf16)], axis=0)


def gather(pieces, hot):
    rows = pieces[0].shape[1]
    total = dot(pieces[0][...], hot[:rows])
    for k in range(1, len(pieces)):
        total = total + dot(pieces[k][...], hot[k * rows : (k + 1) * rows])
    return total


def scatter_add(pieces, hot, pair):
    dims = pair.shape[0] // 2
    start = 0
    for piece in pieces:
        part = hot[start : start + piece.shape[0]]
        piece[...] += dot_nt(part, pair[:dims]) + dot_nt(part, pair[dims:])
        start += piece.shape[0]


def add_negatives(pieces, hot, pair):
    count = pair.shape[0] // 2
    start = 0
    for piece in pieces:
        part = hot[start : start + piece.shape[0]]
        piece[...] += dot(part, pair[:count]) + dot(part, pair[count:])
        start += piece.shape[0]


def rows_kernel(table, out, *parts):
    out[...] = table[...].T.astype(bf16)
    each = parts[0].shape[1]
    for k, part in enumerate(parts):
        part[...] = out[:, k * each : (k + 1) * each]


def ids_kernel(count, heads, tails, kinds, negatives, ids_out):
    blocks, _, width = ids_out.shape
    for j in range(blocks - 1):
        at = slice(j * width, (j + 1) * width)
        block = jnp.concatenate([heads[:, at], tails[:, at], kinds[:, at]], axis=0)
        ids_out[j] = block.astype(jnp.int16)
    last = jnp.concatenate([negatives[...], jnp.full((2, width), count[0, 0], i32)], axis=0)
    ids_out[blocks - 1] = last.astype(jnp.int16)


def plan_kernel(n, codes, *refs):
    sources, (plan, step_ids, negative_ids) = refs[:-3], refs[-3:]
    team = len(sources)
    most, _, width = step_ids.shape
    me = codes[0]
    counts, blocks = [], []
    for k, ids in enumerate(sources):
        last = ids[most].astype(i32)
        counts.append(jnp.max(last[1:2]))
        blocks.append(lax.div(counts[k] + (width - 1), i32(width)))
        negative_ids[k] = last[0:1] ^ codes[1]
    total = sum(blocks)
    low = lax.div(me * total, i32(team))
    high = lax.div((me + 1) * total, i32(team))
    plan[2 * most] = high - low
    before = []
    for k in range(team):
        ahead = [jnp.where((me ^ j) < (me ^ k), blocks[j], 0) for j in range(team) if j != k]
        before.append(sum(ahead))
        seen = (before[k] < high) & (before[k] + blocks[k] > low)
        plan[2 * most + 1 + k] = seen.astype(i32)

    def one_step(i, carry):
        line = jnp.minimum(low + i, high - 1)
        for k, ids in enumerate(sources):

            @pl.when((line >= before[k]) & (line < before[k] + blocks[k]))
            def _(k=k, ids=ids):
                nth = line - before[k]
                plan[i] = k
                plan[most + i] = jnp.clip(counts[k] - nth * width, 0, width)
                entries = ids[nth].astype(i32)
                near, away = (0, 1) if k < n else (1, 0)
                step_ids[i, 0:1] = entries[near : near + 1] ^ codes[1]
                step_ids[i, 1:2] = entries[away : away + 1] ^ codes[1]
                step_ids[i, 2:3] = entries[2:3]

        return carry

    lax.fori_loop(0, high - low, one_step, 0)


def near_kernel(plan, ids, relations, *refs):
    slab, (rows_out, operator_out, rel_full, rel_split) = refs[:-4], refs[-4:]
    dims = relations.shape[1]
    n, rows = len(slab), slab[0].shape[1]
    rel_full[...] = jnp.zeros_like(rel_full)
    rel_full[: relations.shape[0], :] = relations[...]
    rel_split[...] = split(rel_full[...].T)

    def one_block(i):
        entries = ids[i]
        rows_out[i] = gather(slab, one_hot(entries[0:1], n * rows)).astype(bf16)
        both = dot(rel_split[...], one_hot(entries[2:3], rel_full.shape[0]))
        operator_out[i] = both[:dims] + both[dims:]

    steps = plan[2 * ids.shape[0]]

    def two_blocks(i, carry):
        one_block(2 * i)
        one_block(2 * i + 1)
        return carry

    lax.fori_loop(0, steps >> 1, two_blocks, 0)
    pl.when((steps & 1) == 1)(lambda: one_block(steps - 1))


def edge_kernel(n, cuts, codes, plan, ids, negative_ids, near_in, operator_in, *refs):
    near, refs = refs[:n], refs[n:]
    pieces, refs = refs[:cuts], refs[cuts:]
    near_grad, away_grad, negative_out = refs[:3]
    away_other = refs[3 : n + 2]
    relation_out = refs[n + 2 : -6]
    table, table_t, negative_grad, relation_sum, ordered, away = refs[-6:]
    each = pieces[0].shape[1]
    for k, piece in enumerate(pieces):
        away[:, k * each : (k + 1) * each] = piece[...]
    most, _, width = ids.shape
    steps = plan[2 * most]
    count = table.shape[0]
    for piece in (*away_other, relation_sum):
        piece[...] = jnp.zeros_like(piece)
    rows = near[0].shape[1]

    def one_block(i, carry):
        here = plan[i]
        swapped = here >= n

        def take_table(slab):
            found = gather(slab, one_hot(negative_ids[here], n * rows))
            table_t[...] = found.astype(bf16)
            table[...] = found.T.astype(bf16)
            negative_grad[...] = jnp.zeros_like(negative_grad)

        fresh = (i == 0) | (plan[jnp.maximum(i - 1, 0)] != here)
        pl.when(fresh & ~swapped)(lambda: take_table([away]))
        pl.when(fresh & swapped)(lambda: take_table(near))

        entries = ids[i]

        def score(swapped):
            alive = (lax.broadcasted_iota(i32, (1, width), 1) < plan[most + i]).astype(f32)
            near_rows = near_in[i].astype(f32)
            away_hot = one_hot(entries[1:2], n * rows)
            away_rows = gather([away], away_hot)
            head, tail = (away_rows, near_rows) if swapped else (near_rows, away_rows)
            operator = operator_in[i]
            query = head * operator
            query_b = query.astype(bf16)
            positive = jnp.sum(query * tail, axis=0, keepdims=True)
            scores = dot(table[...], query_b)
            pos_coef = -jax.nn.sigmoid(-positive) * alive
            neg_coef = (jax.nn.sigmoid(scores) * (alive * (1.0 / count))).astype(bf16)
            query_grad = pos_coef * tail + dot(table_t[...], neg_coef)
            negative_grad[...] += dot_nt(neg_coef, query_b)
            head_pair, tail_pair = split(query_grad * operator), split(pos_coef * query)
            near_pair, away_pair = (tail_pair, head_pair) if swapped else (head_pair, tail_pair)
            near_grad[i] = near_pair
            away_grad[i] = away_pair
            scatter_add(away_other, away_hot[rows:], away_pair)
            scatter_add([relation_sum], one_hot(entries[2:3], relation_sum.shape[0]), split(query_grad * head))

        pl.when(~swapped)(lambda: score(False))
        pl.when(swapped)(lambda: score(True))

        ends = (i == steps - 1) | (plan[jnp.minimum(i + 1, steps - 1)] != here)

        @pl.when(ends)
        def _():
            negative_out[here] = split(negative_grad[...])

        @pl.when(ends & ~swapped)
        def _():
            add_negatives(away_other, one_hot(negative_ids[here] - rows, (n - 1) * rows), negative_out[here])

        return carry

    lax.fori_loop(0, steps, one_block, 0)
    chunk = relation_out[0].shape[0]
    ordered[...] = jnp.zeros_like(ordered)
    ordered[: relation_sum.shape[0], :] = relation_sum[...]
    start = 0
    for piece in relation_out:
        for k in range(0, piece.shape[0], chunk):
            at = pl.multiple_of(codes[2] ^ (start + k), chunk)
            piece[k : k + chunk, :] = ordered[pl.ds(at, chunk), :]
        start += piece.shape[0]


def scatter_kernel(row, start, first, plan, ids, negative_ids, grads, negative_grads, *sums):
    most = ids.shape[0]
    height = sum(piece.shape[0] for piece in sums)
    for piece in sums:
        piece[...] = jnp.zeros_like(piece)

    steps = plan[2 * most]

    def hot_of(i):
        return one_hot(ids[i][row : row + 1] - start, height)

    def two_blocks(i, carry):
        hot = jnp.concatenate([hot_of(2 * i), hot_of(2 * i + 1)], axis=1)
        scatter_add(sums, hot, jnp.concatenate([grads[2 * i], grads[2 * i + 1]], axis=1))
        return carry

    lax.fori_loop(0, steps >> 1, two_blocks, 0)

    @pl.when((steps & 1) == 1)
    def _():
        scatter_add(sums, hot_of(steps - 1), grads[steps - 1])

    for k in range(first, first + negative_ids.shape[0] // 2):

        @pl.when(plan[2 * most + 1 + k] != 0)
        def _(k=k):
            add_negatives(sums, one_hot(negative_ids[k] - start, height), negative_grads[k])


def entity_kernel(table, state, returned, own, new_table, new_state):
    grad = returned[...] + own[...]
    lanes = 128
    before = jnp.broadcast_to(state[...], (lanes, table.shape[0])).T[:, :1]
    after = before + jnp.mean(grad * grad, axis=-1, keepdims=True)
    new_table[...] = table[...] - learn_rate * grad / jnp.sqrt(after)
    new_state[...] = jnp.broadcast_to(after, (table.shape[0], lanes)).T[:1]


def relation_kernel(chunk, codes, relations, state, mine, theirs, out, grad, column):
    chunks = mine.shape[0] // chunk
    for k in range(2 * chunks):
        part = (mine, theirs)[k // chunks]
        start = (k % chunks) * chunk
        grad[pl.ds(pl.multiple_of(codes[2] ^ (k * chunk), chunk), chunk), :] = part[start : start + chunk, :]
    count = relations.shape[0]
    column[...] = jnp.ones_like(column)
    column[:, :count] = jnp.broadcast_to(state[...], (column.shape[0], count))
    g = grad[:count, :]
    total = column[...].T[:count, :1] + jnp.mean(g * g, axis=-1, keepdims=True)
    out[...] = relations[...] - learn_rate * g / jnp.sqrt(total)


def exchange(x, axis, mask):
    return lax.ppermute(x, axis, [(i, i ^ mask) for i in range(lax.axis_size(axis))])


def on_device(
    entity_table,
    entity_state,
    relations,
    relation_state,
    head_rows,
    tail_rows,
    relation_ids,
    negative_rows,
    edge_counts,
):
    n = lax.axis_size("sub")
    n_dom = lax.axis_size("dom")
    me_sub = lax.axis_index("sub")
    me_dom = lax.axis_index("dom")
    pair = n_dom // 2
    team = 2 * n
    rows, dims = entity_table.shape
    slots = head_rows.shape[2]
    count = negative_rows.shape[2]
    width = count
    most = slots // width
    rel_rows = -(-relations.shape[0] // 256) * 256
    chips = 2 * n
    chunk = rel_rows // (2 * chips)
    me = lax.shift_right_logical(me_dom, pair.bit_length() - 1) * n + me_sub
    chunk_code = (me_dom & 1) * chips + ((me_dom >> 1) & 1) * n + me_sub
    codes = jnp.stack([me, me_sub * rows, chunk_code * chunk]).astype(i32)

    in_vmem = pl.BlockSpec(memory_space=pltpu.VMEM)
    in_smem = pl.BlockSpec(memory_space=pltpu.SMEM)

    def call(kernel, name, outs, scratch, unit, scalars, arrays, held=True, fetch=False):
        place = (lambda x, t: pltpu.VMEM(x, t)) if held else jax.ShapeDtypeStruct
        return pl.pallas_call(
            kernel,
            in_specs=[in_smem] * len(scalars) + [in_vmem] * len(arrays),
            out_specs=[in_vmem] * len(outs),
            out_shape=[place(x, t) for x, t in outs],
            scratch_shapes=scratch,
            compiler_params=params,
            cost_estimate=pl.CostEstimate(flops=int(slots * dims * unit), bytes_accessed=rows * dims, transcendentals=0),
            name=name,
        )(*scalars, *(pltpu.with_memory_space_constraint(x, pltpu.HBM if fetch else pltpu.VMEM) for x in arrays))

    (ids,) = call(
        ids_kernel,
        "ids_kernel",
        [((most + 1, 3, width), jnp.int16)],
        [],
        1,
        (edge_counts,),
        (
            head_rows.reshape(1, slots),
            tail_rows.reshape(1, slots),
            relation_ids.reshape(1, slots),
            negative_rows.reshape(1, count),
        ),
        fetch=True,
    )
    ids, table = lax.optimization_barrier((ids, entity_table))
    cuts = 2
    local, *cut = call(
        rows_kernel,
        "rows_kernel",
        [((dims, rows), bf16)] + [((dims, rows // cuts), bf16)] * cuts,
        [],
        1,
        (),
        (table,),
        fetch=True,
    )

    def to_peer(x, across, aside):
        pairs = [(d * n + s, (d ^ across) * n + (s ^ aside)) for d in range(n_dom) for s in range(n)]
        return lax.ppermute(x, ("dom", "sub"), pairs)

    def along_sub(x):
        return [x] + [exchange(x, "sub", k) for k in range(1, n)]

    all_ids = along_sub(ids) + along_sub(exchange(ids, "dom", pair))
    near_slab = along_sub(local)
    away_cut = [exchange(x, "dom", pair) for x in cut]
    forwarded = [along_sub(x) for x in away_cut[:-1]]

    plan, step_ids, negative_ids = pl.pallas_call(
        functools.partial(plan_kernel, n),
        in_specs=[in_smem] + [in_vmem] * team,
        out_specs=[in_smem, in_vmem, in_vmem],
        out_shape=[
            jax.ShapeDtypeStruct((2 * most + 1 + team,), i32),
            pltpu.VMEM((most, 3, width), i32),
            pltpu.VMEM((team, 1, width), i32),
        ],
        compiler_params=params,
        cost_estimate=pl.CostEstimate(flops=32 * slots * dims * rows, bytes_accessed=slots * dims, transcendentals=0),
        name="plan_kernel",
    )(codes, *(pltpu.with_memory_space_constraint(x, pltpu.VMEM) for x in all_ids))

    near_plan, away_cut, forwarded = lax.optimization_barrier((plan, away_cut, forwarded))
    forwarded.append(along_sub(away_cut[-1]))
    away_slab = [forwarded[c][k] for k in range(n) for c in range(cuts)]
    near_rows, operator = call(
        near_kernel,
        "near_kernel",
        [((most, dims, width), bf16), ((most, dims, width), f32)],
        [pltpu.VMEM((rel_rows, dims), f32), pltpu.VMEM((2 * dims, rel_rows), bf16)],
        n * rows + 2 * rel_rows,
        (near_plan,),
        (step_ids, relations, *near_slab),
    )
    sums = ((rows, dims), f32)
    pair_out = ((most, 2 * dims, width), bf16)
    near_grad, away_grad, negative_grad, *found = call(
        functools.partial(edge_kernel, n, n * cuts),
        "edge_kernel",
        [pair_out, pair_out, ((team, 2 * count, dims), bf16)]
        + [sums] * (n - 1)
        + [((chunk, dims), f32)] * chips
        + [((chips * chunk, dims), f32)],
        [pltpu.VMEM((count, dims), bf16), pltpu.VMEM((dims, count), bf16), pltpu.VMEM((count, dims), f32)]
        + [pltpu.VMEM((-(-relations.shape[0] // 16) * 16, dims), f32), pltpu.VMEM((rel_rows, dims), f32)]
        + [pltpu.VMEM((dims, n * rows), bf16)],
        3 * n * rows + 3 * count + 2 * rel_rows,
        (codes, plan),
        (step_ids, negative_ids, near_rows, operator, *near_slab, *away_slab),
    )
    away_other, relation_part = found[: n - 1], found[n - 1 :]

    def scatter(name, row, start, parts, first, plan, grads):
        return call(
            functools.partial(scatter_kernel, row, start, first),
            name,
            [sums] * parts,
            [],
            0,
            (plan,),
            (step_ids, negative_ids, grads, negative_grad),
        )

    scale = 2.0 ** -(math.ceil(math.log2(team * slots * 24 / 65504.0)) + 1)

    def narrow(x):
        return (x * scale).astype(jnp.float16)

    def widen(x):
        return x.astype(f32) * (1.0 / scale)

    def to_chip(x, k):
        return to_peer(x, k // n * 2, k % n)

    other_core = exchange(relation_part[chips], "dom", 1)
    partial = [relation_part[k] + other_core[k * chunk : (k + 1) * chunk] for k in range(chips)]
    away_other = [narrow(x) for x in away_other]
    partial, plan, away_other = lax.optimization_barrier((partial, plan, away_other))
    chunk_total = partial[0]
    for k in range(1, chips):
        chunk_total = chunk_total + to_chip(partial[k], k)
    away_received = [widen(exchange(away_other[k - 1], "sub", k)) for k in range(1, n)]
    (away_total,) = scatter("away_kernel", 1, 0, 1, 0, plan, away_grad)
    chunk_total, away_total, plan = lax.optimization_barrier((chunk_total, away_total, plan))
    terms = [chunk_total] + [exchange(chunk_total, "dom", mask) for mask in range(4, n_dom, 4)]
    near_other = scatter("own_other_kernel", 0, rows, n - 1, n, plan, near_grad)
    near_other = [narrow(x) for x in near_other]
    for x in away_received:
        away_total = away_total + x
    away_total = narrow(away_total)
    while len(terms) > 1:
        terms = [terms[k] + terms[k + 1] for k in range(0, len(terms), 2)]
    chunk_total, away_total, near_other, plan = lax.optimization_barrier((terms[0], away_total, near_other, plan))
    near_received = [widen(exchange(near_other[k - 1], "sub", k)) for k in range(1, n)]
    returned = exchange(away_total, "dom", pair)
    mine = jnp.concatenate([chunk_total] + [to_chip(chunk_total, k) for k in range(1, chips)], axis=0)
    (near_sum,) = scatter("own_kernel", 0, 0, 1, n, plan, near_grad)
    returned, mine, near_sum = lax.optimization_barrier((returned, mine, near_sum))
    theirs = exchange(mine, "dom", 1)
    (new_relations,) = call(
        functools.partial(relation_kernel, chunk),
        "relation_kernel",
        [(relations.shape, f32)],
        [pltpu.VMEM((rel_rows, dims), f32), pltpu.VMEM((128, rel_rows), f32)],
        0,
        (codes,),
        (relations, relation_state.reshape(1, -1), mine, theirs),
        held=False,
    )
    returned = widen(returned)
    for x in near_received:
        returned = returned + x
    new_table, new_state = call(
        entity_kernel,
        "entity_kernel",
        [((rows, dims), f32), ((1, rows), f32)],
        [],
        1,
        (),
        (entity_table, entity_state.reshape(1, rows), returned, near_sum),
        held=False,
    )
    return (new_table, new_state.reshape(rows), new_relations)


def solution(mesh):
    in_specs = (
        P(("dom", "sub"), None),
        P(("dom", "sub")),
        P(),
        P(),
        P("dom", "sub", None),
        P("dom", "sub", None),
        P("dom", "sub", None),
        P("dom", "sub", None),
        P("dom", "sub"),
    )
    out_specs = (P(("dom", "sub"), None), P(("dom", "sub")), P())
    return jax.shard_map(
        on_device, mesh=mesh, in_specs=in_specs, out_specs=out_specs, check_vma=False
    )
```

```python
import functools
import math

import jax
import jax.numpy as jnp
from jax import lax
from jax.experimental import pallas as pl
from jax.experimental.pallas import tpu as pltpu
from jax.sharding import PartitionSpec as P

learn_rate = 0.1
bf16 = jnp.bfloat16
f32 = jnp.float32
i32 = jnp.int32
params = pltpu.CompilerParams(vmem_limit_bytes=10 * 2**20)


def dot(a, b):
    return jnp.dot(a, b, preferred_element_type=f32)


def dot_nt(a, b):
    return lax.dot_general(a, b, (((1,), (1,)), ((), ())), preferred_element_type=f32)


def one_hot(ids, rows):
    places = lax.broadcasted_iota(jnp.int16, (rows, ids.shape[1]), 0)
    return jnp.where(places == ids.astype(jnp.int16), jnp.ones((), bf16), jnp.zeros((), bf16))


def split(x):
    high = x.astype(bf16)
    return jnp.concatenate([high, (x - high.astype(f32)).astype(bf16)], axis=0)


def gather(pieces, hot):
    rows = pieces[0].shape[1]
    total = dot(pieces[0][...], hot[:rows])
    for k in range(1, len(pieces)):
        total = total + dot(pieces[k][...], hot[k * rows : (k + 1) * rows])
    return total


def scatter_add(pieces, hot, pair):
    dims = pair.shape[0] // 2
    start = 0
    for piece in pieces:
        part = hot[start : start + piece.shape[0]]
        piece[...] += dot_nt(part, pair[:dims]) + dot_nt(part, pair[dims:])
        start += piece.shape[0]


def add_negatives(pieces, hot, pair):
    count = pair.shape[0] // 2
    start = 0
    for piece in pieces:
        part = hot[start : start + piece.shape[0]]
        piece[...] += dot(part, pair[:count]) + dot(part, pair[count:])
        start += piece.shape[0]


def rows_kernel(table, out):
    out[...] = table[...].T.astype(bf16)


def ids_kernel(count, heads, tails, kinds, negatives, ids_out):
    blocks, _, width = ids_out.shape
    for j in range(blocks - 1):
        at = slice(j * width, (j + 1) * width)
        block = jnp.concatenate([heads[:, at], tails[:, at], kinds[:, at]], axis=0)
        ids_out[j] = block.astype(jnp.int16)
    last = jnp.concatenate([negatives[...], jnp.full((2, width), count[0, 0], i32)], axis=0)
    ids_out[blocks - 1] = last.astype(jnp.int16)


def plan_kernel(n, codes, *refs):
    sources, (plan, step_ids, negative_ids) = refs[:-3], refs[-3:]
    team = len(sources)
    most, _, width = step_ids.shape
    me = codes[0]
    counts, blocks = [], []
    for k, ids in enumerate(sources):
        last = ids[most].astype(i32)
        counts.append(jnp.max(last[1:2]))
        blocks.append(lax.div(counts[k] + (width - 1), i32(width)))
        negative_ids[k] = last[0:1] ^ codes[1]
    total = sum(blocks)
    low = lax.div(me * total, i32(team))
    high = lax.div((me + 1) * total, i32(team))
    plan[2 * most] = high - low
    before = []
    for k in range(team):
        ahead = [jnp.where((me ^ j) < (me ^ k), blocks[j], 0) for j in range(team) if j != k]
        before.append(sum(ahead))
        seen = (before[k] < high) & (before[k] + blocks[k] > low)
        plan[2 * most + 1 + k] = seen.astype(i32)

    def one_step(i, carry):
        line = jnp.minimum(low + i, high - 1)
        for k, ids in enumerate(sources):

            @pl.when((line >= before[k]) & (line < before[k] + blocks[k]))
            def _(k=k, ids=ids):
                nth = line - before[k]
                plan[i] = k
                plan[most + i] = jnp.clip(counts[k] - nth * width, 0, width)
                entries = ids[nth].astype(i32)
                near, away = (0, 1) if k < n else (1, 0)
                step_ids[i, 0:1] = entries[near : near + 1] ^ codes[1]
                step_ids[i, 1:2] = entries[away : away + 1] ^ codes[1]
                step_ids[i, 2:3] = entries[2:3]

        return carry

    lax.fori_loop(0, high - low, one_step, 0)


def near_kernel(plan, ids, relations, *refs):
    slab, (rows_out, operator_out, rel_full, rel_split) = refs[:-4], refs[-4:]
    dims = relations.shape[1]
    n, rows = len(slab), slab[0].shape[1]
    rel_full[...] = jnp.zeros_like(rel_full)
    rel_full[: relations.shape[0], :] = relations[...]
    rel_split[...] = split(rel_full[...].T)

    def one_block(i):
        entries = ids[i]
        rows_out[i] = gather(slab, one_hot(entries[0:1], n * rows)).astype(bf16)
        both = dot(rel_split[...], one_hot(entries[2:3], rel_full.shape[0]))
        operator_out[i] = both[:dims] + both[dims:]

    steps = plan[2 * ids.shape[0]]

    def two_blocks(i, carry):
        one_block(2 * i)
        one_block(2 * i + 1)
        return carry

    lax.fori_loop(0, steps >> 1, two_blocks, 0)
    pl.when((steps & 1) == 1)(lambda: one_block(steps - 1))


def edge_kernel(n, codes, plan, ids, negative_ids, near_in, operator_in, *refs):
    near, away = refs[:n], refs[n : 2 * n]
    near_grad, away_grad, negative_out = refs[2 * n : 2 * n + 3]
    away_other = refs[2 * n + 3 : 3 * n + 2]
    relation_out = refs[3 * n + 2 : -5]
    table, table_t, negative_grad, relation_sum, ordered = refs[-5:]
    most, _, width = ids.shape
    steps = plan[2 * most]
    count = table.shape[0]
    for piece in (*away_other, relation_sum):
        piece[...] = jnp.zeros_like(piece)
    rows = away[0].shape[1]

    def one_block(i, carry):
        here = plan[i]
        swapped = here >= n

        def take_table(slab):
            found = gather(slab, one_hot(negative_ids[here], n * rows))
            table_t[...] = found.astype(bf16)
            table[...] = found.T.astype(bf16)
            negative_grad[...] = jnp.zeros_like(negative_grad)

        fresh = (i == 0) | (plan[jnp.maximum(i - 1, 0)] != here)
        pl.when(fresh & ~swapped)(lambda: take_table(away))
        pl.when(fresh & swapped)(lambda: take_table(near))

        entries = ids[i]

        def score(swapped):
            alive = (lax.broadcasted_iota(i32, (1, width), 1) < plan[most + i]).astype(f32)
            near_rows = near_in[i].astype(f32)
            away_hot = one_hot(entries[1:2], n * rows)
            away_rows = gather(away, away_hot)
            head, tail = (away_rows, near_rows) if swapped else (near_rows, away_rows)
            operator = operator_in[i]
            query = head * operator
            query_b = query.astype(bf16)
            positive = jnp.sum(query * tail, axis=0, keepdims=True)
            scores = dot(table[...], query_b)
            pos_coef = -jax.nn.sigmoid(-positive) * alive
            neg_coef = (jax.nn.sigmoid(scores) * (alive * (1.0 / count))).astype(bf16)
            query_grad = pos_coef * tail + dot(table_t[...], neg_coef)
            negative_grad[...] += dot_nt(neg_coef, query_b)
            head_pair, tail_pair = split(query_grad * operator), split(pos_coef * query)
            near_pair, away_pair = (tail_pair, head_pair) if swapped else (head_pair, tail_pair)
            near_grad[i] = near_pair
            away_grad[i] = away_pair
            scatter_add(away_other, away_hot[rows:], away_pair)
            scatter_add([relation_sum], one_hot(entries[2:3], relation_sum.shape[0]), split(query_grad * head))

        pl.when(~swapped)(lambda: score(False))
        pl.when(swapped)(lambda: score(True))

        ends = (i == steps - 1) | (plan[jnp.minimum(i + 1, steps - 1)] != here)

        @pl.when(ends)
        def _():
            negative_out[here] = split(negative_grad[...])

        @pl.when(ends & ~swapped)
        def _():
            add_negatives(away_other, one_hot(negative_ids[here] - rows, (n - 1) * rows), negative_out[here])

        return carry

    lax.fori_loop(0, steps, one_block, 0)
    chunk = relation_out[0].shape[0]
    ordered[...] = jnp.zeros_like(ordered)
    ordered[: relation_sum.shape[0], :] = relation_sum[...]
    start = 0
    for piece in relation_out:
        for k in range(0, piece.shape[0], chunk):
            at = pl.multiple_of(codes[2] ^ (start + k), chunk)
            piece[k : k + chunk, :] = ordered[pl.ds(at, chunk), :]
        start += piece.shape[0]


def scatter_kernel(row, start, first, plan, ids, negative_ids, grads, negative_grads, *sums):
    most = ids.shape[0]
    height = sum(piece.shape[0] for piece in sums)
    for piece in sums:
        piece[...] = jnp.zeros_like(piece)

    steps = plan[2 * most]

    def hot_of(i):
        return one_hot(ids[i][row : row + 1] - start, height)

    def two_blocks(i, carry):
        hot = jnp.concatenate([hot_of(2 * i), hot_of(2 * i + 1)], axis=1)
        scatter_add(sums, hot, jnp.concatenate([grads[2 * i], grads[2 * i + 1]], axis=1))
        return carry

    lax.fori_loop(0, steps >> 1, two_blocks, 0)

    @pl.when((steps & 1) == 1)
    def _():
        scatter_add(sums, hot_of(steps - 1), grads[steps - 1])

    for k in range(first, first + negative_ids.shape[0] // 2):

        @pl.when(plan[2 * most + 1 + k] != 0)
        def _(k=k):
            add_negatives(sums, one_hot(negative_ids[k] - start, height), negative_grads[k])


def entity_kernel(table, state, returned, own, new_table, new_state):
    grad = returned[...] + own[...]
    lanes = 128
    before = jnp.broadcast_to(state[...], (lanes, table.shape[0])).T[:, :1]
    after = before + jnp.mean(grad * grad, axis=-1, keepdims=True)
    new_table[...] = table[...] - learn_rate * grad / jnp.sqrt(after)
    new_state[...] = jnp.broadcast_to(after, (table.shape[0], lanes)).T[:1]


def relation_kernel(chunk, codes, relations, state, mine, theirs, out, grad, column):
    chunks = mine.shape[0] // chunk
    for k in range(2 * chunks):
        part = (mine, theirs)[k // chunks]
        start = (k % chunks) * chunk
        grad[pl.ds(pl.multiple_of(codes[2] ^ (k * chunk), chunk), chunk), :] = part[start : start + chunk, :]
    count = relations.shape[0]
    column[...] = jnp.ones_like(column)
    column[:, :count] = jnp.broadcast_to(state[...], (column.shape[0], count))
    g = grad[:count, :]
    total = column[...].T[:count, :1] + jnp.mean(g * g, axis=-1, keepdims=True)
    out[...] = relations[...] - learn_rate * g / jnp.sqrt(total)


def exchange(x, axis, mask):
    return lax.ppermute(x, axis, [(i, i ^ mask) for i in range(lax.axis_size(axis))])


def on_device(
    entity_table,
    entity_state,
    relations,
    relation_state,
    head_rows,
    tail_rows,
    relation_ids,
    negative_rows,
    edge_counts,
):
    n = lax.axis_size("sub")
    n_dom = lax.axis_size("dom")
    me_sub = lax.axis_index("sub")
    me_dom = lax.axis_index("dom")
    pair = n_dom // 2
    team = 2 * n
    rows, dims = entity_table.shape
    slots = head_rows.shape[2]
    count = negative_rows.shape[2]
    width = count
    most = slots // width
    rel_rows = -(-relations.shape[0] // 256) * 256
    chips = 2 * n
    chunk = rel_rows // (2 * chips)
    me = lax.shift_right_logical(me_dom, pair.bit_length() - 1) * n + me_sub
    chunk_code = (me_dom & 1) * chips + ((me_dom >> 1) & 1) * n + me_sub
    codes = jnp.stack([me, me_sub * rows, chunk_code * chunk]).astype(i32)

    in_vmem = pl.BlockSpec(memory_space=pltpu.VMEM)
    in_smem = pl.BlockSpec(memory_space=pltpu.SMEM)

    def call(kernel, name, outs, scratch, unit, scalars, arrays, held=True, fetch=False):
        place = (lambda x, t: pltpu.VMEM(x, t)) if held else jax.ShapeDtypeStruct
        return pl.pallas_call(
            kernel,
            in_specs=[in_smem] * len(scalars) + [in_vmem] * len(arrays),
            out_specs=[in_vmem] * len(outs),
            out_shape=[place(x, t) for x, t in outs],
            scratch_shapes=scratch,
            compiler_params=params,
            cost_estimate=pl.CostEstimate(flops=int(slots * dims * unit), bytes_accessed=rows * dims, transcendentals=0),
            name=name,
        )(*scalars, *(pltpu.with_memory_space_constraint(x, pltpu.HBM if fetch else pltpu.VMEM) for x in arrays))

    (ids,) = call(
        ids_kernel,
        "ids_kernel",
        [((most + 1, 3, width), jnp.int16)],
        [],
        1,
        (edge_counts,),
        (
            head_rows.reshape(1, slots),
            tail_rows.reshape(1, slots),
            relation_ids.reshape(1, slots),
            negative_rows.reshape(1, count),
        ),
        fetch=True,
    )
    ids, table = lax.optimization_barrier((ids, entity_table))
    (local,) = call(rows_kernel, "rows_kernel", [((dims, rows), bf16)], [], 1, (), (table,), fetch=True)

    def to_peer(x, across, aside):
        pairs = [(d * n + s, (d ^ across) * n + (s ^ aside)) for d in range(n_dom) for s in range(n)]
        return lax.ppermute(x, ("dom", "sub"), pairs)

    def along_sub(x):
        return [x] + [exchange(x, "sub", k) for k in range(1, n)]

    all_ids = along_sub(ids) + along_sub(exchange(ids, "dom", pair))
    near_slab = along_sub(local)
    away_first = exchange(local, "dom", pair)

    plan, step_ids, negative_ids = pl.pallas_call(
        functools.partial(plan_kernel, n),
        in_specs=[in_smem] + [in_vmem] * team,
        out_specs=[in_smem, in_vmem, in_vmem],
        out_shape=[
            jax.ShapeDtypeStruct((2 * most + 1 + team,), i32),
            pltpu.VMEM((most, 3, width), i32),
            pltpu.VMEM((team, 1, width), i32),
        ],
        compiler_params=params,
        cost_estimate=pl.CostEstimate(flops=32 * slots * dims * rows, bytes_accessed=slots * dims, transcendentals=0),
        name="plan_kernel",
    )(codes, *(pltpu.with_memory_space_constraint(x, pltpu.VMEM) for x in all_ids))

    near_plan, away_first = lax.optimization_barrier((plan, away_first))
    away_slab = along_sub(away_first)
    near_rows, operator = call(
        near_kernel,
        "near_kernel",
        [((most, dims, width), bf16), ((most, dims, width), f32)],
        [pltpu.VMEM((rel_rows, dims), f32), pltpu.VMEM((2 * dims, rel_rows), bf16)],
        n * rows + 2 * rel_rows,
        (near_plan,),
        (step_ids, relations, *near_slab),
    )
    sums = ((rows, dims), f32)
    pair_out = ((most, 2 * dims, width), bf16)
    near_grad, away_grad, negative_grad, *found = call(
        functools.partial(edge_kernel, n),
        "edge_kernel",
        [pair_out, pair_out, ((team, 2 * count, dims), bf16)]
        + [sums] * (n - 1)
        + [((chunk, dims), f32)] * chips
        + [((chips * chunk, dims), f32)],
        [pltpu.VMEM((count, dims), bf16), pltpu.VMEM((dims, count), bf16), pltpu.VMEM((count, dims), f32)]
        + [pltpu.VMEM((-(-relations.shape[0] // 16) * 16, dims), f32), pltpu.VMEM((rel_rows, dims), f32)],
        3 * n * rows + 3 * count + 2 * rel_rows,
        (codes, plan),
        (step_ids, negative_ids, near_rows, operator, *near_slab, *away_slab),
    )
    away_other, relation_part = found[: n - 1], found[n - 1 :]

    def scatter(name, row, start, parts, first, plan, grads):
        return call(
            functools.partial(scatter_kernel, row, start, first),
            name,
            [sums] * parts,
            [],
            0,
            (plan,),
            (step_ids, negative_ids, grads, negative_grad),
        )

    scale = 2.0 ** -(math.ceil(math.log2(team * slots * 24 / 65504.0)) + 1)

    def narrow(x):
        return (x * scale).astype(jnp.float16)

    def widen(x):
        return x.astype(f32) * (1.0 / scale)

    def to_chip(x, k):
        return to_peer(x, k // n * 2, k % n)

    other_core = exchange(relation_part[chips], "dom", 1)
    partial = [relation_part[k] + other_core[k * chunk : (k + 1) * chunk] for k in range(chips)]
    away_other = [narrow(x) for x in away_other]
    away_received = [widen(exchange(away_other[k - 1], "sub", k)) for k in range(1, n)]
    partial, plan = lax.optimization_barrier((partial, plan))
    chunk_total = partial[0]
    for k in range(1, chips):
        chunk_total = chunk_total + to_chip(partial[k], k)
    (away_total,) = scatter("away_kernel", 1, 0, 1, 0, plan, away_grad)
    for x in away_received:
        away_total = away_total + x
    away_total = narrow(away_total)
    chunk_total, away_total, plan = lax.optimization_barrier((chunk_total, away_total, plan))
    terms = [chunk_total] + [exchange(chunk_total, "dom", mask) for mask in range(4, n_dom, 4)]
    returned = exchange(away_total, "dom", pair)
    near_other = scatter("own_other_kernel", 0, rows, n - 1, n, plan, near_grad)
    near_other = [narrow(x) for x in near_other]
    while len(terms) > 1:
        terms = [terms[k] + terms[k + 1] for k in range(0, len(terms), 2)]
    chunk_total, near_other, plan = lax.optimization_barrier((terms[0], near_other, plan))
    near_received = [widen(exchange(near_other[k - 1], "sub", k)) for k in range(1, n)]
    mine = jnp.concatenate([chunk_total] + [to_chip(chunk_total, k) for k in range(1, chips)], axis=0)
    (near_sum,) = scatter("own_kernel", 0, 0, 1, n, plan, near_grad)
    returned, mine, near_sum = lax.optimization_barrier((returned, mine, near_sum))
    theirs = exchange(mine, "dom", 1)
    (new_relations,) = call(
        functools.partial(relation_kernel, chunk),
        "relation_kernel",
        [(relations.shape, f32)],
        [pltpu.VMEM((rel_rows, dims), f32), pltpu.VMEM((128, rel_rows), f32)],
        0,
        (codes,),
        (relations, relation_state.reshape(1, -1), mine, theirs),
        held=False,
    )
    returned = widen(returned)
    for x in near_received:
        returned = returned + x
    new_table, new_state = call(
        entity_kernel,
        "entity_kernel",
        [((rows, dims), f32), ((1, rows), f32)],
        [],
        1,
        (),
        (entity_table, entity_state.reshape(1, rows), returned, near_sum),
        held=False,
    )
    return (new_table, new_state.reshape(rows), new_relations)


def solution(mesh):
    in_specs = (
        P(("dom", "sub"), None),
        P(("dom", "sub")),
        P(),
        P(),
        P("dom", "sub", None),
        P("dom", "sub", None),
        P("dom", "sub", None),
        P("dom", "sub", None),
        P("dom", "sub"),
    )
    out_specs = (P(("dom", "sub"), None), P(("dom", "sub")), P())
    return jax.shard_map(
        on_device, mesh=mesh, in_specs=in_specs, out_specs=out_specs, check_vma=False
    )
```

```python
import functools
import math

import jax
import jax.numpy as jnp
from jax import lax
from jax.experimental import pallas as pl
from jax.experimental.pallas import tpu as pltpu
from jax.sharding import PartitionSpec as P

learn_rate = 0.1
bf16 = jnp.bfloat16
f32 = jnp.float32
i32 = jnp.int32
params = pltpu.CompilerParams(vmem_limit_bytes=10 * 2**20)


def dot(a, b):
    return jnp.dot(a, b, preferred_element_type=f32)


def dot_nt(a, b):
    return lax.dot_general(a, b, (((1,), (1,)), ((), ())), preferred_element_type=f32)


def one_hot(ids, rows):
    places = lax.broadcasted_iota(jnp.int16, (rows, ids.shape[1]), 0)
    return jnp.where(places == ids.astype(jnp.int16), jnp.ones((), bf16), jnp.zeros((), bf16))


def split(x):
    high = x.astype(bf16)
    return jnp.concatenate([high, (x - high.astype(f32)).astype(bf16)], axis=0)


def gather(pieces, hot):
    rows = pieces[0].shape[1]
    total = dot(pieces[0][...], hot[:rows])
    for k in range(1, len(pieces)):
        total = total + dot(pieces[k][...], hot[k * rows : (k + 1) * rows])
    return total


def scatter_add(pieces, hot, pair):
    dims = pair.shape[0] // 2
    start = 0
    for piece in pieces:
        part = hot[start : start + piece.shape[0]]
        piece[...] += dot_nt(part, pair[:dims]) + dot_nt(part, pair[dims:])
        start += piece.shape[0]


def add_negatives(pieces, hot, pair):
    count = pair.shape[0] // 2
    start = 0
    for piece in pieces:
        part = hot[start : start + piece.shape[0]]
        piece[...] += dot(part, pair[:count]) + dot(part, pair[count:])
        start += piece.shape[0]


def rows_kernel(table, out):
    out[...] = table[...].T.astype(bf16)


def ids_kernel(count, heads, tails, kinds, negatives, ids_out):
    blocks, _, width = ids_out.shape
    for j in range(blocks - 1):
        at = slice(j * width, (j + 1) * width)
        block = jnp.concatenate([heads[:, at], tails[:, at], kinds[:, at]], axis=0)
        ids_out[j] = block.astype(jnp.int16)
    last = jnp.concatenate([negatives[...], jnp.full((2, width), count[0, 0], i32)], axis=0)
    ids_out[blocks - 1] = last.astype(jnp.int16)


def plan_kernel(n, codes, *refs):
    sources, (plan, step_ids, negative_ids) = refs[:-3], refs[-3:]
    team = len(sources)
    most, _, width = step_ids.shape
    me = codes[0]
    counts, blocks = [], []
    for k, ids in enumerate(sources):
        last = ids[most].astype(i32)
        counts.append(jnp.max(last[1:2]))
        blocks.append(lax.div(counts[k] + (width - 1), i32(width)))
        negative_ids[k] = last[0:1] ^ codes[1]
    total = sum(blocks)
    low = lax.div(me * total, i32(team))
    high = lax.div((me + 1) * total, i32(team))
    plan[2 * most] = high - low
    before = []
    for k in range(team):
        ahead = [jnp.where((me ^ j) < (me ^ k), blocks[j], 0) for j in range(team) if j != k]
        before.append(sum(ahead))
        seen = (before[k] < high) & (before[k] + blocks[k] > low)
        plan[2 * most + 1 + k] = seen.astype(i32)

    def one_step(i, carry):
        line = jnp.minimum(low + i, high - 1)
        for k, ids in enumerate(sources):

            @pl.when((line >= before[k]) & (line < before[k] + blocks[k]))
            def _(k=k, ids=ids):
                nth = line - before[k]
                plan[i] = k
                plan[most + i] = jnp.clip(counts[k] - nth * width, 0, width)
                entries = ids[nth].astype(i32)
                near, away = (0, 1) if k < n else (1, 0)
                step_ids[i, 0:1] = entries[near : near + 1] ^ codes[1]
                step_ids[i, 1:2] = entries[away : away + 1] ^ codes[1]
                step_ids[i, 2:3] = entries[2:3]

        return carry

    lax.fori_loop(0, high - low, one_step, 0)


def near_kernel(plan, ids, relations, *refs):
    slab, (rows_out, operator_out, rel_full, rel_split) = refs[:-4], refs[-4:]
    dims = relations.shape[1]
    n, rows = len(slab), slab[0].shape[1]
    rel_full[...] = jnp.zeros_like(rel_full)
    rel_full[: relations.shape[0], :] = relations[...]
    rel_split[...] = split(rel_full[...].T)

    def one_block(i):
        entries = ids[i]
        rows_out[i] = gather(slab, one_hot(entries[0:1], n * rows)).astype(bf16)
        both = dot(rel_split[...], one_hot(entries[2:3], rel_full.shape[0]))
        operator_out[i] = both[:dims] + both[dims:]

    steps = plan[2 * ids.shape[0]]

    def two_blocks(i, carry):
        one_block(2 * i)
        one_block(2 * i + 1)
        return carry

    lax.fori_loop(0, steps >> 1, two_blocks, 0)
    pl.when((steps & 1) == 1)(lambda: one_block(steps - 1))


def edge_kernel(n, codes, plan, ids, negative_ids, near_in, operator_in, *refs):
    near, away = refs[:n], refs[n : 2 * n]
    near_grad, away_grad, negative_out = refs[2 * n : 2 * n + 3]
    away_other = refs[2 * n + 3 : 3 * n + 2]
    relation_out = refs[3 * n + 2 : -5]
    table, table_t, negative_grad, relation_sum, ordered = refs[-5:]
    most, _, width = ids.shape
    steps = plan[2 * most]
    count = table.shape[0]
    for piece in (*away_other, relation_sum):
        piece[...] = jnp.zeros_like(piece)
    rows = away[0].shape[1]

    def one_block(i, carry):
        here = plan[i]
        swapped = here >= n

        def take_table(slab):
            found = gather(slab, one_hot(negative_ids[here], n * rows))
            table_t[...] = found.astype(bf16)
            table[...] = found.T.astype(bf16)
            negative_grad[...] = jnp.zeros_like(negative_grad)

        fresh = (i == 0) | (plan[jnp.maximum(i - 1, 0)] != here)
        pl.when(fresh & ~swapped)(lambda: take_table(away))
        pl.when(fresh & swapped)(lambda: take_table(near))

        entries = ids[i]

        def score(swapped):
            alive = (lax.broadcasted_iota(i32, (1, width), 1) < plan[most + i]).astype(f32)
            near_rows = near_in[i].astype(f32)
            away_hot = one_hot(entries[1:2], n * rows)
            away_rows = gather(away, away_hot)
            head, tail = (away_rows, near_rows) if swapped else (near_rows, away_rows)
            operator = operator_in[i]
            query = head * operator
            query_b = query.astype(bf16)
            positive = jnp.sum(query * tail, axis=0, keepdims=True)
            scores = dot(table[...], query_b)
            pos_coef = -jax.nn.sigmoid(-positive) * alive
            neg_coef = (jax.nn.sigmoid(scores) * (alive * (1.0 / count))).astype(bf16)
            query_grad = pos_coef * tail + dot(table_t[...], neg_coef)
            negative_grad[...] += dot_nt(neg_coef, query_b)
            head_pair, tail_pair = split(query_grad * operator), split(pos_coef * query)
            near_pair, away_pair = (tail_pair, head_pair) if swapped else (head_pair, tail_pair)
            near_grad[i] = near_pair
            away_grad[i] = away_pair
            scatter_add(away_other, away_hot[rows:], away_pair)
            scatter_add([relation_sum], one_hot(entries[2:3], relation_sum.shape[0]), split(query_grad * head))

        pl.when(~swapped)(lambda: score(False))
        pl.when(swapped)(lambda: score(True))

        ends = (i == steps - 1) | (plan[jnp.minimum(i + 1, steps - 1)] != here)

        @pl.when(ends)
        def _():
            negative_out[here] = split(negative_grad[...])

        @pl.when(ends & ~swapped)
        def _():
            add_negatives(away_other, one_hot(negative_ids[here] - rows, (n - 1) * rows), negative_out[here])

        return carry

    lax.fori_loop(0, steps, one_block, 0)
    chunk = relation_out[0].shape[0]
    ordered[...] = jnp.zeros_like(ordered)
    ordered[: relation_sum.shape[0], :] = relation_sum[...]
    start = 0
    for piece in relation_out:
        for k in range(0, piece.shape[0], chunk):
            at = pl.multiple_of(codes[2] ^ (start + k), chunk)
            piece[k : k + chunk, :] = ordered[pl.ds(at, chunk), :]
        start += piece.shape[0]


def scatter_kernel(row, start, first, plan, ids, negative_ids, grads, negative_grads, *sums):
    most = ids.shape[0]
    height = sum(piece.shape[0] for piece in sums)
    for piece in sums:
        piece[...] = jnp.zeros_like(piece)

    steps = plan[2 * most]

    def hot_of(i):
        return one_hot(ids[i][row : row + 1] - start, height)

    def two_blocks(i, carry):
        hot = jnp.concatenate([hot_of(2 * i), hot_of(2 * i + 1)], axis=1)
        scatter_add(sums, hot, jnp.concatenate([grads[2 * i], grads[2 * i + 1]], axis=1))
        return carry

    lax.fori_loop(0, steps >> 1, two_blocks, 0)

    @pl.when((steps & 1) == 1)
    def _():
        scatter_add(sums, hot_of(steps - 1), grads[steps - 1])

    for k in range(first, first + negative_ids.shape[0] // 2):

        @pl.when(plan[2 * most + 1 + k] != 0)
        def _(k=k):
            add_negatives(sums, one_hot(negative_ids[k] - start, height), negative_grads[k])


def entity_kernel(table, state, returned, own, new_table, new_state):
    grad = returned[...] + own[...]
    lanes = 128
    before = jnp.broadcast_to(state[...], (lanes, table.shape[0])).T[:, :1]
    after = before + jnp.mean(grad * grad, axis=-1, keepdims=True)
    new_table[...] = table[...] - learn_rate * grad / jnp.sqrt(after)
    new_state[...] = jnp.broadcast_to(after, (table.shape[0], lanes)).T[:1]


def relation_kernel(chunk, codes, relations, state, mine, theirs, out, grad, column):
    chunks = mine.shape[0] // chunk
    for k in range(2 * chunks):
        part = (mine, theirs)[k // chunks]
        start = (k % chunks) * chunk
        grad[pl.ds(pl.multiple_of(codes[2] ^ (k * chunk), chunk), chunk), :] = part[start : start + chunk, :]
    count = relations.shape[0]
    column[...] = jnp.ones_like(column)
    column[:, :count] = jnp.broadcast_to(state[...], (column.shape[0], count))
    g = grad[:count, :]
    total = column[...].T[:count, :1] + jnp.mean(g * g, axis=-1, keepdims=True)
    out[...] = relations[...] - learn_rate * g / jnp.sqrt(total)


def exchange(x, axis, mask):
    return lax.ppermute(x, axis, [(i, i ^ mask) for i in range(lax.axis_size(axis))])


def on_device(
    entity_table,
    entity_state,
    relations,
    relation_state,
    head_rows,
    tail_rows,
    relation_ids,
    negative_rows,
    edge_counts,
):
    n = lax.axis_size("sub")
    n_dom = lax.axis_size("dom")
    me_sub = lax.axis_index("sub")
    me_dom = lax.axis_index("dom")
    pair = n_dom // 2
    team = 2 * n
    rows, dims = entity_table.shape
    slots = head_rows.shape[2]
    count = negative_rows.shape[2]
    width = count
    most = slots // width
    rel_rows = -(-relations.shape[0] // 256) * 256
    chips = 2 * n
    chunk = rel_rows // (2 * chips)
    me = lax.shift_right_logical(me_dom, pair.bit_length() - 1) * n + me_sub
    chunk_code = (me_dom & 1) * chips + ((me_dom >> 1) & 1) * n + me_sub
    codes = jnp.stack([me, me_sub * rows, chunk_code * chunk]).astype(i32)

    in_vmem = pl.BlockSpec(memory_space=pltpu.VMEM)
    in_smem = pl.BlockSpec(memory_space=pltpu.SMEM)

    def call(kernel, name, outs, scratch, unit, scalars, arrays, held=True, fetch=False):
        place = (lambda x, t: pltpu.VMEM(x, t)) if held else jax.ShapeDtypeStruct
        return pl.pallas_call(
            kernel,
            in_specs=[in_smem] * len(scalars) + [in_vmem] * len(arrays),
            out_specs=[in_vmem] * len(outs),
            out_shape=[place(x, t) for x, t in outs],
            scratch_shapes=scratch,
            compiler_params=params,
            cost_estimate=pl.CostEstimate(flops=int(slots * dims * unit), bytes_accessed=rows * dims, transcendentals=0),
            name=name,
        )(*scalars, *(pltpu.with_memory_space_constraint(x, pltpu.HBM if fetch else pltpu.VMEM) for x in arrays))

    (ids,) = call(
        ids_kernel,
        "ids_kernel",
        [((most + 1, 3, width), jnp.int16)],
        [],
        1,
        (edge_counts,),
        (
            head_rows.reshape(1, slots),
            tail_rows.reshape(1, slots),
            relation_ids.reshape(1, slots),
            negative_rows.reshape(1, count),
        ),
        fetch=True,
    )
    ids, table = lax.optimization_barrier((ids, entity_table))
    (local,) = call(rows_kernel, "rows_kernel", [((dims, rows), bf16)], [], 1, (), (table,), fetch=True)

    def to_peer(x, across, aside):
        pairs = [(d * n + s, (d ^ across) * n + (s ^ aside)) for d in range(n_dom) for s in range(n)]
        return lax.ppermute(x, ("dom", "sub"), pairs)

    def along_sub(x):
        return [x] + [exchange(x, "sub", k) for k in range(1, n)]

    all_ids = along_sub(ids) + along_sub(exchange(ids, "dom", pair))
    near_slab = along_sub(local)
    away_first = exchange(local, "dom", pair)

    plan, step_ids, negative_ids = pl.pallas_call(
        functools.partial(plan_kernel, n),
        in_specs=[in_smem] + [in_vmem] * team,
        out_specs=[in_smem, in_vmem, in_vmem],
        out_shape=[
            jax.ShapeDtypeStruct((2 * most + 1 + team,), i32),
            pltpu.VMEM((most, 3, width), i32),
            pltpu.VMEM((team, 1, width), i32),
        ],
        compiler_params=params,
        cost_estimate=pl.CostEstimate(flops=32 * slots * dims * rows, bytes_accessed=slots * dims, transcendentals=0),
        name="plan_kernel",
    )(codes, *(pltpu.with_memory_space_constraint(x, pltpu.VMEM) for x in all_ids))

    near_plan, away_first = lax.optimization_barrier((plan, away_first))
    away_slab = along_sub(away_first)
    near_rows, operator = call(
        near_kernel,
        "near_kernel",
        [((most, dims, width), bf16), ((most, dims, width), f32)],
        [pltpu.VMEM((rel_rows, dims), f32), pltpu.VMEM((2 * dims, rel_rows), bf16)],
        n * rows + 2 * rel_rows,
        (near_plan,),
        (step_ids, relations, *near_slab),
    )
    sums = ((rows, dims), f32)
    pair_out = ((most, 2 * dims, width), bf16)
    near_grad, away_grad, negative_grad, *found = call(
        functools.partial(edge_kernel, n),
        "edge_kernel",
        [pair_out, pair_out, ((team, 2 * count, dims), bf16)]
        + [sums] * (n - 1)
        + [((chunk, dims), f32)] * chips
        + [((chips * chunk, dims), f32)],
        [pltpu.VMEM((count, dims), bf16), pltpu.VMEM((dims, count), bf16), pltpu.VMEM((count, dims), f32)]
        + [pltpu.VMEM((-(-relations.shape[0] // 16) * 16, dims), f32), pltpu.VMEM((rel_rows, dims), f32)],
        3 * n * rows + 3 * count + 2 * rel_rows,
        (codes, plan),
        (step_ids, negative_ids, near_rows, operator, *near_slab, *away_slab),
    )
    away_other, relation_part = found[: n - 1], found[n - 1 :]

    def scatter(name, row, start, parts, first, plan, grads):
        return call(
            functools.partial(scatter_kernel, row, start, first),
            name,
            [sums] * parts,
            [],
            0,
            (plan,),
            (step_ids, negative_ids, grads, negative_grad),
        )

    scale = 2.0 ** -(math.ceil(math.log2(team * slots * 24 / 65504.0)) + 1)
    plane_scale = 2.0 ** -(math.ceil(math.log2(2 * chips * slots * 18 / 65504.0)) + 1)

    def narrow(x, scale=scale):
        return (x * scale).astype(jnp.float16)

    def widen(x, scale=scale):
        return x.astype(f32) * (1.0 / scale)

    def to_chip(x, k):
        return to_peer(x, k // n * 2, k % n)

    other_core = exchange(relation_part[chips], "dom", 1)
    partial = [relation_part[k] + other_core[k * chunk : (k + 1) * chunk] for k in range(chips)]
    away_other = [narrow(x) for x in away_other]
    away_received = [widen(exchange(away_other[k - 1], "sub", k)) for k in range(1, n)]
    partial, plan = lax.optimization_barrier((partial, plan))
    chunk_total = partial[0]
    for k in range(1, chips):
        chunk_total = chunk_total + to_chip(partial[k], k)
    (away_total,) = scatter("away_kernel", 1, 0, 1, 0, plan, away_grad)
    for x in away_received:
        away_total = away_total + x
    away_total = narrow(away_total)
    chunk_total = narrow(chunk_total, plane_scale)
    chunk_total, away_total, plan = lax.optimization_barrier((chunk_total, away_total, plan))
    terms = [chunk_total] + [exchange(chunk_total, "dom", mask) for mask in range(4, n_dom, 4)]
    terms = [widen(x, plane_scale) for x in terms]
    returned = exchange(away_total, "dom", pair)
    near_other = scatter("own_other_kernel", 0, rows, n - 1, n, plan, near_grad)
    near_other = [narrow(x) for x in near_other]
    while len(terms) > 1:
        terms = [terms[k] + terms[k + 1] for k in range(0, len(terms), 2)]
    chunk_total, near_other, plan = lax.optimization_barrier((terms[0], near_other, plan))
    near_received = [widen(exchange(near_other[k - 1], "sub", k)) for k in range(1, n)]
    mine = jnp.concatenate([chunk_total] + [to_chip(chunk_total, k) for k in range(1, chips)], axis=0)
    (near_sum,) = scatter("own_kernel", 0, 0, 1, n, plan, near_grad)
    returned, mine, near_sum = lax.optimization_barrier((returned, mine, near_sum))
    theirs = exchange(mine, "dom", 1)
    (new_relations,) = call(
        functools.partial(relation_kernel, chunk),
        "relation_kernel",
        [(relations.shape, f32)],
        [pltpu.VMEM((rel_rows, dims), f32), pltpu.VMEM((128, rel_rows), f32)],
        0,
        (codes,),
        (relations, relation_state.reshape(1, -1), mine, theirs),
        held=False,
    )
    returned = widen(returned)
    for x in near_received:
        returned = returned + x
    new_table, new_state = call(
        entity_kernel,
        "entity_kernel",
        [((rows, dims), f32), ((1, rows), f32)],
        [],
        1,
        (),
        (entity_table, entity_state.reshape(1, rows), returned, near_sum),
        held=False,
    )
    return (new_table, new_state.reshape(rows), new_relations)


def solution(mesh):
    in_specs = (
        P(("dom", "sub"), None),
        P(("dom", "sub")),
        P(),
        P(),
        P("dom", "sub", None),
        P("dom", "sub", None),
        P("dom", "sub", None),
        P("dom", "sub", None),
        P("dom", "sub"),
    )
    out_specs = (P(("dom", "sub"), None), P(("dom", "sub")), P())
    return jax.shard_map(
        on_device, mesh=mesh, in_specs=in_specs, out_specs=out_specs, check_vma=False
    )
```

```python
import functools
import math

import jax
import jax.numpy as jnp
from jax import lax
from jax.experimental import pallas as pl
from jax.experimental.pallas import tpu as pltpu
from jax.sharding import PartitionSpec as P

learn_rate = 0.1
bf16 = jnp.bfloat16
f32 = jnp.float32
i32 = jnp.int32
params = pltpu.CompilerParams(vmem_limit_bytes=10 * 2**20)


def dot(a, b):
    return jnp.dot(a, b, preferred_element_type=f32)


def dot_nt(a, b):
    return lax.dot_general(a, b, (((1,), (1,)), ((), ())), preferred_element_type=f32)


def one_hot(ids, rows):
    places = lax.broadcasted_iota(jnp.int16, (rows, ids.shape[1]), 0)
    return jnp.where(places == ids.astype(jnp.int16), jnp.ones((), bf16), jnp.zeros((), bf16))


def split(x):
    high = x.astype(bf16)
    return jnp.concatenate([high, (x - high.astype(f32)).astype(bf16)], axis=0)


def gather(pieces, hot):
    rows = pieces[0].shape[1]
    total = dot(pieces[0][...], hot[:rows])
    for k in range(1, len(pieces)):
        total = total + dot(pieces[k][...], hot[k * rows : (k + 1) * rows])
    return total


def scatter_add(pieces, hot, pair):
    dims = pair.shape[0] // 2
    start = 0
    for piece in pieces:
        part = hot[start : start + piece.shape[0]]
        piece[...] += dot_nt(part, pair[:dims]) + dot_nt(part, pair[dims:])
        start += piece.shape[0]


def add_negatives(pieces, hot, pair):
    count = pair.shape[0] // 2
    start = 0
    for piece in pieces:
        part = hot[start : start + piece.shape[0]]
        piece[...] += dot(part, pair[:count]) + dot(part, pair[count:])
        start += piece.shape[0]


def rows_kernel(table, out):
    out[...] = table[...].T.astype(bf16)


def ids_kernel(count, heads, tails, kinds, negatives, ids_out):
    blocks, _, width = ids_out.shape
    for j in range(blocks - 1):
        at = slice(j * width, (j + 1) * width)
        block = jnp.concatenate([heads[:, at], tails[:, at], kinds[:, at]], axis=0)
        ids_out[j] = block.astype(jnp.int16)
    last = jnp.concatenate([negatives[...], jnp.full((2, width), count[0, 0], i32)], axis=0)
    ids_out[blocks - 1] = last.astype(jnp.int16)


def plan_kernel(n, codes, *refs):
    sources, (plan, step_ids, negative_ids) = refs[:-3], refs[-3:]
    team = len(sources)
    most, _, width = step_ids.shape
    me = codes[0]
    counts, blocks = [], []
    for k, ids in enumerate(sources):
        last = ids[most].astype(i32)
        counts.append(jnp.max(last[1:2]))
        blocks.append(lax.div(counts[k] + (width - 1), i32(width)))
        negative_ids[k] = last[0:1] ^ codes[1]
    total = sum(blocks)
    low = lax.div(me * total, i32(team))
    high = lax.div((me + 1) * total, i32(team))
    plan[2 * most] = high - low
    before = []
    for k in range(team):
        ahead = [jnp.where((me ^ j) < (me ^ k), blocks[j], 0) for j in range(team) if j != k]
        before.append(sum(ahead))
        seen = (before[k] < high) & (before[k] + blocks[k] > low)
        plan[2 * most + 1 + k] = seen.astype(i32)

    def one_step(i, carry):
        line = jnp.minimum(low + i, high - 1)
        for k, ids in enumerate(sources):

            @pl.when((line >= before[k]) & (line < before[k] + blocks[k]))
            def _(k=k, ids=ids):
                nth = line - before[k]
                plan[i] = k
                plan[most + i] = jnp.clip(counts[k] - nth * width, 0, width)
                entries = ids[nth].astype(i32)
                near, away = (0, 1) if k < n else (1, 0)
                step_ids[i, 0:1] = entries[near : near + 1] ^ codes[1]
                step_ids[i, 1:2] = entries[away : away + 1] ^ codes[1]
                step_ids[i, 2:3] = entries[2:3]

        return carry

    lax.fori_loop(0, high - low, one_step, 0)


def near_kernel(plan, ids, relations, *refs):
    slab, (rows_out, operator_out, rel_full, rel_split) = refs[:-4], refs[-4:]
    dims = relations.shape[1]
    n, rows = len(slab), slab[0].shape[1]
    rel_full[...] = jnp.zeros_like(rel_full)
    rel_full[: relations.shape[0], :] = relations[...]
    rel_split[...] = split(rel_full[...].T)

    def one_block(i):
        entries = ids[i]
        rows_out[i] = gather(slab, one_hot(entries[0:1], n * rows)).astype(bf16)
        both = dot(rel_split[...], one_hot(entries[2:3], rel_full.shape[0]))
        operator_out[i] = both[:dims] + both[dims:]

    steps = plan[2 * ids.shape[0]]

    def two_blocks(i, carry):
        one_block(2 * i)
        one_block(2 * i + 1)
        return carry

    lax.fori_loop(0, steps >> 1, two_blocks, 0)
    pl.when((steps & 1) == 1)(lambda: one_block(steps - 1))


def edge_kernel(n, codes, plan, ids, negative_ids, near_in, operator_in, *refs):
    near, away = refs[:n], refs[n : 2 * n]
    near_grad, away_grad, negative_out = refs[2 * n : 2 * n + 3]
    away_other = refs[2 * n + 3 : 3 * n + 2]
    relation_out = refs[3 * n + 2 : -5]
    table, table_t, negative_grad, relation_sum, ordered = refs[-5:]
    most, _, width = ids.shape
    steps = plan[2 * most]
    count = table.shape[0]
    for piece in (*away_other, relation_sum):
        piece[...] = jnp.zeros_like(piece)
    rows = away[0].shape[1]

    def one_block(i, carry):
        here = plan[i]
        swapped = here >= n

        def take_table(slab):
            found = gather(slab, one_hot(negative_ids[here], n * rows))
            table_t[...] = found.astype(bf16)
            table[...] = found.T.astype(bf16)
            negative_grad[...] = jnp.zeros_like(negative_grad)

        fresh = (i == 0) | (plan[jnp.maximum(i - 1, 0)] != here)
        pl.when(fresh & ~swapped)(lambda: take_table(away))
        pl.when(fresh & swapped)(lambda: take_table(near))

        entries = ids[i]

        def score(swapped):
            alive = (lax.broadcasted_iota(i32, (1, width), 1) < plan[most + i]).astype(f32)
            near_rows = near_in[i].astype(f32)
            away_hot = one_hot(entries[1:2], n * rows)
            away_rows = gather(away, away_hot)
            head, tail = (away_rows, near_rows) if swapped else (near_rows, away_rows)
            operator = operator_in[i]
            query = head * operator
            query_b = query.astype(bf16)
            positive = jnp.sum(query * tail, axis=0, keepdims=True)
            scores = dot(table[...], query_b)
            pos_coef = -jax.nn.sigmoid(-positive) * alive
            neg_coef = (jax.nn.sigmoid(scores) * (alive * (1.0 / count))).astype(bf16)
            query_grad = pos_coef * tail + dot(table_t[...], neg_coef)
            negative_grad[...] += dot_nt(neg_coef, query_b)
            head_pair, tail_pair = split(query_grad * operator), split(pos_coef * query)
            near_pair, away_pair = (tail_pair, head_pair) if swapped else (head_pair, tail_pair)
            near_grad[i] = near_pair
            away_grad[i] = away_pair
            scatter_add(away_other, away_hot[rows:], away_pair)
            scatter_add([relation_sum], one_hot(entries[2:3], relation_sum.shape[0]), split(query_grad * head))

        pl.when(~swapped)(lambda: score(False))
        pl.when(swapped)(lambda: score(True))

        ends = (i == steps - 1) | (plan[jnp.minimum(i + 1, steps - 1)] != here)

        @pl.when(ends)
        def _():
            negative_out[here] = split(negative_grad[...])

        @pl.when(ends & ~swapped)
        def _():
            add_negatives(away_other, one_hot(negative_ids[here] - rows, (n - 1) * rows), negative_out[here])

        return carry

    lax.fori_loop(0, steps, one_block, 0)
    chunk = relation_out[0].shape[0]
    ordered[...] = jnp.zeros_like(ordered)
    ordered[: relation_sum.shape[0], :] = relation_sum[...]
    start = 0
    for piece in relation_out:
        for k in range(0, piece.shape[0], chunk):
            at = pl.multiple_of(codes[2] ^ (start + k), chunk)
            piece[k : k + chunk, :] = ordered[pl.ds(at, chunk), :]
        start += piece.shape[0]


def scatter_kernel(row, start, first, plan, ids, negative_ids, grads, negative_grads, *sums):
    most = ids.shape[0]
    height = sum(piece.shape[0] for piece in sums)
    for piece in sums:
        piece[...] = jnp.zeros_like(piece)

    steps = plan[2 * most]

    def hot_of(i):
        return one_hot(ids[i][row : row + 1] - start, height)

    def two_blocks(i, carry):
        hot = jnp.concatenate([hot_of(2 * i), hot_of(2 * i + 1)], axis=1)
        scatter_add(sums, hot, jnp.concatenate([grads[2 * i], grads[2 * i + 1]], axis=1))
        return carry

    lax.fori_loop(0, steps >> 1, two_blocks, 0)

    @pl.when((steps & 1) == 1)
    def _():
        scatter_add(sums, hot_of(steps - 1), grads[steps - 1])

    for k in range(first, first + negative_ids.shape[0] // 2):

        @pl.when(plan[2 * most + 1 + k] != 0)
        def _(k=k):
            add_negatives(sums, one_hot(negative_ids[k] - start, height), negative_grads[k])


def entity_kernel(table, state, returned, own, new_table, new_state):
    grad = returned[...] + own[...]
    lanes = 128
    before = jnp.broadcast_to(state[...], (lanes, table.shape[0])).T[:, :1]
    after = before + jnp.mean(grad * grad, axis=-1, keepdims=True)
    new_table[...] = table[...] - learn_rate * grad / jnp.sqrt(after)
    new_state[...] = jnp.broadcast_to(after, (table.shape[0], lanes)).T[:1]


def relation_kernel(chunk, codes, relations, state, mine, theirs, out, grad, column):
    chunks = mine.shape[0] // chunk
    for k in range(2 * chunks):
        part = (mine, theirs)[k // chunks]
        start = (k % chunks) * chunk
        grad[pl.ds(pl.multiple_of(codes[2] ^ (k * chunk), chunk), chunk), :] = part[start : start + chunk, :]
    count = relations.shape[0]
    column[...] = jnp.ones_like(column)
    column[:, :count] = jnp.broadcast_to(state[...], (column.shape[0], count))
    g = grad[:count, :]
    total = column[...].T[:count, :1] + jnp.mean(g * g, axis=-1, keepdims=True)
    out[...] = relations[...] - learn_rate * g / jnp.sqrt(total)


def exchange(x, axis, mask):
    return lax.ppermute(x, axis, [(i, i ^ mask) for i in range(lax.axis_size(axis))])


def on_device(
    entity_table,
    entity_state,
    relations,
    relation_state,
    head_rows,
    tail_rows,
    relation_ids,
    negative_rows,
    edge_counts,
):
    n = lax.axis_size("sub")
    n_dom = lax.axis_size("dom")
    me_sub = lax.axis_index("sub")
    me_dom = lax.axis_index("dom")
    pair = n_dom // 2
    team = 2 * n
    rows, dims = entity_table.shape
    slots = head_rows.shape[2]
    count = negative_rows.shape[2]
    width = count
    most = slots // width
    rel_rows = -(-relations.shape[0] // 256) * 256
    chips = 2 * n
    chunk = rel_rows // (2 * chips)
    me = lax.shift_right_logical(me_dom, pair.bit_length() - 1) * n + me_sub
    chunk_code = (me_dom & 1) * chips + ((me_dom >> 1) & 1) * n + me_sub
    codes = jnp.stack([me, me_sub * rows, chunk_code * chunk]).astype(i32)

    in_vmem = pl.BlockSpec(memory_space=pltpu.VMEM)
    in_smem = pl.BlockSpec(memory_space=pltpu.SMEM)

    def call(kernel, name, outs, scratch, unit, scalars, arrays, held=True, fetch=False):
        place = (lambda x, t: pltpu.VMEM(x, t)) if held else jax.ShapeDtypeStruct
        return pl.pallas_call(
            kernel,
            in_specs=[in_smem] * len(scalars) + [in_vmem] * len(arrays),
            out_specs=[in_vmem] * len(outs),
            out_shape=[place(x, t) for x, t in outs],
            scratch_shapes=scratch,
            compiler_params=params,
            cost_estimate=pl.CostEstimate(flops=int(slots * dims * unit), bytes_accessed=rows * dims, transcendentals=0),
            name=name,
        )(*scalars, *(pltpu.with_memory_space_constraint(x, pltpu.HBM if fetch else pltpu.VMEM) for x in arrays))

    (ids,) = call(
        ids_kernel,
        "ids_kernel",
        [((most + 1, 3, width), jnp.int16)],
        [],
        1,
        (edge_counts,),
        (
            head_rows.reshape(1, slots),
            tail_rows.reshape(1, slots),
            relation_ids.reshape(1, slots),
            negative_rows.reshape(1, count),
        ),
        fetch=True,
    )
    ids, table = lax.optimization_barrier((ids, entity_table))
    (local,) = call(rows_kernel, "rows_kernel", [((dims, rows), bf16)], [], 1, (), (table,), fetch=True)

    def to_peer(x, across, aside):
        pairs = [(d * n + s, (d ^ across) * n + (s ^ aside)) for d in range(n_dom) for s in range(n)]
        return lax.ppermute(x, ("dom", "sub"), pairs)

    def along_sub(x):
        return [x] + [exchange(x, "sub", k) for k in range(1, n)]

    all_ids = along_sub(ids) + along_sub(exchange(ids, "dom", pair))
    near_slab = along_sub(local)
    away_first = exchange(local, "dom", pair)

    plan, step_ids, negative_ids = pl.pallas_call(
        functools.partial(plan_kernel, n),
        in_specs=[in_smem] + [in_vmem] * team,
        out_specs=[in_smem, in_vmem, in_vmem],
        out_shape=[
            jax.ShapeDtypeStruct((2 * most + 1 + team,), i32),
            pltpu.VMEM((most, 3, width), i32),
            pltpu.VMEM((team, 1, width), i32),
        ],
        compiler_params=params,
        cost_estimate=pl.CostEstimate(flops=32 * slots * dims * rows, bytes_accessed=slots * dims, transcendentals=0),
        name="plan_kernel",
    )(codes, *(pltpu.with_memory_space_constraint(x, pltpu.VMEM) for x in all_ids))

    near_plan, away_first = lax.optimization_barrier((plan, away_first))
    away_slab = along_sub(away_first)
    near_rows, operator = call(
        near_kernel,
        "near_kernel",
        [((most, dims, width), bf16), ((most, dims, width), f32)],
        [pltpu.VMEM((rel_rows, dims), f32), pltpu.VMEM((2 * dims, rel_rows), bf16)],
        n * rows + 2 * rel_rows,
        (near_plan,),
        (step_ids, relations, *near_slab),
    )
    sums = ((rows, dims), f32)
    pair_out = ((most, 2 * dims, width), bf16)
    near_grad, away_grad, negative_grad, *found = call(
        functools.partial(edge_kernel, n),
        "edge_kernel",
        [pair_out, pair_out, ((team, 2 * count, dims), bf16)]
        + [sums] * (n - 1)
        + [((chunk, dims), f32)] * chips
        + [((chips * chunk, dims), f32)],
        [pltpu.VMEM((count, dims), bf16), pltpu.VMEM((dims, count), bf16), pltpu.VMEM((count, dims), f32)]
        + [pltpu.VMEM((-(-relations.shape[0] // 16) * 16, dims), f32), pltpu.VMEM((rel_rows, dims), f32)],
        3 * n * rows + 3 * count + 2 * rel_rows,
        (codes, plan),
        (step_ids, negative_ids, near_rows, operator, *near_slab, *away_slab),
    )
    away_other, relation_part = found[: n - 1], found[n - 1 :]

    def scatter(name, row, start, parts, first, plan, grads):
        return call(
            functools.partial(scatter_kernel, row, start, first),
            name,
            [sums] * parts,
            [],
            0,
            (plan,),
            (step_ids, negative_ids, grads, negative_grad),
        )

    scale = 2.0 ** -(math.ceil(math.log2(team * slots * 24 / 65504.0)) + 1)
    plane_scale = 2.0 ** -(math.ceil(math.log2(2 * chips * slots * 18 / 65504.0)) + 1)

    def narrow(x, scale=scale):
        return (x * scale).astype(jnp.float16)

    def widen(x, scale=scale):
        return x.astype(f32) * (1.0 / scale)

    def to_chip(x, k):
        return to_peer(x, k // n * 2, k % n)

    other_core = exchange(relation_part[chips], "dom", 1)
    partial = [relation_part[k] + other_core[k * chunk : (k + 1) * chunk] for k in range(chips)]
    away_other = [narrow(x) for x in away_other]
    away_received = [widen(exchange(away_other[k - 1], "sub", k)) for k in range(1, n)]
    partial, plan = lax.optimization_barrier((partial, plan))
    chunk_total = partial[0]
    for k in range(1, chips):
        chunk_total = chunk_total + to_chip(partial[k], k)
    (away_total,) = scatter("away_kernel", 1, 0, 1, 0, plan, away_grad)
    for x in away_received:
        away_total = away_total + x
    away_total = narrow(away_total)
    chunk_total = narrow(chunk_total, plane_scale)
    chunk_total, away_total, plan = lax.optimization_barrier((chunk_total, away_total, plan))
    terms = [chunk_total] + [exchange(chunk_total, "dom", mask) for mask in range(4, n_dom, 4)]
    terms = [widen(x, plane_scale) for x in terms]
    near_other = scatter("own_other_kernel", 0, rows, n - 1, n, plan, near_grad)
    near_other = [narrow(x) for x in near_other]
    while len(terms) > 1:
        terms = [terms[k] + terms[k + 1] for k in range(0, len(terms), 2)]
    chunk_total, away_total, near_other, plan = lax.optimization_barrier((terms[0], away_total, near_other, plan))
    returned = exchange(away_total, "dom", pair)
    near_received = [widen(exchange(near_other[k - 1], "sub", k)) for k in range(1, n)]
    mine = jnp.concatenate([chunk_total] + [to_chip(chunk_total, k) for k in range(1, chips)], axis=0)
    (near_sum,) = scatter("own_kernel", 0, 0, 1, n, plan, near_grad)
    returned, mine, near_sum = lax.optimization_barrier((returned, mine, near_sum))
    theirs = exchange(mine, "dom", 1)
    (new_relations,) = call(
        functools.partial(relation_kernel, chunk),
        "relation_kernel",
        [(relations.shape, f32)],
        [pltpu.VMEM((rel_rows, dims), f32), pltpu.VMEM((128, rel_rows), f32)],
        0,
        (codes,),
        (relations, relation_state.reshape(1, -1), mine, theirs),
        held=False,
    )
    returned = widen(returned)
    for x in near_received:
        returned = returned + x
    new_table, new_state = call(
        entity_kernel,
        "entity_kernel",
        [((rows, dims), f32), ((1, rows), f32)],
        [],
        1,
        (),
        (entity_table, entity_state.reshape(1, rows), returned, near_sum),
        held=False,
    )
    return (new_table, new_state.reshape(rows), new_relations)


def solution(mesh):
    in_specs = (
        P(("dom", "sub"), None),
        P(("dom", "sub")),
        P(),
        P(),
        P("dom", "sub", None),
        P("dom", "sub", None),
        P("dom", "sub", None),
        P("dom", "sub", None),
        P("dom", "sub"),
    )
    out_specs = (P(("dom", "sub"), None), P(("dom", "sub")), P())
    return jax.shard_map(
        on_device, mesh=mesh, in_specs=in_specs, out_specs=out_specs, check_vma=False
    )
```

```python
import functools
import math

import jax
import jax.numpy as jnp
from jax import lax
from jax.experimental import pallas as pl
from jax.experimental.pallas import tpu as pltpu
from jax.sharding import PartitionSpec as P

learn_rate = 0.1
bf16 = jnp.bfloat16
f32 = jnp.float32
i32 = jnp.int32
params = pltpu.CompilerParams(vmem_limit_bytes=10 * 2**20)


def dot(a, b):
    return jnp.dot(a, b, preferred_element_type=f32)


def dot_nt(a, b):
    return lax.dot_general(a, b, (((1,), (1,)), ((), ())), preferred_element_type=f32)


def one_hot(ids, rows):
    places = lax.broadcasted_iota(jnp.int16, (rows, ids.shape[1]), 0)
    return jnp.where(places == ids.astype(jnp.int16), jnp.ones((), bf16), jnp.zeros((), bf16))


def split(x):
    high = x.astype(bf16)
    return jnp.concatenate([high, (x - high.astype(f32)).astype(bf16)], axis=0)


def gather(pieces, hot):
    rows = pieces[0].shape[1]
    total = dot(pieces[0][...], hot[:rows])
    for k in range(1, len(pieces)):
        total = total + dot(pieces[k][...], hot[k * rows : (k + 1) * rows])
    return total


def scatter_add(pieces, hot, pair):
    dims = pair.shape[0] // 2
    start = 0
    for piece in pieces:
        part = hot[start : start + piece.shape[0]]
        piece[...] += dot_nt(part, pair[:dims]) + dot_nt(part, pair[dims:])
        start += piece.shape[0]


def add_negatives(pieces, hot, pair):
    count = pair.shape[0] // 2
    start = 0
    for piece in pieces:
        part = hot[start : start + piece.shape[0]]
        piece[...] += dot(part, pair[:count]) + dot(part, pair[count:])
        start += piece.shape[0]


def rows_kernel(table, out):
    out[...] = table[...].T.astype(bf16)


def ids_kernel(count, heads, tails, kinds, negatives, ids_out):
    blocks, _, width = ids_out.shape
    for j in range(blocks - 1):
        at = slice(j * width, (j + 1) * width)
        block = jnp.concatenate([heads[:, at], tails[:, at], kinds[:, at]], axis=0)
        ids_out[j] = block.astype(jnp.int16)
    last = jnp.concatenate([negatives[...], jnp.full((2, width), count[0, 0], i32)], axis=0)
    ids_out[blocks - 1] = last.astype(jnp.int16)


def plan_kernel(n, codes, *refs):
    sources, (plan, step_ids, negative_ids) = refs[:-3], refs[-3:]
    team = len(sources)
    most, _, width = step_ids.shape
    me = codes[0]
    counts, blocks = [], []
    for k, ids in enumerate(sources):
        last = ids[most].astype(i32)
        counts.append(jnp.max(last[1:2]))
        blocks.append(lax.div(counts[k] + (width - 1), i32(width)))
        negative_ids[k] = last[0:1] ^ codes[1]
    total = sum(blocks)
    low = lax.div(me * total, i32(team))
    high = lax.div((me + 1) * total, i32(team))
    plan[2 * most] = high - low
    before = []
    for k in range(team):
        ahead = [jnp.where((me ^ j) < (me ^ k), blocks[j], 0) for j in range(team) if j != k]
        before.append(sum(ahead))
        seen = (before[k] < high) & (before[k] + blocks[k] > low)
        plan[2 * most + 1 + k] = seen.astype(i32)

    def one_step(i, carry):
        line = jnp.minimum(low + i, high - 1)
        for k, ids in enumerate(sources):

            @pl.when((line >= before[k]) & (line < before[k] + blocks[k]))
            def _(k=k, ids=ids):
                nth = line - before[k]
                plan[i] = k
                plan[most + i] = jnp.clip(counts[k] - nth * width, 0, width)
                entries = ids[nth].astype(i32)
                near, away = (0, 1) if k < n else (1, 0)
                step_ids[i, 0:1] = entries[near : near + 1] ^ codes[1]
                step_ids[i, 1:2] = entries[away : away + 1] ^ codes[1]
                step_ids[i, 2:3] = entries[2:3]

        return carry

    lax.fori_loop(0, high - low, one_step, 0)


def near_kernel(plan, ids, relations, *refs):
    slab, (rows_out, operator_out, rel_full, rel_split) = refs[:-4], refs[-4:]
    dims = relations.shape[1]
    n, rows = len(slab), slab[0].shape[1]
    rel_full[...] = jnp.zeros_like(rel_full)
    rel_full[: relations.shape[0], :] = relations[...]
    rel_split[...] = split(rel_full[...].T)

    def one_block(i):
        entries = ids[i]
        rows_out[i] = gather(slab, one_hot(entries[0:1], n * rows)).astype(bf16)
        both = dot(rel_split[...], one_hot(entries[2:3], rel_full.shape[0]))
        operator_out[i] = both[:dims] + both[dims:]

    steps = plan[2 * ids.shape[0]]

    def two_blocks(i, carry):
        one_block(2 * i)
        one_block(2 * i + 1)
        return carry

    lax.fori_loop(0, steps >> 1, two_blocks, 0)
    pl.when((steps & 1) == 1)(lambda: one_block(steps - 1))


def edge_kernel(n, codes, plan, ids, negative_ids, near_in, operator_in, *refs):
    near, away = refs[:n], refs[n : 2 * n]
    near_grad, away_grad, negative_out = refs[2 * n : 2 * n + 3]
    away_other = refs[2 * n + 3 : 3 * n + 2]
    relation_out = refs[3 * n + 2 : -5]
    table, table_t, negative_grad, relation_sum, ordered = refs[-5:]
    most, _, width = ids.shape
    steps = plan[2 * most]
    count = table.shape[0]
    for piece in (*away_other, relation_sum):
        piece[...] = jnp.zeros_like(piece)
    rows = away[0].shape[1]

    def one_block(i, carry):
        here = plan[i]
        swapped = here >= n

        def take_table(slab):
            found = gather(slab, one_hot(negative_ids[here], n * rows))
            table_t[...] = found.astype(bf16)
            table[...] = found.T.astype(bf16)
            negative_grad[...] = jnp.zeros_like(negative_grad)

        fresh = (i == 0) | (plan[jnp.maximum(i - 1, 0)] != here)
        pl.when(fresh & ~swapped)(lambda: take_table(away))
        pl.when(fresh & swapped)(lambda: take_table(near))

        entries = ids[i]

        def score(swapped):
            alive = (lax.broadcasted_iota(i32, (1, width), 1) < plan[most + i]).astype(f32)
            near_rows = near_in[i].astype(f32)
            away_hot = one_hot(entries[1:2], n * rows)
            away_rows = gather(away, away_hot)
            head, tail = (away_rows, near_rows) if swapped else (near_rows, away_rows)
            operator = operator_in[i]
            query = head * operator
            query_b = query.astype(bf16)
            positive = jnp.sum(query * tail, axis=0, keepdims=True)
            scores = dot(table[...], query_b)
            pos_coef = -jax.nn.sigmoid(-positive) * alive
            neg_coef = (jax.nn.sigmoid(scores) * (alive * (1.0 / count))).astype(bf16)
            query_grad = pos_coef * tail + dot(table_t[...], neg_coef)
            negative_grad[...] += dot_nt(neg_coef, query_b)
            head_pair, tail_pair = split(query_grad * operator), split(pos_coef * query)
            near_pair, away_pair = (tail_pair, head_pair) if swapped else (head_pair, tail_pair)
            near_grad[i] = near_pair
            away_grad[i] = away_pair
            scatter_add(away_other, away_hot[rows:], away_pair)
            scatter_add([relation_sum], one_hot(entries[2:3], relation_sum.shape[0]), split(query_grad * head))

        pl.when(~swapped)(lambda: score(False))
        pl.when(swapped)(lambda: score(True))

        ends = (i == steps - 1) | (plan[jnp.minimum(i + 1, steps - 1)] != here)

        @pl.when(ends)
        def _():
            negative_out[here] = split(negative_grad[...])

        @pl.when(ends & ~swapped)
        def _():
            add_negatives(away_other, one_hot(negative_ids[here] - rows, (n - 1) * rows), negative_out[here])

        return carry

    lax.fori_loop(0, steps, one_block, 0)
    chunk = relation_out[0].shape[0]
    ordered[...] = jnp.zeros_like(ordered)
    ordered[: relation_sum.shape[0], :] = relation_sum[...]
    start = 0
    for piece in relation_out:
        for k in range(0, piece.shape[0], chunk):
            at = pl.multiple_of(codes[2] ^ (start + k), chunk)
            piece[k : k + chunk, :] = ordered[pl.ds(at, chunk), :]
        start += piece.shape[0]


def scatter_kernel(row, start, first, plan, ids, negative_ids, grads, negative_grads, *sums):
    most = ids.shape[0]
    height = sum(piece.shape[0] for piece in sums)
    for piece in sums:
        piece[...] = jnp.zeros_like(piece)

    steps = plan[2 * most]

    def hot_of(i):
        return one_hot(ids[i][row : row + 1] - start, height)

    def two_blocks(i, carry):
        hot = jnp.concatenate([hot_of(2 * i), hot_of(2 * i + 1)], axis=1)
        scatter_add(sums, hot, jnp.concatenate([grads[2 * i], grads[2 * i + 1]], axis=1))
        return carry

    lax.fori_loop(0, steps >> 1, two_blocks, 0)

    @pl.when((steps & 1) == 1)
    def _():
        scatter_add(sums, hot_of(steps - 1), grads[steps - 1])

    for k in range(first, first + negative_ids.shape[0] // 2):

        @pl.when(plan[2 * most + 1 + k] != 0)
        def _(k=k):
            add_negatives(sums, one_hot(negative_ids[k] - start, height), negative_grads[k])


def entity_kernel(table, state, returned, own, new_table, new_state):
    grad = returned[...] + own[...]
    lanes = 128
    before = jnp.broadcast_to(state[...], (lanes, table.shape[0])).T[:, :1]
    after = before + jnp.mean(grad * grad, axis=-1, keepdims=True)
    new_table[...] = table[...] - learn_rate * grad / jnp.sqrt(after)
    new_state[...] = jnp.broadcast_to(after, (table.shape[0], lanes)).T[:1]


def relation_kernel(chunk, codes, relations, state, mine, theirs, out, grad, column):
    chunks = mine.shape[0] // chunk
    for k in range(2 * chunks):
        part = (mine, theirs)[k // chunks]
        start = (k % chunks) * chunk
        grad[pl.ds(pl.multiple_of(codes[2] ^ (k * chunk), chunk), chunk), :] = part[start : start + chunk, :]
    count = relations.shape[0]
    column[...] = jnp.ones_like(column)
    column[:, :count] = jnp.broadcast_to(state[...], (column.shape[0], count))
    g = grad[:count, :]
    total = column[...].T[:count, :1] + jnp.mean(g * g, axis=-1, keepdims=True)
    out[...] = relations[...] - learn_rate * g / jnp.sqrt(total)


def exchange(x, axis, mask):
    return lax.ppermute(x, axis, [(i, i ^ mask) for i in range(lax.axis_size(axis))])


def on_device(
    entity_table,
    entity_state,
    relations,
    relation_state,
    head_rows,
    tail_rows,
    relation_ids,
    negative_rows,
    edge_counts,
):
    n = lax.axis_size("sub")
    n_dom = lax.axis_size("dom")
    me_sub = lax.axis_index("sub")
    me_dom = lax.axis_index("dom")
    pair = n_dom // 2
    team = 2 * n
    rows, dims = entity_table.shape
    slots = head_rows.shape[2]
    count = negative_rows.shape[2]
    width = count
    most = slots // width
    rel_rows = -(-relations.shape[0] // 256) * 256
    chips = 2 * n
    chunk = rel_rows // (2 * chips)
    me = lax.shift_right_logical(me_dom, pair.bit_length() - 1) * n + me_sub
    chunk_code = (me_dom & 1) * chips + ((me_dom >> 1) & 1) * n + me_sub
    codes = jnp.stack([me, me_sub * rows, chunk_code * chunk]).astype(i32)

    in_vmem = pl.BlockSpec(memory_space=pltpu.VMEM)
    in_smem = pl.BlockSpec(memory_space=pltpu.SMEM)

    def call(kernel, name, outs, scratch, unit, scalars, arrays, held=True, fetch=False):
        place = (lambda x, t: pltpu.VMEM(x, t)) if held else jax.ShapeDtypeStruct
        return pl.pallas_call(
            kernel,
            in_specs=[in_smem] * len(scalars) + [in_vmem] * len(arrays),
            out_specs=[in_vmem] * len(outs),
            out_shape=[place(x, t) for x, t in outs],
            scratch_shapes=scratch,
            compiler_params=params,
            cost_estimate=pl.CostEstimate(flops=int(slots * dims * unit), bytes_accessed=rows * dims, transcendentals=0),
            name=name,
        )(*scalars, *(pltpu.with_memory_space_constraint(x, pltpu.HBM if fetch else pltpu.VMEM) for x in arrays))

    (ids,) = call(
        ids_kernel,
        "ids_kernel",
        [((most + 1, 3, width), jnp.int16)],
        [],
        1,
        (edge_counts,),
        (
            head_rows.reshape(1, slots),
            tail_rows.reshape(1, slots),
            relation_ids.reshape(1, slots),
            negative_rows.reshape(1, count),
        ),
        fetch=True,
    )
    ids, table = lax.optimization_barrier((ids, entity_table))
    (local,) = call(rows_kernel, "rows_kernel", [((dims, rows), bf16)], [], 1, (), (table,), fetch=True)

    def to_peer(x, across, aside):
        pairs = [(d * n + s, (d ^ across) * n + (s ^ aside)) for d in range(n_dom) for s in range(n)]
        return lax.ppermute(x, ("dom", "sub"), pairs)

    def along_sub(x):
        return [x] + [exchange(x, "sub", k) for k in range(1, n)]

    all_ids = along_sub(ids) + along_sub(exchange(ids, "dom", pair))
    near_slab = along_sub(local)
    away_first = exchange(local, "dom", pair)

    plan, step_ids, negative_ids = pl.pallas_call(
        functools.partial(plan_kernel, n),
        in_specs=[in_smem] + [in_vmem] * team,
        out_specs=[in_smem, in_vmem, in_vmem],
        out_shape=[
            jax.ShapeDtypeStruct((2 * most + 1 + team,), i32),
            pltpu.VMEM((most, 3, width), i32),
            pltpu.VMEM((team, 1, width), i32),
        ],
        compiler_params=params,
        cost_estimate=pl.CostEstimate(flops=32 * slots * dims * rows, bytes_accessed=slots * dims, transcendentals=0),
        name="plan_kernel",
    )(codes, *(pltpu.with_memory_space_constraint(x, pltpu.VMEM) for x in all_ids))

    near_plan, away_first = lax.optimization_barrier((plan, away_first))
    away_slab = along_sub(away_first)
    near_rows, operator = call(
        near_kernel,
        "near_kernel",
        [((most, dims, width), bf16), ((most, dims, width), f32)],
        [pltpu.VMEM((rel_rows, dims), f32), pltpu.VMEM((2 * dims, rel_rows), bf16)],
        n * rows + 2 * rel_rows,
        (near_plan,),
        (step_ids, relations, *near_slab),
    )
    sums = ((rows, dims), f32)
    pair_out = ((most, 2 * dims, width), bf16)
    near_grad, away_grad, negative_grad, *found = call(
        functools.partial(edge_kernel, n),
        "edge_kernel",
        [pair_out, pair_out, ((team, 2 * count, dims), bf16)]
        + [sums] * (n - 1)
        + [((chunk, dims), f32)] * chips
        + [((chips * chunk, dims), f32)],
        [pltpu.VMEM((count, dims), bf16), pltpu.VMEM((dims, count), bf16), pltpu.VMEM((count, dims), f32)]
        + [pltpu.VMEM((-(-relations.shape[0] // 16) * 16, dims), f32), pltpu.VMEM((rel_rows, dims), f32)],
        3 * n * rows + 3 * count + 2 * rel_rows,
        (codes, plan),
        (step_ids, negative_ids, near_rows, operator, *near_slab, *away_slab),
    )
    away_other, relation_part = found[: n - 1], found[n - 1 :]

    def scatter(name, row, start, parts, first, plan, grads):
        return call(
            functools.partial(scatter_kernel, row, start, first),
            name,
            [sums] * parts,
            [],
            0,
            (plan,),
            (step_ids, negative_ids, grads, negative_grad),
        )

    scale = 2.0 ** -(math.ceil(math.log2(team * slots * 24 / 65504.0)) + 1)
    plane_scale = 2.0 ** -(math.ceil(math.log2(2 * chips * slots * 18 / 65504.0)) + 1)

    def narrow(x, scale=scale):
        return (x * scale).astype(jnp.float16)

    def widen(x, scale=scale):
        return x.astype(f32) * (1.0 / scale)

    def to_chip(x, k):
        return to_peer(x, k // n * 2, k % n)

    other_core = exchange(relation_part[chips], "dom", 1)
    partial = [relation_part[k] + other_core[k * chunk : (k + 1) * chunk] for k in range(chips)]
    away_other = [narrow(x) for x in away_other]
    partial, plan, away_other = lax.optimization_barrier((partial, plan, away_other))
    chunk_total = partial[0]
    for k in range(1, chips):
        chunk_total = chunk_total + to_chip(partial[k], k)
    away_received = [widen(exchange(away_other[k - 1], "sub", k)) for k in range(1, n)]
    (away_total,) = scatter("away_kernel", 1, 0, 1, 0, plan, away_grad)
    chunk_total = narrow(chunk_total, plane_scale)
    chunk_total, away_total, plan = lax.optimization_barrier((chunk_total, away_total, plan))
    terms = [chunk_total] + [exchange(chunk_total, "dom", mask) for mask in range(4, n_dom, 4)]
    terms = [widen(x, plane_scale) for x in terms]
    near_other = scatter("own_other_kernel", 0, rows, n - 1, n, plan, near_grad)
    near_other = [narrow(x) for x in near_other]
    for x in away_received:
        away_total = away_total + x
    away_total = narrow(away_total)
    while len(terms) > 1:
        terms = [terms[k] + terms[k + 1] for k in range(0, len(terms), 2)]
    chunk_total, away_total, near_other, plan = lax.optimization_barrier((terms[0], away_total, near_other, plan))
    returned = exchange(away_total, "dom", pair)
    near_received = [widen(exchange(near_other[k - 1], "sub", k)) for k in range(1, n)]
    mine = jnp.concatenate([chunk_total] + [to_chip(chunk_total, k) for k in range(1, chips)], axis=0)
    (near_sum,) = scatter("own_kernel", 0, 0, 1, n, plan, near_grad)
    returned, mine, near_sum = lax.optimization_barrier((returned, mine, near_sum))
    theirs = exchange(mine, "dom", 1)
    (new_relations,) = call(
        functools.partial(relation_kernel, chunk),
        "relation_kernel",
        [(relations.shape, f32)],
        [pltpu.VMEM((rel_rows, dims), f32), pltpu.VMEM((128, rel_rows), f32)],
        0,
        (codes,),
        (relations, relation_state.reshape(1, -1), mine, theirs),
        held=False,
    )
    returned = widen(returned)
    for x in near_received:
        returned = returned + x
    new_table, new_state = call(
        entity_kernel,
        "entity_kernel",
        [((rows, dims), f32), ((1, rows), f32)],
        [],
        1,
        (),
        (entity_table, entity_state.reshape(1, rows), returned, near_sum),
        held=False,
    )
    return (new_table, new_state.reshape(rows), new_relations)


def solution(mesh):
    in_specs = (
        P(("dom", "sub"), None),
        P(("dom", "sub")),
        P(),
        P(),
        P("dom", "sub", None),
        P("dom", "sub", None),
        P("dom", "sub", None),
        P("dom", "sub", None),
        P("dom", "sub"),
    )
    out_specs = (P(("dom", "sub"), None), P(("dom", "sub")), P())
    return jax.shard_map(
        on_device, mesh=mesh, in_specs=in_specs, out_specs=out_specs, check_vma=False
    )
```

```python
import functools
import math

import jax
import jax.numpy as jnp
from jax import lax
from jax.experimental import pallas as pl
from jax.experimental.pallas import tpu as pltpu
from jax.sharding import PartitionSpec as P

learn_rate = 0.1
bf16 = jnp.bfloat16
f32 = jnp.float32
i32 = jnp.int32
params = pltpu.CompilerParams(vmem_limit_bytes=10 * 2**20)


def dot(a, b):
    return jnp.dot(a, b, preferred_element_type=f32)


def dot_nt(a, b):
    return lax.dot_general(a, b, (((1,), (1,)), ((), ())), preferred_element_type=f32)


def one_hot(ids, rows):
    places = lax.broadcasted_iota(jnp.int16, (rows, ids.shape[1]), 0)
    return jnp.where(places == ids.astype(jnp.int16), jnp.ones((), bf16), jnp.zeros((), bf16))


def split(x):
    high = x.astype(bf16)
    return jnp.concatenate([high, (x - high.astype(f32)).astype(bf16)], axis=0)


def gather(pieces, hot):
    rows = pieces[0].shape[1]
    total = dot(pieces[0][...], hot[:rows])
    for k in range(1, len(pieces)):
        total = total + dot(pieces[k][...], hot[k * rows : (k + 1) * rows])
    return total


def scatter_add(pieces, hot, pair):
    dims = pair.shape[0] // 2
    start = 0
    for piece in pieces:
        part = hot[start : start + piece.shape[0]]
        piece[...] += dot_nt(part, pair[:dims]) + dot_nt(part, pair[dims:])
        start += piece.shape[0]


def add_negatives(pieces, hot, pair):
    count = pair.shape[0] // 2
    start = 0
    for piece in pieces:
        part = hot[start : start + piece.shape[0]]
        piece[...] += dot(part, pair[:count]) + dot(part, pair[count:])
        start += piece.shape[0]


def rows_kernel(table, out):
    out[...] = table[...].T.astype(bf16)


def ids_kernel(count, heads, tails, kinds, negatives, ids_out, upper_out):
    blocks, _, width = ids_out.shape
    for j in range(blocks - 1):
        at = slice(j * width, (j + 1) * width)
        block = jnp.concatenate([heads[:, at], tails[:, at], kinds[:, at]], axis=0)
        ids_out[j] = block.astype(jnp.int16)
    last = jnp.concatenate([negatives[...], jnp.full((2, width), count[0, 0], i32)], axis=0)
    ids_out[blocks - 1] = last.astype(jnp.int16)
    upper_out[...] = ids_out[blocks - upper_out.shape[0] :]


def plan_kernel(n, codes, *refs):
    sources, (plan, step_ids, negative_ids) = refs[:-3], refs[-3:]
    team = len(sources)
    most, _, width = step_ids.shape
    offset = most + 1 - sources[-1].shape[0]
    me = codes[0]
    counts, blocks, movable = [], [], []
    for k, ids in enumerate(sources):
        last = ids[ids.shape[0] - 1].astype(i32)
        counts.append(jnp.max(last[1:2]))
        blocks.append(lax.div(counts[k] + (width - 1), i32(width)))
        movable.append(jnp.maximum(blocks[k] - offset, 0))
        negative_ids[k] = last[0:1] ^ codes[1]
    surplus = sum(blocks[:n]) - sum(blocks[n:])
    starts, lengths = [], []
    for k in range(team):
        side = range(n) if k < n else range(n, team)
        moved = jnp.maximum(lax.div(surplus if k < n else -surplus, i32(2)), 0)
        later = [jnp.where((me ^ j) > (me ^ k), movable[j], 0) for j in side if j != k]
        moved = jnp.clip(moved - sum(later), 0, movable[k])
        starts.append(0 if k < n else blocks[k] - moved)
        lengths.append(blocks[k] - moved if k < n else moved)
    total = sum(lengths)
    place = codes[3]
    low = lax.div(place * total, i32(n))
    high = lax.div((place + 1) * total, i32(n))
    plan[2 * most] = high - low
    before = []
    for k in range(team):
        ahead = [jnp.where((me ^ j) < (me ^ k), lengths[j], 0) for j in range(team) if j != k]
        before.append(sum(ahead))
        seen = (lengths[k] > 0) & (before[k] < high) & (before[k] + lengths[k] > low)
        plan[2 * most + 1 + k] = seen.astype(i32)

    def one_step(i, carry):
        line = low + i
        for k, ids in enumerate(sources):

            @pl.when((line >= before[k]) & (line < before[k] + lengths[k]))
            def _(k=k, ids=ids):
                nth = line - before[k] + starts[k]
                plan[i] = k
                plan[most + i] = jnp.clip(counts[k] - nth * width, 0, width)
                entries = ids[nth - (most + 1 - ids.shape[0])].astype(i32)
                near, away = (0, 1) if k < n else (1, 0)
                step_ids[i, 0:1] = entries[near : near + 1] ^ codes[1]
                step_ids[i, 1:2] = entries[away : away + 1] ^ codes[1]
                step_ids[i, 2:3] = entries[2:3]

        return carry

    lax.fori_loop(0, high - low, one_step, 0)


def near_kernel(plan, ids, relations, *refs):
    slab, (rows_out, operator_out, rel_full, rel_split) = refs[:-4], refs[-4:]
    dims = relations.shape[1]
    n, rows = len(slab), slab[0].shape[1]
    rel_full[...] = jnp.zeros_like(rel_full)
    rel_full[: relations.shape[0], :] = relations[...]
    rel_split[...] = split(rel_full[...].T)

    def one_block(i):
        entries = ids[i]
        rows_out[i] = gather(slab, one_hot(entries[0:1], n * rows)).astype(bf16)
        both = dot(rel_split[...], one_hot(entries[2:3], rel_full.shape[0]))
        operator_out[i] = both[:dims] + both[dims:]

    steps = plan[2 * ids.shape[0]]

    def two_blocks(i, carry):
        one_block(2 * i)
        one_block(2 * i + 1)
        return carry

    lax.fori_loop(0, steps >> 1, two_blocks, 0)
    pl.when((steps & 1) == 1)(lambda: one_block(steps - 1))


def edge_kernel(n, codes, plan, ids, negative_ids, near_in, operator_in, *refs):
    near, away = refs[:n], refs[n : 2 * n]
    near_grad, away_grad, negative_out = refs[2 * n : 2 * n + 3]
    away_other = refs[2 * n + 3 : 3 * n + 2]
    relation_out = refs[3 * n + 2 : -5]
    table, table_t, negative_grad, relation_sum, ordered = refs[-5:]
    most, _, width = ids.shape
    steps = plan[2 * most]
    count = table.shape[0]
    for piece in (*away_other, relation_sum):
        piece[...] = jnp.zeros_like(piece)
    rows = away[0].shape[1]

    def one_block(i, carry):
        here = plan[i]
        swapped = here >= n

        def take_table(slab):
            found = gather(slab, one_hot(negative_ids[here], n * rows))
            table_t[...] = found.astype(bf16)
            table[...] = found.T.astype(bf16)
            negative_grad[...] = jnp.zeros_like(negative_grad)

        fresh = (i == 0) | (plan[jnp.maximum(i - 1, 0)] != here)
        pl.when(fresh & ~swapped)(lambda: take_table(away))
        pl.when(fresh & swapped)(lambda: take_table(near))

        entries = ids[i]

        def score(swapped):
            alive = (lax.broadcasted_iota(i32, (1, width), 1) < plan[most + i]).astype(f32)
            near_rows = near_in[i].astype(f32)
            away_hot = one_hot(entries[1:2], n * rows)
            away_rows = gather(away, away_hot)
            head, tail = (away_rows, near_rows) if swapped else (near_rows, away_rows)
            operator = operator_in[i]
            query = head * operator
            query_b = query.astype(bf16)
            positive = jnp.sum(query * tail, axis=0, keepdims=True)
            scores = dot(table[...], query_b)
            pos_coef = -jax.nn.sigmoid(-positive) * alive
            neg_coef = (jax.nn.sigmoid(scores) * (alive * (1.0 / count))).astype(bf16)
            query_grad = pos_coef * tail + dot(table_t[...], neg_coef)
            negative_grad[...] += dot_nt(neg_coef, query_b)
            head_pair, tail_pair = split(query_grad * operator), split(pos_coef * query)
            near_pair, away_pair = (tail_pair, head_pair) if swapped else (head_pair, tail_pair)
            near_grad[i] = near_pair
            away_grad[i] = away_pair
            scatter_add(away_other, away_hot[rows:], away_pair)
            scatter_add([relation_sum], one_hot(entries[2:3], relation_sum.shape[0]), split(query_grad * head))

        pl.when(~swapped)(lambda: score(False))
        pl.when(swapped)(lambda: score(True))

        ends = (i == steps - 1) | (plan[jnp.minimum(i + 1, steps - 1)] != here)

        @pl.when(ends)
        def _():
            negative_out[here] = split(negative_grad[...])

        @pl.when(ends & ~swapped)
        def _():
            add_negatives(away_other, one_hot(negative_ids[here] - rows, (n - 1) * rows), negative_out[here])

        return carry

    lax.fori_loop(0, steps, one_block, 0)
    chunk = relation_out[0].shape[0]
    ordered[...] = jnp.zeros_like(ordered)
    ordered[: relation_sum.shape[0], :] = relation_sum[...]
    start = 0
    for piece in relation_out:
        for k in range(0, piece.shape[0], chunk):
            at = pl.multiple_of(codes[2] ^ (start + k), chunk)
            piece[k : k + chunk, :] = ordered[pl.ds(at, chunk), :]
        start += piece.shape[0]


def scatter_kernel(row, start, first, plan, ids, negative_ids, grads, negative_grads, *sums):
    most = ids.shape[0]
    height = sum(piece.shape[0] for piece in sums)
    for piece in sums:
        piece[...] = jnp.zeros_like(piece)

    steps = plan[2 * most]

    def hot_of(i):
        return one_hot(ids[i][row : row + 1] - start, height)

    def two_blocks(i, carry):
        hot = jnp.concatenate([hot_of(2 * i), hot_of(2 * i + 1)], axis=1)
        scatter_add(sums, hot, jnp.concatenate([grads[2 * i], grads[2 * i + 1]], axis=1))
        return carry

    lax.fori_loop(0, steps >> 1, two_blocks, 0)

    @pl.when((steps & 1) == 1)
    def _():
        scatter_add(sums, hot_of(steps - 1), grads[steps - 1])

    for k in range(first, first + negative_ids.shape[0] // 2):

        @pl.when(plan[2 * most + 1 + k] != 0)
        def _(k=k):
            add_negatives(sums, one_hot(negative_ids[k] - start, height), negative_grads[k])


def entity_kernel(table, state, returned, own, new_table, new_state):
    grad = returned[...] + own[...]
    lanes = 128
    before = jnp.broadcast_to(state[...], (lanes, table.shape[0])).T[:, :1]
    after = before + jnp.mean(grad * grad, axis=-1, keepdims=True)
    new_table[...] = table[...] - learn_rate * grad / jnp.sqrt(after)
    new_state[...] = jnp.broadcast_to(after, (table.shape[0], lanes)).T[:1]


def relation_kernel(chunk, codes, relations, state, mine, theirs, out, grad, column):
    chunks = mine.shape[0] // chunk
    for k in range(2 * chunks):
        part = (mine, theirs)[k // chunks]
        start = (k % chunks) * chunk
        grad[pl.ds(pl.multiple_of(codes[2] ^ (k * chunk), chunk), chunk), :] = part[start : start + chunk, :]
    count = relations.shape[0]
    column[...] = jnp.ones_like(column)
    column[:, :count] = jnp.broadcast_to(state[...], (column.shape[0], count))
    g = grad[:count, :]
    total = column[...].T[:count, :1] + jnp.mean(g * g, axis=-1, keepdims=True)
    out[...] = relations[...] - learn_rate * g / jnp.sqrt(total)


def exchange(x, axis, mask):
    return lax.ppermute(x, axis, [(i, i ^ mask) for i in range(lax.axis_size(axis))])


def on_device(
    entity_table,
    entity_state,
    relations,
    relation_state,
    head_rows,
    tail_rows,
    relation_ids,
    negative_rows,
    edge_counts,
):
    n = lax.axis_size("sub")
    n_dom = lax.axis_size("dom")
    me_sub = lax.axis_index("sub")
    me_dom = lax.axis_index("dom")
    pair = n_dom // 2
    team = 2 * n
    rows, dims = entity_table.shape
    slots = head_rows.shape[2]
    count = negative_rows.shape[2]
    width = count
    most = slots // width
    rel_rows = -(-relations.shape[0] // 256) * 256
    chips = 2 * n
    chunk = rel_rows // (2 * chips)
    me = lax.shift_right_logical(me_dom, pair.bit_length() - 1) * n + me_sub
    chunk_code = (me_dom & 1) * chips + ((me_dom >> 1) & 1) * n + me_sub
    codes = jnp.stack([me, me_sub * rows, chunk_code * chunk, me_sub]).astype(i32)

    in_vmem = pl.BlockSpec(memory_space=pltpu.VMEM)
    in_smem = pl.BlockSpec(memory_space=pltpu.SMEM)

    def call(kernel, name, outs, scratch, unit, scalars, arrays, held=True, fetch=False):
        place = (lambda x, t: pltpu.VMEM(x, t)) if held else jax.ShapeDtypeStruct
        return pl.pallas_call(
            kernel,
            in_specs=[in_smem] * len(scalars) + [in_vmem] * len(arrays),
            out_specs=[in_vmem] * len(outs),
            out_shape=[place(x, t) for x, t in outs],
            scratch_shapes=scratch,
            compiler_params=params,
            cost_estimate=pl.CostEstimate(flops=int(slots * dims * unit), bytes_accessed=rows * dims, transcendentals=0),
            name=name,
        )(*scalars, *(pltpu.with_memory_space_constraint(x, pltpu.HBM if fetch else pltpu.VMEM) for x in arrays))

    ids, upper = call(
        ids_kernel,
        "ids_kernel",
        [((most + 1, 3, width), jnp.int16), ((most + 1 - most // 2, 3, width), jnp.int16)],
        [],
        1,
        (edge_counts,),
        (
            head_rows.reshape(1, slots),
            tail_rows.reshape(1, slots),
            relation_ids.reshape(1, slots),
            negative_rows.reshape(1, count),
        ),
        fetch=True,
    )
    ids, upper, table = lax.optimization_barrier((ids, upper, entity_table))
    (local,) = call(rows_kernel, "rows_kernel", [((dims, rows), bf16)], [], 1, (), (table,), fetch=True)

    def to_peer(x, across, aside):
        pairs = [(d * n + s, (d ^ across) * n + (s ^ aside)) for d in range(n_dom) for s in range(n)]
        return lax.ppermute(x, ("dom", "sub"), pairs)

    def along_sub(x):
        return [x] + [exchange(x, "sub", k) for k in range(1, n)]

    all_ids = along_sub(ids) + along_sub(exchange(upper, "dom", pair))
    near_slab = along_sub(local)
    away_first = exchange(local, "dom", pair)

    plan, step_ids, negative_ids = pl.pallas_call(
        functools.partial(plan_kernel, n),
        in_specs=[in_smem] + [in_vmem] * team,
        out_specs=[in_smem, in_vmem, in_vmem],
        out_shape=[
            jax.ShapeDtypeStruct((2 * most + 1 + team,), i32),
            pltpu.VMEM((most, 3, width), i32),
            pltpu.VMEM((team, 1, width), i32),
        ],
        compiler_params=params,
        cost_estimate=pl.CostEstimate(flops=32 * slots * dims * rows, bytes_accessed=slots * dims, transcendentals=0),
        name="plan_kernel",
    )(codes, *(pltpu.with_memory_space_constraint(x, pltpu.VMEM) for x in all_ids))

    near_plan, away_first = lax.optimization_barrier((plan, away_first))
    away_slab = along_sub(away_first)
    near_rows, operator = call(
        near_kernel,
        "near_kernel",
        [((most, dims, width), bf16), ((most, dims, width), f32)],
        [pltpu.VMEM((rel_rows, dims), f32), pltpu.VMEM((2 * dims, rel_rows), bf16)],
        n * rows + 2 * rel_rows,
        (near_plan,),
        (step_ids, relations, *near_slab),
    )
    sums = ((rows, dims), f32)
    pair_out = ((most, 2 * dims, width), bf16)
    near_grad, away_grad, negative_grad, *found = call(
        functools.partial(edge_kernel, n),
        "edge_kernel",
        [pair_out, pair_out, ((team, 2 * count, dims), bf16)]
        + [sums] * (n - 1)
        + [((chunk, dims), f32)] * chips
        + [((chips * chunk, dims), f32)],
        [pltpu.VMEM((count, dims), bf16), pltpu.VMEM((dims, count), bf16), pltpu.VMEM((count, dims), f32)]
        + [pltpu.VMEM((-(-relations.shape[0] // 16) * 16, dims), f32), pltpu.VMEM((rel_rows, dims), f32)],
        3 * n * rows + 3 * count + 2 * rel_rows,
        (codes, plan),
        (step_ids, negative_ids, near_rows, operator, *near_slab, *away_slab),
    )
    away_other, relation_part = found[: n - 1], found[n - 1 :]

    def scatter(name, row, start, parts, first, plan, grads):
        return call(
            functools.partial(scatter_kernel, row, start, first),
            name,
            [sums] * parts,
            [],
            0,
            (plan,),
            (step_ids, negative_ids, grads, negative_grad),
        )

    scale = 2.0 ** -(math.ceil(math.log2(team * slots * 24 / 65504.0)) + 1)
    plane_scale = 2.0 ** -(math.ceil(math.log2(2 * chips * slots * 18 / 65504.0)) + 1)

    def narrow(x, scale=scale):
        return (x * scale).astype(jnp.float16)

    def widen(x, scale=scale):
        return x.astype(f32) * (1.0 / scale)

    def to_chip(x, k):
        return to_peer(x, k // n * 2, k % n)

    other_core = exchange(relation_part[chips], "dom", 1)
    partial = [relation_part[k] + other_core[k * chunk : (k + 1) * chunk] for k in range(chips)]
    away_other = [narrow(x) for x in away_other]
    partial, plan, away_other = lax.optimization_barrier((partial, plan, away_other))
    chunk_total = partial[0]
    for k in range(1, chips):
        chunk_total = chunk_total + to_chip(partial[k], k)
    away_received = [widen(exchange(away_other[k - 1], "sub", k)) for k in range(1, n)]
    (away_total,) = scatter("away_kernel", 1, 0, 1, 0, plan, away_grad)
    chunk_total = narrow(chunk_total, plane_scale)
    chunk_total, away_total, plan = lax.optimization_barrier((chunk_total, away_total, plan))
    terms = [chunk_total] + [exchange(chunk_total, "dom", mask) for mask in range(4, n_dom, 4)]
    terms = [widen(x, plane_scale) for x in terms]
    near_other = scatter("own_other_kernel", 0, rows, n - 1, n, plan, near_grad)
    near_other = [narrow(x) for x in near_other]
    for x in away_received:
        away_total = away_total + x
    away_total = narrow(away_total)
    while len(terms) > 1:
        terms = [terms[k] + terms[k + 1] for k in range(0, len(terms), 2)]
    chunk_total, away_total, near_other, plan = lax.optimization_barrier((terms[0], away_total, near_other, plan))
    returned = exchange(away_total, "dom", pair)
    near_received = [widen(exchange(near_other[k - 1], "sub", k)) for k in range(1, n)]
    mine = jnp.concatenate([chunk_total] + [to_chip(chunk_total, k) for k in range(1, chips)], axis=0)
    (near_sum,) = scatter("own_kernel", 0, 0, 1, n, plan, near_grad)
    returned, mine, near_sum = lax.optimization_barrier((returned, mine, near_sum))
    theirs = exchange(mine, "dom", 1)
    (new_relations,) = call(
        functools.partial(relation_kernel, chunk),
        "relation_kernel",
        [(relations.shape, f32)],
        [pltpu.VMEM((rel_rows, dims), f32), pltpu.VMEM((128, rel_rows), f32)],
        0,
        (codes,),
        (relations, relation_state.reshape(1, -1), mine, theirs),
        held=False,
    )
    returned = widen(returned)
    for x in near_received:
        returned = returned + x
    new_table, new_state = call(
        entity_kernel,
        "entity_kernel",
        [((rows, dims), f32), ((1, rows), f32)],
        [],
        1,
        (),
        (entity_table, entity_state.reshape(1, rows), returned, near_sum),
        held=False,
    )
    return (new_table, new_state.reshape(rows), new_relations)


def solution(mesh):
    in_specs = (
        P(("dom", "sub"), None),
        P(("dom", "sub")),
        P(),
        P(),
        P("dom", "sub", None),
        P("dom", "sub", None),
        P("dom", "sub", None),
        P("dom", "sub", None),
        P("dom", "sub"),
    )
    out_specs = (P(("dom", "sub"), None), P(("dom", "sub")), P())
    return jax.shard_map(
        on_device, mesh=mesh, in_specs=in_specs, out_specs=out_specs, check_vma=False
    )
```

```python
import functools
import math

import jax
import jax.numpy as jnp
from jax import lax
from jax.experimental import pallas as pl
from jax.experimental.pallas import tpu as pltpu
from jax.sharding import PartitionSpec as P

learn_rate = 0.1
bf16 = jnp.bfloat16
f32 = jnp.float32
i32 = jnp.int32
params = pltpu.CompilerParams(vmem_limit_bytes=10 * 2**20)


def dot(a, b):
    return jnp.dot(a, b, preferred_element_type=f32)


def dot_nt(a, b):
    return lax.dot_general(a, b, (((1,), (1,)), ((), ())), preferred_element_type=f32)


def one_hot(ids, rows):
    places = lax.broadcasted_iota(jnp.int16, (rows, ids.shape[1]), 0)
    return jnp.where(places == ids.astype(jnp.int16), jnp.ones((), bf16), jnp.zeros((), bf16))


def split(x):
    high = x.astype(bf16)
    return jnp.concatenate([high, (x - high.astype(f32)).astype(bf16)], axis=0)


def gather(pieces, hot):
    rows = pieces[0].shape[1]
    total = dot(pieces[0][...], hot[:rows])
    for k in range(1, len(pieces)):
        total = total + dot(pieces[k][...], hot[k * rows : (k + 1) * rows])
    return total


def scatter_add(pieces, hot, pair):
    dims = pair.shape[0] // 2
    start = 0
    for piece in pieces:
        part = hot[start : start + piece.shape[0]]
        piece[...] += dot_nt(part, pair[:dims]) + dot_nt(part, pair[dims:])
        start += piece.shape[0]


def add_negatives(pieces, hot, pair):
    count = pair.shape[0] // 2
    start = 0
    for piece in pieces:
        part = hot[start : start + piece.shape[0]]
        piece[...] += dot(part, pair[:count]) + dot(part, pair[count:])
        start += piece.shape[0]


def rows_kernel(table, out):
    out[...] = table[...].T.astype(bf16)


def ids_kernel(count, heads, tails, kinds, negatives, ids_out, upper_out):
    blocks, _, width = ids_out.shape
    for j in range(blocks - 1):
        at = slice(j * width, (j + 1) * width)
        block = jnp.concatenate([heads[:, at], tails[:, at], kinds[:, at]], axis=0)
        ids_out[j] = block.astype(jnp.int16)
    last = jnp.concatenate([negatives[...], jnp.full((2, width), count[0, 0], i32)], axis=0)
    ids_out[blocks - 1] = last.astype(jnp.int16)
    upper_out[...] = ids_out[blocks - upper_out.shape[0] :]


def plan_kernel(n, codes, *refs):
    sources, (plan, step_ids, negative_ids) = refs[:-3], refs[-3:]
    team = len(sources)
    most, _, width = step_ids.shape
    offset = most + 1 - sources[-1].shape[0]
    me = codes[0]
    counts, blocks, movable = [], [], []
    for k, ids in enumerate(sources):
        last = ids[ids.shape[0] - 1].astype(i32)
        counts.append(jnp.max(last[1:2]))
        blocks.append(lax.div(counts[k] + (width - 1), i32(width)))
        movable.append(jnp.maximum(blocks[k] - offset, 0))
        negative_ids[k] = last[0:1] ^ codes[1]
    surplus = sum(blocks[:n]) - sum(blocks[n:])
    starts, lengths = [], []
    for k in range(team):
        side = range(n) if k < n else range(n, team)
        moved = jnp.maximum(lax.div(surplus if k < n else -surplus, i32(2)), 0)
        later = [jnp.where((me ^ j) > (me ^ k), movable[j], 0) for j in side if j != k]
        moved = jnp.clip(moved - sum(later), 0, movable[k])
        starts.append(0 if k < n else blocks[k] - moved)
        lengths.append(blocks[k] - moved if k < n else moved)
    total = sum(lengths)
    place = codes[3]
    low = lax.div(place * total, i32(n))
    high = lax.div((place + 1) * total, i32(n))
    plan[2 * most] = high - low
    before = []
    for k in range(team):
        ahead = [jnp.where((me ^ j) < (me ^ k), lengths[j], 0) for j in range(team) if j != k]
        before.append(sum(ahead))
        seen = (lengths[k] > 0) & (before[k] < high) & (before[k] + lengths[k] > low)
        plan[2 * most + 1 + k] = seen.astype(i32)

    def one_step(i, carry):
        line = low + i
        for k, ids in enumerate(sources):

            @pl.when((line >= before[k]) & (line < before[k] + lengths[k]))
            def _(k=k, ids=ids):
                nth = line - before[k] + starts[k]
                plan[i] = k
                plan[most + i] = jnp.clip(counts[k] - nth * width, 0, width)
                entries = ids[nth - (most + 1 - ids.shape[0])].astype(i32)
                near, away = (0, 1) if k < n else (1, 0)
                step_ids[i, 0:1] = entries[near : near + 1] ^ codes[1]
                step_ids[i, 1:2] = entries[away : away + 1] ^ codes[1]
                step_ids[i, 2:3] = entries[2:3]

        return carry

    lax.fori_loop(0, high - low, one_step, 0)


def near_kernel(plan, ids, relations, *refs):
    slab, (rows_out, operator_out, rel_full, rel_split) = refs[:-4], refs[-4:]
    dims = relations.shape[1]
    n, rows = len(slab), slab[0].shape[1]
    rel_full[...] = jnp.zeros_like(rel_full)
    rel_full[: relations.shape[0], :] = relations[...]
    rel_split[...] = split(rel_full[...].T)

    def one_block(i):
        entries = ids[i]
        rows_out[i] = gather(slab, one_hot(entries[0:1], n * rows)).astype(bf16)
        both = dot(rel_split[...], one_hot(entries[2:3], rel_full.shape[0]))
        operator_out[i] = both[:dims] + both[dims:]

    steps = plan[2 * ids.shape[0]]

    def two_blocks(i, carry):
        one_block(2 * i)
        one_block(2 * i + 1)
        return carry

    lax.fori_loop(0, steps >> 1, two_blocks, 0)
    pl.when((steps & 1) == 1)(lambda: one_block(steps - 1))


def edge_kernel(n, codes, plan, ids, negative_ids, near_in, operator_in, *refs):
    near, away = refs[:n], refs[n : 2 * n]
    near_grad, away_grad, negative_out = refs[2 * n : 2 * n + 3]
    away_other = refs[2 * n + 3 : 3 * n + 2]
    relation_out = refs[3 * n + 2 : -5]
    table, table_t, negative_grad, relation_sum, ordered = refs[-5:]
    most, _, width = ids.shape
    steps = plan[2 * most]
    count = table.shape[0]
    for piece in (*away_other, relation_sum):
        piece[...] = jnp.zeros_like(piece)
    rows = away[0].shape[1]

    def one_block(i, carry):
        here = plan[i]
        swapped = here >= n

        def take_table(slab):
            found = gather(slab, one_hot(negative_ids[here], n * rows))
            table_t[...] = found.astype(bf16)
            table[...] = found.T.astype(bf16)
            negative_grad[...] = jnp.zeros_like(negative_grad)

        fresh = (i == 0) | (plan[jnp.maximum(i - 1, 0)] != here)
        pl.when(fresh & ~swapped)(lambda: take_table(away))
        pl.when(fresh & swapped)(lambda: take_table(near))

        entries = ids[i]

        def score(swapped):
            alive = (lax.broadcasted_iota(i32, (1, width), 1) < plan[most + i]).astype(f32)
            near_rows = near_in[i].astype(f32)
            away_hot = one_hot(entries[1:2], n * rows)
            away_rows = gather(away, away_hot)
            head, tail = (away_rows, near_rows) if swapped else (near_rows, away_rows)
            operator = operator_in[i]
            query = head * operator
            query_b = query.astype(bf16)
            positive = jnp.sum(query * tail, axis=0, keepdims=True)
            scores = dot(table[...], query_b)
            pos_coef = -jax.nn.sigmoid(-positive) * alive
            neg_coef = (jax.nn.sigmoid(scores) * (alive * (1.0 / count))).astype(bf16)
            query_grad = pos_coef * tail + dot(table_t[...], neg_coef)
            negative_grad[...] += dot_nt(neg_coef, query_b)
            head_pair, tail_pair = split(query_grad * operator), split(pos_coef * query)
            near_pair, away_pair = (tail_pair, head_pair) if swapped else (head_pair, tail_pair)
            near_grad[i] = near_pair
            away_grad[i] = away_pair
            scatter_add(away_other, away_hot[rows:], away_pair)
            scatter_add([relation_sum], one_hot(entries[2:3], relation_sum.shape[0]), split(query_grad * head))

        pl.when(~swapped)(lambda: score(False))
        pl.when(swapped)(lambda: score(True))

        ends = (i == steps - 1) | (plan[jnp.minimum(i + 1, steps - 1)] != here)

        @pl.when(ends)
        def _():
            negative_out[here] = split(negative_grad[...])

        @pl.when(ends & ~swapped)
        def _():
            add_negatives(away_other, one_hot(negative_ids[here] - rows, (n - 1) * rows), negative_out[here])

        return carry

    lax.fori_loop(0, steps, one_block, 0)
    chunk = relation_out[0].shape[0]
    ordered[...] = jnp.zeros_like(ordered)
    ordered[: relation_sum.shape[0], :] = relation_sum[...]
    start = 0
    for piece in relation_out:
        for k in range(0, piece.shape[0], chunk):
            at = pl.multiple_of(codes[2] ^ (start + k), chunk)
            piece[k : k + chunk, :] = ordered[pl.ds(at, chunk), :]
        start += piece.shape[0]


def scatter_kernel(row, start, first, plan, ids, negative_ids, grads, negative_grads, *sums):
    most = ids.shape[0]
    height = sum(piece.shape[0] for piece in sums)
    for piece in sums:
        piece[...] = jnp.zeros_like(piece)

    steps = plan[2 * most]

    def hot_of(i):
        return one_hot(ids[i][row : row + 1] - start, height)

    def two_blocks(i, carry):
        hot = jnp.concatenate([hot_of(2 * i), hot_of(2 * i + 1)], axis=1)
        scatter_add(sums, hot, jnp.concatenate([grads[2 * i], grads[2 * i + 1]], axis=1))
        return carry

    lax.fori_loop(0, steps >> 1, two_blocks, 0)

    @pl.when((steps & 1) == 1)
    def _():
        scatter_add(sums, hot_of(steps - 1), grads[steps - 1])

    for k in range(first, first + negative_ids.shape[0] // 2):

        @pl.when(plan[2 * most + 1 + k] != 0)
        def _(k=k):
            add_negatives(sums, one_hot(negative_ids[k] - start, height), negative_grads[k])


def entity_kernel(table, state, returned, own, new_table, new_state):
    grad = returned[...] + own[...]
    lanes = 128
    before = jnp.broadcast_to(state[...], (lanes, table.shape[0])).T[:, :1]
    after = before + jnp.mean(grad * grad, axis=-1, keepdims=True)
    new_table[...] = table[...] - learn_rate * grad / jnp.sqrt(after)
    new_state[...] = jnp.broadcast_to(after, (table.shape[0], lanes)).T[:1]


def relation_kernel(chunk, codes, relations, state, mine, theirs, out, grad, column):
    chunks = mine.shape[0] // chunk
    for k in range(2 * chunks):
        part = (mine, theirs)[k // chunks]
        start = (k % chunks) * chunk
        grad[pl.ds(pl.multiple_of(codes[2] ^ (k * chunk), chunk), chunk), :] = part[start : start + chunk, :]
    count = relations.shape[0]
    column[...] = jnp.ones_like(column)
    column[:, :count] = jnp.broadcast_to(state[...], (column.shape[0], count))
    g = grad[:count, :]
    total = column[...].T[:count, :1] + jnp.mean(g * g, axis=-1, keepdims=True)
    out[...] = relations[...] - learn_rate * g / jnp.sqrt(total)


def exchange(x, axis, mask):
    return lax.ppermute(x, axis, [(i, i ^ mask) for i in range(lax.axis_size(axis))])


def on_device(
    entity_table,
    entity_state,
    relations,
    relation_state,
    head_rows,
    tail_rows,
    relation_ids,
    negative_rows,
    edge_counts,
):
    n = lax.axis_size("sub")
    n_dom = lax.axis_size("dom")
    me_sub = lax.axis_index("sub")
    me_dom = lax.axis_index("dom")
    pair = n_dom // 2
    team = 2 * n
    rows, dims = entity_table.shape
    slots = head_rows.shape[2]
    count = negative_rows.shape[2]
    width = count
    most = slots // width
    rel_rows = -(-relations.shape[0] // 256) * 256
    chips = 2 * n
    chunk = rel_rows // (2 * chips)
    me = lax.shift_right_logical(me_dom, pair.bit_length() - 1) * n + me_sub
    chunk_code = (me_dom & 1) * chips + ((me_dom >> 1) & 1) * n + me_sub
    codes = jnp.stack([me, me_sub * rows, chunk_code * chunk, me_sub]).astype(i32)

    in_vmem = pl.BlockSpec(memory_space=pltpu.VMEM)
    in_smem = pl.BlockSpec(memory_space=pltpu.SMEM)

    def call(kernel, name, outs, scratch, unit, scalars, arrays, held=True, fetch=False):
        place = (lambda x, t: pltpu.VMEM(x, t)) if held else jax.ShapeDtypeStruct
        return pl.pallas_call(
            kernel,
            in_specs=[in_smem] * len(scalars) + [in_vmem] * len(arrays),
            out_specs=[in_vmem] * len(outs),
            out_shape=[place(x, t) for x, t in outs],
            scratch_shapes=scratch,
            compiler_params=params,
            cost_estimate=pl.CostEstimate(flops=int(slots * dims * unit), bytes_accessed=rows * dims, transcendentals=0),
            name=name,
        )(*scalars, *(pltpu.with_memory_space_constraint(x, pltpu.HBM if fetch else pltpu.VMEM) for x in arrays))

    ids, upper = call(
        ids_kernel,
        "ids_kernel",
        [((most + 1, 3, width), jnp.int16), ((most + 1 - most // 2, 3, width), jnp.int16)],
        [],
        1,
        (edge_counts,),
        (
            head_rows.reshape(1, slots),
            tail_rows.reshape(1, slots),
            relation_ids.reshape(1, slots),
            negative_rows.reshape(1, count),
        ),
        fetch=True,
    )
    ids, upper, table = lax.optimization_barrier((ids, upper, entity_table))
    (local,) = call(rows_kernel, "rows_kernel", [((dims, rows), bf16)], [], 1, (), (table,), fetch=True)

    def to_peer(x, across, aside):
        pairs = [(d * n + s, (d ^ across) * n + (s ^ aside)) for d in range(n_dom) for s in range(n)]
        return lax.ppermute(x, ("dom", "sub"), pairs)

    def along_sub(x):
        return [x] + [exchange(x, "sub", k) for k in range(1, n)]

    away_first = exchange(local, "dom", pair)
    across, local = lax.optimization_barrier((exchange(upper, "dom", pair), local))
    all_ids = along_sub(ids) + along_sub(across)
    near_slab = along_sub(local)

    plan, step_ids, negative_ids = pl.pallas_call(
        functools.partial(plan_kernel, n),
        in_specs=[in_smem] + [in_vmem] * team,
        out_specs=[in_smem, in_vmem, in_vmem],
        out_shape=[
            jax.ShapeDtypeStruct((2 * most + 1 + team,), i32),
            pltpu.VMEM((most, 3, width), i32),
            pltpu.VMEM((team, 1, width), i32),
        ],
        compiler_params=params,
        cost_estimate=pl.CostEstimate(flops=32 * slots * dims * rows, bytes_accessed=slots * dims, transcendentals=0),
        name="plan_kernel",
    )(codes, *(pltpu.with_memory_space_constraint(x, pltpu.VMEM) for x in all_ids))

    near_plan, away_first = lax.optimization_barrier((plan, away_first))
    away_slab = along_sub(away_first)
    near_rows, operator = call(
        near_kernel,
        "near_kernel",
        [((most, dims, width), bf16), ((most, dims, width), f32)],
        [pltpu.VMEM((rel_rows, dims), f32), pltpu.VMEM((2 * dims, rel_rows), bf16)],
        n * rows + 2 * rel_rows,
        (near_plan,),
        (step_ids, relations, *near_slab),
    )
    sums = ((rows, dims), f32)
    pair_out = ((most, 2 * dims, width), bf16)
    near_grad, away_grad, negative_grad, *found = call(
        functools.partial(edge_kernel, n),
        "edge_kernel",
        [pair_out, pair_out, ((team, 2 * count, dims), bf16)]
        + [sums] * (n - 1)
        + [((chunk, dims), f32)] * chips
        + [((chips * chunk, dims), f32)],
        [pltpu.VMEM((count, dims), bf16), pltpu.VMEM((dims, count), bf16), pltpu.VMEM((count, dims), f32)]
        + [pltpu.VMEM((-(-relations.shape[0] // 16) * 16, dims), f32), pltpu.VMEM((rel_rows, dims), f32)],
        3 * n * rows + 3 * count + 2 * rel_rows,
        (codes, plan),
        (step_ids, negative_ids, near_rows, operator, *near_slab, *away_slab),
    )
    away_other, relation_part = found[: n - 1], found[n - 1 :]

    def scatter(name, row, start, parts, first, plan, grads):
        return call(
            functools.partial(scatter_kernel, row, start, first),
            name,
            [sums] * parts,
            [],
            0,
            (plan,),
            (step_ids, negative_ids, grads, negative_grad),
        )

    scale = 2.0 ** -(math.ceil(math.log2(team * slots * 24 / 65504.0)) + 1)
    plane_scale = 2.0 ** -(math.ceil(math.log2(2 * chips * slots * 18 / 65504.0)) + 1)

    def narrow(x, scale=scale):
        return (x * scale).astype(jnp.float16)

    def widen(x, scale=scale):
        return x.astype(f32) * (1.0 / scale)

    def to_chip(x, k):
        return to_peer(x, k // n * 2, k % n)

    other_core = exchange(relation_part[chips], "dom", 1)
    partial = [relation_part[k] + other_core[k * chunk : (k + 1) * chunk] for k in range(chips)]
    away_other = [narrow(x) for x in away_other]
    partial, plan, away_other = lax.optimization_barrier((partial, plan, away_other))
    chunk_total = partial[0]
    for k in range(1, chips):
        chunk_total = chunk_total + to_chip(partial[k], k)
    away_received = [widen(exchange(away_other[k - 1], "sub", k)) for k in range(1, n)]
    (away_total,) = scatter("away_kernel", 1, 0, 1, 0, plan, away_grad)
    chunk_total = narrow(chunk_total, plane_scale)
    chunk_total, away_total, plan = lax.optimization_barrier((chunk_total, away_total, plan))
    terms = [chunk_total] + [exchange(chunk_total, "dom", mask) for mask in range(4, n_dom, 4)]
    terms = [widen(x, plane_scale) for x in terms]
    near_other = scatter("own_other_kernel", 0, rows, n - 1, n, plan, near_grad)
    near_other = [narrow(x) for x in near_other]
    for x in away_received:
        away_total = away_total + x
    away_total = narrow(away_total)
    while len(terms) > 1:
        terms = [terms[k] + terms[k + 1] for k in range(0, len(terms), 2)]
    chunk_total, away_total, near_other, plan = lax.optimization_barrier((terms[0], away_total, near_other, plan))
    returned = exchange(away_total, "dom", pair)
    near_received = [widen(exchange(near_other[k - 1], "sub", k)) for k in range(1, n)]
    mine = jnp.concatenate([chunk_total] + [to_chip(chunk_total, k) for k in range(1, chips)], axis=0)
    (near_sum,) = scatter("own_kernel", 0, 0, 1, n, plan, near_grad)
    returned, mine, near_sum = lax.optimization_barrier((returned, mine, near_sum))
    theirs = exchange(mine, "dom", 1)
    (new_relations,) = call(
        functools.partial(relation_kernel, chunk),
        "relation_kernel",
        [(relations.shape, f32)],
        [pltpu.VMEM((rel_rows, dims), f32), pltpu.VMEM((128, rel_rows), f32)],
        0,
        (codes,),
        (relations, relation_state.reshape(1, -1), mine, theirs),
        held=False,
    )
    returned = widen(returned)
    for x in near_received:
        returned = returned + x
    new_table, new_state = call(
        entity_kernel,
        "entity_kernel",
        [((rows, dims), f32), ((1, rows), f32)],
        [],
        1,
        (),
        (entity_table, entity_state.reshape(1, rows), returned, near_sum),
        held=False,
    )
    return (new_table, new_state.reshape(rows), new_relations)


def solution(mesh):
    in_specs = (
        P(("dom", "sub"), None),
        P(("dom", "sub")),
        P(),
        P(),
        P("dom", "sub", None),
        P("dom", "sub", None),
        P("dom", "sub", None),
        P("dom", "sub", None),
        P("dom", "sub"),
    )
    out_specs = (P(("dom", "sub"), None), P(("dom", "sub")), P())
    return jax.shard_map(
        on_device, mesh=mesh, in_specs=in_specs, out_specs=out_specs, check_vma=False
    )
```

```python
import functools
import math

import jax
import jax.numpy as jnp
from jax import lax
from jax.experimental import pallas as pl
from jax.experimental.pallas import tpu as pltpu
from jax.sharding import PartitionSpec as P

learn_rate = 0.1
bf16 = jnp.bfloat16
f32 = jnp.float32
i32 = jnp.int32
params = pltpu.CompilerParams(vmem_limit_bytes=10 * 2**20)


def dot(a, b):
    return jnp.dot(a, b, preferred_element_type=f32)


def dot_nt(a, b):
    return lax.dot_general(a, b, (((1,), (1,)), ((), ())), preferred_element_type=f32)


def one_hot(ids, rows):
    places = lax.broadcasted_iota(jnp.int16, (rows, ids.shape[1]), 0)
    return jnp.where(places == ids.astype(jnp.int16), jnp.ones((), bf16), jnp.zeros((), bf16))


def split(x):
    high = x.astype(bf16)
    return jnp.concatenate([high, (x - high.astype(f32)).astype(bf16)], axis=0)


def gather(pieces, hot):
    rows = pieces[0].shape[1]
    total = dot(pieces[0][...], hot[:rows])
    for k in range(1, len(pieces)):
        total = total + dot(pieces[k][...], hot[k * rows : (k + 1) * rows])
    return total


def scatter_add(pieces, hot, pair):
    dims = pair.shape[0] // 2
    start = 0
    for piece in pieces:
        part = hot[start : start + piece.shape[0]]
        piece[...] += dot_nt(part, pair[:dims]) + dot_nt(part, pair[dims:])
        start += piece.shape[0]


def add_negatives(pieces, hot, pair):
    count = pair.shape[0] // 2
    start = 0
    for piece in pieces:
        part = hot[start : start + piece.shape[0]]
        piece[...] += dot(part, pair[:count]) + dot(part, pair[count:])
        start += piece.shape[0]


def rows_kernel(table, out):
    out[...] = table[...].T.astype(bf16)


def ids_kernel(count, heads, tails, kinds, negatives, ids_out):
    blocks, _, width = ids_out.shape
    for j in range(blocks - 1):
        at = slice(j * width, (j + 1) * width)
        block = jnp.concatenate([heads[:, at], tails[:, at], kinds[:, at]], axis=0)
        ids_out[j] = block.astype(jnp.int16)
    last = jnp.concatenate([negatives[...], jnp.full((2, width), count[0, 0], i32)], axis=0)
    ids_out[blocks - 1] = last.astype(jnp.int16)


def plan_kernel(n, codes, *refs):
    sources, (plan, step_ids, negative_ids) = refs[:-3], refs[-3:]
    team = len(sources)
    most, _, width = step_ids.shape
    me = codes[0]
    counts, blocks = [], []
    for k, ids in enumerate(sources):
        last = ids[most].astype(i32)
        counts.append(jnp.max(last[1:2]))
        blocks.append(lax.div(counts[k] + (width - 1), i32(width)))
        negative_ids[k] = last[0:1] ^ codes[1]
    total = sum(blocks)
    low = lax.div(me * total, i32(team))
    high = lax.div((me + 1) * total, i32(team))
    plan[2 * most] = high - low
    before = []
    for k in range(team):
        ahead = [jnp.where((me ^ j) < (me ^ k), blocks[j], 0) for j in range(team) if j != k]
        before.append(sum(ahead))
        seen = (before[k] < high) & (before[k] + blocks[k] > low)
        plan[2 * most + 1 + k] = seen.astype(i32)

    def one_step(i, carry):
        line = jnp.minimum(low + i, high - 1)
        for k, ids in enumerate(sources):

            @pl.when((line >= before[k]) & (line < before[k] + blocks[k]))
            def _(k=k, ids=ids):
                nth = line - before[k]
                plan[i] = k
                plan[most + i] = jnp.clip(counts[k] - nth * width, 0, width)
                entries = ids[nth].astype(i32)
                near, away = (0, 1) if k < n else (1, 0)
                step_ids[i, 0:1] = entries[near : near + 1] ^ codes[1]
                step_ids[i, 1:2] = entries[away : away + 1] ^ codes[1]
                step_ids[i, 2:3] = entries[2:3]

        return carry

    lax.fori_loop(0, high - low, one_step, 0)


def near_kernel(plan, ids, relations, *refs):
    slab, (rows_out, operator_out, rel_full, rel_split) = refs[:-4], refs[-4:]
    dims = relations.shape[1]
    n, rows = len(slab), slab[0].shape[1]
    rel_full[...] = jnp.zeros_like(rel_full)
    rel_full[: relations.shape[0], :] = relations[...]
    rel_split[...] = split(rel_full[...].T)

    def one_block(i):
        entries = ids[i]
        rows_out[i] = gather(slab, one_hot(entries[0:1], n * rows)).astype(bf16)
        both = dot(rel_split[...], one_hot(entries[2:3], rel_full.shape[0]))
        operator_out[i] = both[:dims] + both[dims:]

    steps = plan[2 * ids.shape[0]]

    def two_blocks(i, carry):
        one_block(2 * i)
        one_block(2 * i + 1)
        return carry

    lax.fori_loop(0, steps >> 1, two_blocks, 0)
    pl.when((steps & 1) == 1)(lambda: one_block(steps - 1))


def edge_kernel(n, codes, plan, ids, negative_ids, near_in, operator_in, *refs):
    near, away = refs[:n], refs[n : 2 * n]
    near_grad, away_grad, negative_out = refs[2 * n : 2 * n + 3]
    away_other = refs[2 * n + 3 : 3 * n + 2]
    relation_out = refs[3 * n + 2 : -5]
    table, table_t, negative_grad, relation_sum, ordered = refs[-5:]
    most, _, width = ids.shape
    steps = plan[2 * most]
    count = table.shape[0]
    for piece in (*away_other, relation_sum):
        piece[...] = jnp.zeros_like(piece)
    rows = away[0].shape[1]

    def one_block(i, carry):
        here = plan[i]
        swapped = here >= n

        def take_table(slab):
            found = gather(slab, one_hot(negative_ids[here], n * rows))
            table_t[...] = found.astype(bf16)
            table[...] = found.T.astype(bf16)
            negative_grad[...] = jnp.zeros_like(negative_grad)

        fresh = (i == 0) | (plan[jnp.maximum(i - 1, 0)] != here)
        pl.when(fresh & ~swapped)(lambda: take_table(away))
        pl.when(fresh & swapped)(lambda: take_table(near))

        entries = ids[i]

        def score(swapped):
            alive = (lax.broadcasted_iota(i32, (1, width), 1) < plan[most + i]).astype(f32)
            near_rows = near_in[i].astype(f32)
            away_hot = one_hot(entries[1:2], n * rows)
            away_rows = gather(away, away_hot)
            head, tail = (away_rows, near_rows) if swapped else (near_rows, away_rows)
            operator = operator_in[i]
            query = head * operator
            query_b = query.astype(bf16)
            positive = jnp.sum(query * tail, axis=0, keepdims=True)
            scores = dot(table[...], query_b)
            pos_coef = -jax.nn.sigmoid(-positive) * alive
            neg_coef = (jax.nn.sigmoid(scores) * (alive * (1.0 / count))).astype(bf16)
            query_grad = pos_coef * tail + dot(table_t[...], neg_coef)
            negative_grad[...] += dot_nt(neg_coef, query_b)
            head_pair, tail_pair = split(query_grad * operator), split(pos_coef * query)
            near_pair, away_pair = (tail_pair, head_pair) if swapped else (head_pair, tail_pair)
            near_grad[i] = near_pair
            away_grad[i] = away_pair
            scatter_add(away_other, away_hot[rows:], away_pair)
            scatter_add([relation_sum], one_hot(entries[2:3], relation_sum.shape[0]), split(query_grad * head))

        pl.when(~swapped)(lambda: score(False))
        pl.when(swapped)(lambda: score(True))

        ends = (i == steps - 1) | (plan[jnp.minimum(i + 1, steps - 1)] != here)

        @pl.when(ends)
        def _():
            negative_out[here] = split(negative_grad[...])

        @pl.when(ends & ~swapped)
        def _():
            add_negatives(away_other, one_hot(negative_ids[here] - rows, (n - 1) * rows), negative_out[here])

        return carry

    lax.fori_loop(0, steps, one_block, 0)
    chunk = relation_out[0].shape[0]
    ordered[...] = jnp.zeros_like(ordered)
    ordered[: relation_sum.shape[0], :] = relation_sum[...]
    start = 0
    for piece in relation_out:
        for k in range(0, piece.shape[0], chunk):
            at = pl.multiple_of(codes[2] ^ (start + k), chunk)
            piece[k : k + chunk, :] = ordered[pl.ds(at, chunk), :]
        start += piece.shape[0]


def scatter_kernel(row, start, first, plan, ids, negative_ids, grads, negative_grads, *sums):
    most = ids.shape[0]
    height = sum(piece.shape[0] for piece in sums)
    for piece in sums:
        piece[...] = jnp.zeros_like(piece)

    steps = plan[2 * most]

    def hot_of(i):
        return one_hot(ids[i][row : row + 1] - start, height)

    def two_blocks(i, carry):
        hot = jnp.concatenate([hot_of(2 * i), hot_of(2 * i + 1)], axis=1)
        scatter_add(sums, hot, jnp.concatenate([grads[2 * i], grads[2 * i + 1]], axis=1))
        return carry

    lax.fori_loop(0, steps >> 1, two_blocks, 0)

    @pl.when((steps & 1) == 1)
    def _():
        scatter_add(sums, hot_of(steps - 1), grads[steps - 1])

    for k in range(first, first + negative_ids.shape[0] // 2):

        @pl.when(plan[2 * most + 1 + k] != 0)
        def _(k=k):
            add_negatives(sums, one_hot(negative_ids[k] - start, height), negative_grads[k])


def entity_kernel(table, state, returned, own, new_table, new_state):
    grad = returned[...] + own[...]
    lanes = 128
    before = jnp.broadcast_to(state[...], (lanes, table.shape[0])).T[:, :1]
    after = before + jnp.mean(grad * grad, axis=-1, keepdims=True)
    new_table[...] = table[...] - learn_rate * grad / jnp.sqrt(after)
    new_state[...] = jnp.broadcast_to(after, (table.shape[0], lanes)).T[:1]


def update_chunks(chunk, first, codes, grads, column, rows):
    for k in range(grads.shape[0] // chunk):
        at = pl.ds(pl.multiple_of(codes[2] ^ ((first + k) * chunk), chunk), chunk)
        g = grads[k * chunk : (k + 1) * chunk, :]
        total = column[at, :1] + jnp.mean(g * g, axis=-1, keepdims=True)
        rows[at, :] = rows[at, :] - learn_rate * g / jnp.sqrt(total)


def relation_mine_kernel(chunk, codes, relations, state, mine, rows, column, wide):
    count = relations.shape[0]
    wide[...] = jnp.ones_like(wide)
    wide[:, :count] = jnp.broadcast_to(state[...], (wide.shape[0], count))
    column[...] = wide[...].T
    rows[...] = jnp.zeros_like(rows)
    rows[:count, :] = relations[...]
    update_chunks(chunk, 0, codes, mine, column, rows)


def relation_theirs_kernel(chunk, codes, before, column, theirs, out, rows):
    rows[...] = before[...]
    update_chunks(chunk, theirs.shape[0] // chunk, codes, theirs, column, rows)
    out[...] = rows[: out.shape[0], :]


def exchange(x, axis, mask):
    return lax.ppermute(x, axis, [(i, i ^ mask) for i in range(lax.axis_size(axis))])


def on_device(
    entity_table,
    entity_state,
    relations,
    relation_state,
    head_rows,
    tail_rows,
    relation_ids,
    negative_rows,
    edge_counts,
):
    n = lax.axis_size("sub")
    n_dom = lax.axis_size("dom")
    me_sub = lax.axis_index("sub")
    me_dom = lax.axis_index("dom")
    pair = n_dom // 2
    team = 2 * n
    rows, dims = entity_table.shape
    slots = head_rows.shape[2]
    count = negative_rows.shape[2]
    width = count
    most = slots // width
    rel_rows = -(-relations.shape[0] // 256) * 256
    chips = 2 * n
    chunk = rel_rows // (2 * chips)
    me = lax.shift_right_logical(me_dom, pair.bit_length() - 1) * n + me_sub
    chunk_code = (me_dom & 1) * chips + ((me_dom >> 1) & 1) * n + me_sub
    codes = jnp.stack([me, me_sub * rows, chunk_code * chunk]).astype(i32)

    in_vmem = pl.BlockSpec(memory_space=pltpu.VMEM)
    in_smem = pl.BlockSpec(memory_space=pltpu.SMEM)

    def call(kernel, name, outs, scratch, unit, scalars, arrays, held=True, fetch=False):
        place = (lambda x, t: pltpu.VMEM(x, t)) if held else jax.ShapeDtypeStruct
        return pl.pallas_call(
            kernel,
            in_specs=[in_smem] * len(scalars) + [in_vmem] * len(arrays),
            out_specs=[in_vmem] * len(outs),
            out_shape=[place(x, t) for x, t in outs],
            scratch_shapes=scratch,
            compiler_params=params,
            cost_estimate=pl.CostEstimate(flops=int(slots * dims * unit), bytes_accessed=rows * dims, transcendentals=0),
            name=name,
        )(*scalars, *(pltpu.with_memory_space_constraint(x, pltpu.HBM if fetch else pltpu.VMEM) for x in arrays))

    (ids,) = call(
        ids_kernel,
        "ids_kernel",
        [((most + 1, 3, width), jnp.int16)],
        [],
        1,
        (edge_counts,),
        (
            head_rows.reshape(1, slots),
            tail_rows.reshape(1, slots),
            relation_ids.reshape(1, slots),
            negative_rows.reshape(1, count),
        ),
        fetch=True,
    )
    ids, table = lax.optimization_barrier((ids, entity_table))
    (local,) = call(rows_kernel, "rows_kernel", [((dims, rows), bf16)], [], 1, (), (table,), fetch=True)

    def to_peer(x, across, aside):
        pairs = [(d * n + s, (d ^ across) * n + (s ^ aside)) for d in range(n_dom) for s in range(n)]
        return lax.ppermute(x, ("dom", "sub"), pairs)

    def along_sub(x):
        return [x] + [exchange(x, "sub", k) for k in range(1, n)]

    all_ids = along_sub(ids) + along_sub(exchange(ids, "dom", pair))
    near_slab = along_sub(local)
    away_first = exchange(local, "dom", pair)

    plan, step_ids, negative_ids = pl.pallas_call(
        functools.partial(plan_kernel, n),
        in_specs=[in_smem] + [in_vmem] * team,
        out_specs=[in_smem, in_vmem, in_vmem],
        out_shape=[
            jax.ShapeDtypeStruct((2 * most + 1 + team,), i32),
            pltpu.VMEM((most, 3, width), i32),
            pltpu.VMEM((team, 1, width), i32),
        ],
        compiler_params=params,
        cost_estimate=pl.CostEstimate(flops=32 * slots * dims * rows, bytes_accessed=slots * dims, transcendentals=0),
        name="plan_kernel",
    )(codes, *(pltpu.with_memory_space_constraint(x, pltpu.VMEM) for x in all_ids))

    near_plan, away_first = lax.optimization_barrier((plan, away_first))
    away_slab = along_sub(away_first)
    near_rows, operator = call(
        near_kernel,
        "near_kernel",
        [((most, dims, width), bf16), ((most, dims, width), f32)],
        [pltpu.VMEM((rel_rows, dims), f32), pltpu.VMEM((2 * dims, rel_rows), bf16)],
        n * rows + 2 * rel_rows,
        (near_plan,),
        (step_ids, relations, *near_slab),
    )
    sums = ((rows, dims), f32)
    pair_out = ((most, 2 * dims, width), bf16)
    near_grad, away_grad, negative_grad, *found = call(
        functools.partial(edge_kernel, n),
        "edge_kernel",
        [pair_out, pair_out, ((team, 2 * count, dims), bf16)]
        + [sums] * (n - 1)
        + [((chunk, dims), f32)] * chips
        + [((chips * chunk, dims), f32)],
        [pltpu.VMEM((count, dims), bf16), pltpu.VMEM((dims, count), bf16), pltpu.VMEM((count, dims), f32)]
        + [pltpu.VMEM((-(-relations.shape[0] // 16) * 16, dims), f32), pltpu.VMEM((rel_rows, dims), f32)],
        3 * n * rows + 3 * count + 2 * rel_rows,
        (codes, plan),
        (step_ids, negative_ids, near_rows, operator, *near_slab, *away_slab),
    )
    away_other, relation_part = found[: n - 1], found[n - 1 :]

    def scatter(name, row, start, parts, first, plan, grads):
        return call(
            functools.partial(scatter_kernel, row, start, first),
            name,
            [sums] * parts,
            [],
            0,
            (plan,),
            (step_ids, negative_ids, grads, negative_grad),
        )

    scale = 2.0 ** -(math.ceil(math.log2(team * slots * 24 / 65504.0)) + 1)
    plane_scale = 2.0 ** -(math.ceil(math.log2(2 * chips * slots * 18 / 65504.0)) + 1)

    def narrow(x, scale=scale):
        return (x * scale).astype(jnp.float16)

    def widen(x, scale=scale):
        return x.astype(f32) * (1.0 / scale)

    def to_chip(x, k):
        return to_peer(x, k // n * 2, k % n)

    other_core = exchange(relation_part[chips], "dom", 1)
    partial = [relation_part[k] + other_core[k * chunk : (k + 1) * chunk] for k in range(chips)]
    away_other = [narrow(x) for x in away_other]
    partial, plan, away_other = lax.optimization_barrier((partial, plan, away_other))
    chunk_total = partial[0]
    for k in range(1, chips):
        chunk_total = chunk_total + to_chip(partial[k], k)
    away_received = [widen(exchange(away_other[k - 1], "sub", k)) for k in range(1, n)]
    (away_total,) = scatter("away_kernel", 1, 0, 1, 0, plan, away_grad)
    chunk_total = narrow(chunk_total, plane_scale)
    chunk_total, away_total, plan = lax.optimization_barrier((chunk_total, away_total, plan))
    terms = [chunk_total] + [exchange(chunk_total, "dom", mask) for mask in range(4, n_dom, 4)]
    terms = [widen(x, plane_scale) for x in terms]
    near_other = scatter("own_other_kernel", 0, rows, n - 1, n, plan, near_grad)
    near_other = [narrow(x) for x in near_other]
    for x in away_received:
        away_total = away_total + x
    away_total = narrow(away_total)
    while len(terms) > 1:
        terms = [terms[k] + terms[k + 1] for k in range(0, len(terms), 2)]
    chunk_total, away_total, near_other, plan = lax.optimization_barrier((terms[0], away_total, near_other, plan))
    returned = exchange(away_total, "dom", pair)
    near_received = [widen(exchange(near_other[k - 1], "sub", k)) for k in range(1, n)]
    mine = jnp.concatenate([chunk_total] + [to_chip(chunk_total, k) for k in range(1, chips)], axis=0)
    (near_sum,) = scatter("own_kernel", 0, 0, 1, n, plan, near_grad)
    half_done, column = call(
        functools.partial(relation_mine_kernel, chunk),
        "relation_mine_kernel",
        [((rel_rows, dims), f32), ((rel_rows, 128), f32)],
        [pltpu.VMEM((128, rel_rows), f32)],
        0,
        (codes,),
        (relations, relation_state.reshape(1, -1), mine),
    )
    returned, mine, near_sum, half_done = lax.optimization_barrier((returned, mine, near_sum, half_done))
    theirs = exchange(mine, "dom", 1)
    (new_relations,) = call(
        functools.partial(relation_theirs_kernel, chunk),
        "relation_theirs_kernel",
        [(relations.shape, f32)],
        [pltpu.VMEM((rel_rows, dims), f32)],
        0,
        (codes,),
        (half_done, column, theirs),
        held=False,
    )
    returned = widen(returned)
    for x in near_received:
        returned = returned + x
    new_table, new_state = call(
        entity_kernel,
        "entity_kernel",
        [((rows, dims), f32), ((1, rows), f32)],
        [],
        1,
        (),
        (entity_table, entity_state.reshape(1, rows), returned, near_sum),
        held=False,
    )
    return (new_table, new_state.reshape(rows), new_relations)


def solution(mesh):
    in_specs = (
        P(("dom", "sub"), None),
        P(("dom", "sub")),
        P(),
        P(),
        P("dom", "sub", None),
        P("dom", "sub", None),
        P("dom", "sub", None),
        P("dom", "sub", None),
        P("dom", "sub"),
    )
    out_specs = (P(("dom", "sub"), None), P(("dom", "sub")), P())
    return jax.shard_map(
        on_device, mesh=mesh, in_specs=in_specs, out_specs=out_specs, check_vma=False
    )
```

```python
import functools
import math

import jax
import jax.numpy as jnp
from jax import lax
from jax.experimental import pallas as pl
from jax.experimental.pallas import tpu as pltpu
from jax.sharding import PartitionSpec as P

learn_rate = 0.1
bf16 = jnp.bfloat16
f32 = jnp.float32
i32 = jnp.int32
params = pltpu.CompilerParams(vmem_limit_bytes=10 * 2**20)


def dot(a, b):
    return jnp.dot(a, b, preferred_element_type=f32)


def dot_nt(a, b):
    return lax.dot_general(a, b, (((1,), (1,)), ((), ())), preferred_element_type=f32)


def one_hot(ids, rows):
    places = lax.broadcasted_iota(jnp.int16, (rows, ids.shape[1]), 0)
    return jnp.where(places == ids.astype(jnp.int16), jnp.ones((), bf16), jnp.zeros((), bf16))


def split(x):
    high = x.astype(bf16)
    return jnp.concatenate([high, (x - high.astype(f32)).astype(bf16)], axis=0)


def gather(pieces, hot):
    rows = pieces[0].shape[1]
    total = dot(pieces[0][...], hot[:rows])
    for k in range(1, len(pieces)):
        total = total + dot(pieces[k][...], hot[k * rows : (k + 1) * rows])
    return total


def scatter_add(pieces, hot, pair):
    dims = pair.shape[0] // 2
    start = 0
    for piece in pieces:
        part = hot[start : start + piece.shape[0]]
        piece[...] += dot_nt(part, pair[:dims]) + dot_nt(part, pair[dims:])
        start += piece.shape[0]


def add_negatives(pieces, hot, pair):
    count = pair.shape[0] // 2
    start = 0
    for piece in pieces:
        part = hot[start : start + piece.shape[0]]
        piece[...] += dot(part, pair[:count]) + dot(part, pair[count:])
        start += piece.shape[0]


def rows_kernel(table, out):
    out[...] = table[...].T.astype(bf16)


def ids_kernel(count, heads, tails, kinds, negatives, ids_out):
    blocks, _, width = ids_out.shape
    for j in range(blocks - 1):
        at = slice(j * width, (j + 1) * width)
        block = jnp.concatenate([heads[:, at], tails[:, at], kinds[:, at]], axis=0)
        ids_out[j] = block.astype(jnp.int16)
    last = jnp.concatenate([negatives[...], jnp.full((2, width), count[0, 0], i32)], axis=0)
    ids_out[blocks - 1] = last.astype(jnp.int16)


def plan_kernel(n, codes, *refs):
    sources, (plan, step_ids, negative_ids) = refs[:-3], refs[-3:]
    team = len(sources)
    most, _, width = step_ids.shape
    me = codes[0]
    counts, blocks = [], []
    for k, ids in enumerate(sources):
        last = ids[most].astype(i32)
        counts.append(jnp.max(last[1:2]))
        blocks.append(lax.div(counts[k] + (width - 1), i32(width)))
        negative_ids[k] = last[0:1] ^ codes[1]
    total = sum(blocks)
    low = lax.div(me * total, i32(team))
    high = lax.div((me + 1) * total, i32(team))
    plan[2 * most] = high - low
    before = []
    for k in range(team):
        ahead = [jnp.where((me ^ j) < (me ^ k), blocks[j], 0) for j in range(team) if j != k]
        before.append(sum(ahead))
        seen = (before[k] < high) & (before[k] + blocks[k] > low)
        plan[2 * most + 1 + k] = seen.astype(i32)

    def one_step(i, carry):
        line = jnp.minimum(low + i, high - 1)
        for k, ids in enumerate(sources):

            @pl.when((line >= before[k]) & (line < before[k] + blocks[k]))
            def _(k=k, ids=ids):
                nth = line - before[k]
                plan[i] = k
                plan[most + i] = jnp.clip(counts[k] - nth * width, 0, width)
                entries = ids[nth].astype(i32)
                near, away = (0, 1) if k < n else (1, 0)
                step_ids[i, 0:1] = entries[near : near + 1] ^ codes[1]
                step_ids[i, 1:2] = entries[away : away + 1] ^ codes[1]
                step_ids[i, 2:3] = entries[2:3]

        return carry

    lax.fori_loop(0, high - low, one_step, 0)


def near_kernel(plan, ids, relations, *refs):
    slab, (rows_out, operator_out, rel_full, rel_split) = refs[:-4], refs[-4:]
    dims = relations.shape[1]
    n, rows = len(slab), slab[0].shape[1]
    rel_full[...] = jnp.zeros_like(rel_full)
    rel_full[: relations.shape[0], :] = relations[...]
    rel_split[...] = split(rel_full[...].T)

    def one_block(i):
        entries = ids[i]
        rows_out[i] = gather(slab, one_hot(entries[0:1], n * rows)).astype(bf16)
        both = dot(rel_split[...], one_hot(entries[2:3], rel_full.shape[0]))
        operator_out[i] = both[:dims] + both[dims:]

    steps = plan[2 * ids.shape[0]]

    def two_blocks(i, carry):
        one_block(2 * i)
        one_block(2 * i + 1)
        return carry

    lax.fori_loop(0, steps >> 1, two_blocks, 0)
    pl.when((steps & 1) == 1)(lambda: one_block(steps - 1))


def edge_kernel(n, codes, plan, ids, negative_ids, near_in, operator_in, *refs):
    near, away = refs[:n], refs[n : 2 * n]
    near_grad, away_grad, negative_out = refs[2 * n : 2 * n + 3]
    away_other = refs[2 * n + 3 : 3 * n + 2]
    relation_out = refs[3 * n + 2 : -5]
    table, table_t, negative_grad, relation_sum, ordered = refs[-5:]
    most, _, width = ids.shape
    steps = plan[2 * most]
    count = table.shape[0]
    for piece in (*away_other, relation_sum):
        piece[...] = jnp.zeros_like(piece)
    rows = away[0].shape[1]

    def one_block(i, carry):
        here = plan[i]
        swapped = here >= n

        def take_table(slab):
            found = gather(slab, one_hot(negative_ids[here], n * rows))
            table_t[...] = found.astype(bf16)
            table[...] = found.T.astype(bf16)
            negative_grad[...] = jnp.zeros_like(negative_grad)

        fresh = (i == 0) | (plan[jnp.maximum(i - 1, 0)] != here)
        pl.when(fresh & ~swapped)(lambda: take_table(away))
        pl.when(fresh & swapped)(lambda: take_table(near))

        entries = ids[i]

        def score(swapped):
            alive = (lax.broadcasted_iota(i32, (1, width), 1) < plan[most + i]).astype(f32)
            near_rows = near_in[i].astype(f32)
            away_hot = one_hot(entries[1:2], n * rows)
            away_rows = gather(away, away_hot)
            head, tail = (away_rows, near_rows) if swapped else (near_rows, away_rows)
            operator = operator_in[i]
            query = head * operator
            query_b = query.astype(bf16)
            positive = jnp.sum(query * tail, axis=0, keepdims=True)
            scores = dot(table[...], query_b)
            pos_coef = -jax.nn.sigmoid(-positive) * alive
            neg_coef = (jax.nn.sigmoid(scores) * (alive * (1.0 / count))).astype(bf16)
            query_grad = pos_coef * tail + dot(table_t[...], neg_coef)
            negative_grad[...] += dot_nt(neg_coef, query_b)
            head_pair, tail_pair = split(query_grad * operator), split(pos_coef * query)
            near_pair, away_pair = (tail_pair, head_pair) if swapped else (head_pair, tail_pair)
            near_grad[i] = near_pair
            away_grad[i] = away_pair
            scatter_add(away_other, away_hot[rows:], away_pair)
            scatter_add([relation_sum], one_hot(entries[2:3], relation_sum.shape[0]), split(query_grad * head))

        pl.when(~swapped)(lambda: score(False))
        pl.when(swapped)(lambda: score(True))

        ends = (i == steps - 1) | (plan[jnp.minimum(i + 1, steps - 1)] != here)

        @pl.when(ends)
        def _():
            negative_out[here] = split(negative_grad[...])

        @pl.when(ends & ~swapped)
        def _():
            add_negatives(away_other, one_hot(negative_ids[here] - rows, (n - 1) * rows), negative_out[here])

        return carry

    lax.fori_loop(0, steps, one_block, 0)
    chunk = relation_out[0].shape[0]
    ordered[...] = jnp.zeros_like(ordered)
    ordered[: relation_sum.shape[0], :] = relation_sum[...]
    start = 0
    for piece in relation_out:
        for k in range(0, piece.shape[0], chunk):
            at = pl.multiple_of(codes[2] ^ (start + k), chunk)
            piece[k : k + chunk, :] = ordered[pl.ds(at, chunk), :]
        start += piece.shape[0]


def scatter_kernel(row, start, first, plan, ids, negative_ids, grads, negative_grads, *sums):
    most = ids.shape[0]
    height = sum(piece.shape[0] for piece in sums)
    for piece in sums:
        piece[...] = jnp.zeros_like(piece)

    steps = plan[2 * most]

    def hot_of(i):
        return one_hot(ids[i][row : row + 1] - start, height)

    def four_blocks(i, carry):
        hot = jnp.concatenate([hot_of(4 * i + k) for k in range(4)], axis=1)
        scatter_add(sums, hot, jnp.concatenate([grads[4 * i + k] for k in range(4)], axis=1))
        return carry

    def one_block(i, carry):
        scatter_add(sums, hot_of(i), grads[i])
        return carry

    lax.fori_loop(0, steps >> 2, four_blocks, 0)
    lax.fori_loop((steps >> 2) << 2, steps, one_block, 0)

    for k in range(first, first + negative_ids.shape[0] // 2):

        @pl.when(plan[2 * most + 1 + k] != 0)
        def _(k=k):
            add_negatives(sums, one_hot(negative_ids[k] - start, height), negative_grads[k])


def entity_kernel(table, state, returned, own, new_table, new_state):
    grad = returned[...] + own[...]
    lanes = 128
    before = jnp.broadcast_to(state[...], (lanes, table.shape[0])).T[:, :1]
    after = before + jnp.mean(grad * grad, axis=-1, keepdims=True)
    new_table[...] = table[...] - learn_rate * grad / jnp.sqrt(after)
    new_state[...] = jnp.broadcast_to(after, (table.shape[0], lanes)).T[:1]


def relation_kernel(chunk, codes, relations, state, mine, theirs, out, grad, column):
    chunks = mine.shape[0] // chunk
    for k in range(2 * chunks):
        part = (mine, theirs)[k // chunks]
        start = (k % chunks) * chunk
        grad[pl.ds(pl.multiple_of(codes[2] ^ (k * chunk), chunk), chunk), :] = part[start : start + chunk, :]
    count = relations.shape[0]
    column[...] = jnp.ones_like(column)
    column[:, :count] = jnp.broadcast_to(state[...], (column.shape[0], count))
    g = grad[:count, :]
    total = column[...].T[:count, :1] + jnp.mean(g * g, axis=-1, keepdims=True)
    out[...] = relations[...] - learn_rate * g / jnp.sqrt(total)


def exchange(x, axis, mask):
    return lax.ppermute(x, axis, [(i, i ^ mask) for i in range(lax.axis_size(axis))])


def on_device(
    entity_table,
    entity_state,
    relations,
    relation_state,
    head_rows,
    tail_rows,
    relation_ids,
    negative_rows,
    edge_counts,
):
    n = lax.axis_size("sub")
    n_dom = lax.axis_size("dom")
    me_sub = lax.axis_index("sub")
    me_dom = lax.axis_index("dom")
    pair = n_dom // 2
    team = 2 * n
    rows, dims = entity_table.shape
    slots = head_rows.shape[2]
    count = negative_rows.shape[2]
    width = count
    most = slots // width
    rel_rows = -(-relations.shape[0] // 256) * 256
    chips = 2 * n
    chunk = rel_rows // (2 * chips)
    me = lax.shift_right_logical(me_dom, pair.bit_length() - 1) * n + me_sub
    chunk_code = (me_dom & 1) * chips + ((me_dom >> 1) & 1) * n + me_sub
    codes = jnp.stack([me, me_sub * rows, chunk_code * chunk]).astype(i32)

    in_vmem = pl.BlockSpec(memory_space=pltpu.VMEM)
    in_smem = pl.BlockSpec(memory_space=pltpu.SMEM)

    def call(kernel, name, outs, scratch, unit, scalars, arrays, held=True, fetch=False):
        place = (lambda x, t: pltpu.VMEM(x, t)) if held else jax.ShapeDtypeStruct
        return pl.pallas_call(
            kernel,
            in_specs=[in_smem] * len(scalars) + [in_vmem] * len(arrays),
            out_specs=[in_vmem] * len(outs),
            out_shape=[place(x, t) for x, t in outs],
            scratch_shapes=scratch,
            compiler_params=params,
            cost_estimate=pl.CostEstimate(flops=int(slots * dims * unit), bytes_accessed=rows * dims, transcendentals=0),
            name=name,
        )(*scalars, *(pltpu.with_memory_space_constraint(x, pltpu.HBM if fetch else pltpu.VMEM) for x in arrays))

    (ids,) = call(
        ids_kernel,
        "ids_kernel",
        [((most + 1, 3, width), jnp.int16)],
        [],
        1,
        (edge_counts,),
        (
            head_rows.reshape(1, slots),
            tail_rows.reshape(1, slots),
            relation_ids.reshape(1, slots),
            negative_rows.reshape(1, count),
        ),
        fetch=True,
    )
    ids, table = lax.optimization_barrier((ids, entity_table))
    (local,) = call(rows_kernel, "rows_kernel", [((dims, rows), bf16)], [], 1, (), (table,), fetch=True)

    def to_peer(x, across, aside):
        pairs = [(d * n + s, (d ^ across) * n + (s ^ aside)) for d in range(n_dom) for s in range(n)]
        return lax.ppermute(x, ("dom", "sub"), pairs)

    def along_sub(x):
        return [x] + [exchange(x, "sub", k) for k in range(1, n)]

    all_ids = along_sub(ids) + along_sub(exchange(ids, "dom", pair))
    near_slab = along_sub(local)
    away_first = exchange(local, "dom", pair)

    plan, step_ids, negative_ids = pl.pallas_call(
        functools.partial(plan_kernel, n),
        in_specs=[in_smem] + [in_vmem] * team,
        out_specs=[in_smem, in_vmem, in_vmem],
        out_shape=[
            jax.ShapeDtypeStruct((2 * most + 1 + team,), i32),
            pltpu.VMEM((most, 3, width), i32),
            pltpu.VMEM((team, 1, width), i32),
        ],
        compiler_params=params,
        cost_estimate=pl.CostEstimate(flops=32 * slots * dims * rows, bytes_accessed=slots * dims, transcendentals=0),
        name="plan_kernel",
    )(codes, *(pltpu.with_memory_space_constraint(x, pltpu.VMEM) for x in all_ids))

    near_plan, away_first = lax.optimization_barrier((plan, away_first))
    away_slab = along_sub(away_first)
    near_rows, operator = call(
        near_kernel,
        "near_kernel",
        [((most, dims, width), bf16), ((most, dims, width), f32)],
        [pltpu.VMEM((rel_rows, dims), f32), pltpu.VMEM((2 * dims, rel_rows), bf16)],
        n * rows + 2 * rel_rows,
        (near_plan,),
        (step_ids, relations, *near_slab),
    )
    sums = ((rows, dims), f32)
    pair_out = ((most, 2 * dims, width), bf16)
    near_grad, away_grad, negative_grad, *found = call(
        functools.partial(edge_kernel, n),
        "edge_kernel",
        [pair_out, pair_out, ((team, 2 * count, dims), bf16)]
        + [sums] * (n - 1)
        + [((chunk, dims), f32)] * chips
        + [((chips * chunk, dims), f32)],
        [pltpu.VMEM((count, dims), bf16), pltpu.VMEM((dims, count), bf16), pltpu.VMEM((count, dims), f32)]
        + [pltpu.VMEM((-(-relations.shape[0] // 16) * 16, dims), f32), pltpu.VMEM((rel_rows, dims), f32)],
        3 * n * rows + 3 * count + 2 * rel_rows,
        (codes, plan),
        (step_ids, negative_ids, near_rows, operator, *near_slab, *away_slab),
    )
    away_other, relation_part = found[: n - 1], found[n - 1 :]

    def scatter(name, row, start, parts, first, plan, grads):
        return call(
            functools.partial(scatter_kernel, row, start, first),
            name,
            [sums] * parts,
            [],
            0,
            (plan,),
            (step_ids, negative_ids, grads, negative_grad),
        )

    scale = 2.0 ** -(math.ceil(math.log2(team * slots * 24 / 65504.0)) + 1)
    plane_scale = 2.0 ** -(math.ceil(math.log2(2 * chips * slots * 18 / 65504.0)) + 1)

    def narrow(x, scale=scale):
        return (x * scale).astype(jnp.float16)

    def widen(x, scale=scale):
        return x.astype(f32) * (1.0 / scale)

    def to_chip(x, k):
        return to_peer(x, k // n * 2, k % n)

    other_core = exchange(relation_part[chips], "dom", 1)
    partial = [relation_part[k] + other_core[k * chunk : (k + 1) * chunk] for k in range(chips)]
    away_other = [narrow(x) for x in away_other]
    partial, plan, away_other = lax.optimization_barrier((partial, plan, away_other))
    chunk_total = partial[0]
    for k in range(1, chips):
        chunk_total = chunk_total + to_chip(partial[k], k)
    away_received = [widen(exchange(away_other[k - 1], "sub", k)) for k in range(1, n)]
    (away_total,) = scatter("away_kernel", 1, 0, 1, 0, plan, away_grad)
    chunk_total = narrow(chunk_total, plane_scale)
    chunk_total, away_total, plan = lax.optimization_barrier((chunk_total, away_total, plan))
    terms = [chunk_total] + [exchange(chunk_total, "dom", mask) for mask in range(4, n_dom, 4)]
    terms = [widen(x, plane_scale) for x in terms]
    near_other = scatter("own_other_kernel", 0, rows, n - 1, n, plan, near_grad)
    near_other = [narrow(x) for x in near_other]
    for x in away_received:
        away_total = away_total + x
    away_total = narrow(away_total)
    while len(terms) > 1:
        terms = [terms[k] + terms[k + 1] for k in range(0, len(terms), 2)]
    chunk_total, away_total, near_other, plan = lax.optimization_barrier((terms[0], away_total, near_other, plan))
    returned = exchange(away_total, "dom", pair)
    near_received = [widen(exchange(near_other[k - 1], "sub", k)) for k in range(1, n)]
    mine = jnp.concatenate([chunk_total] + [to_chip(chunk_total, k) for k in range(1, chips)], axis=0)
    (near_sum,) = scatter("own_kernel", 0, 0, 1, n, plan, near_grad)
    returned, mine, near_sum = lax.optimization_barrier((returned, mine, near_sum))
    theirs = exchange(mine, "dom", 1)
    (new_relations,) = call(
        functools.partial(relation_kernel, chunk),
        "relation_kernel",
        [(relations.shape, f32)],
        [pltpu.VMEM((rel_rows, dims), f32), pltpu.VMEM((128, rel_rows), f32)],
        0,
        (codes,),
        (relations, relation_state.reshape(1, -1), mine, theirs),
        held=False,
    )
    returned = widen(returned)
    for x in near_received:
        returned = returned + x
    new_table, new_state = call(
        entity_kernel,
        "entity_kernel",
        [((rows, dims), f32), ((1, rows), f32)],
        [],
        1,
        (),
        (entity_table, entity_state.reshape(1, rows), returned, near_sum),
        held=False,
    )
    return (new_table, new_state.reshape(rows), new_relations)


def solution(mesh):
    in_specs = (
        P(("dom", "sub"), None),
        P(("dom", "sub")),
        P(),
        P(),
        P("dom", "sub", None),
        P("dom", "sub", None),
        P("dom", "sub", None),
        P("dom", "sub", None),
        P("dom", "sub"),
    )
    out_specs = (P(("dom", "sub"), None), P(("dom", "sub")), P())
    return jax.shard_map(
        on_device, mesh=mesh, in_specs=in_specs, out_specs=out_specs, check_vma=False
    )
```
